256 devices in a mesh: dom: 16 (over z, core), head: 16 (over x, y).
Axes of the slice: x: 4, y: 4, z: 8, core: 2. Of those that a mesh axis runs over, the one named last changes fastest.
Arguments:
- features: bfloat16 [32768, 1024], P(('dom', 'head')), as said below
- w_query: bfloat16 [1024, 1024], P(None, 'head'), as said below
- w_key: bfloat16 [1024, 1024], P(None, 'head'), as said below
- w_value: bfloat16 [1024, 1024], P(None, 'head'), may hold values from -0.1875 to 0.1875
- w_output: bfloat16 [1024, 1024], P('head'), may hold values from -0.1875 to 0.1875
- cotangent: bfloat16 [32768, 1024], P(('dom', 'head')), may hold values from -24 to 24
- cross_source: int32 [16, 16], P('dom'), may hold values from 0 to 255, as said below
- cross_target: int32 [16, 16], P('dom'), may hold values from 0 to 15, as said below
- cross_count: int32 [16], P('dom'), may hold values from 12 to 16, as said below
Outputs:
- layer_out: bfloat16 [32768, 1024], P(('dom', 'head'))
- grad_features: bfloat16 [32768, 1024], P(('dom', 'head'))
- w_query_grad: float32 [1024, 1024], P('dom', 'head')
- w_key_grad: float32 [1024, 1024], P('dom', 'head')
- w_value_grad: float32 [1024, 1024], P('dom', 'head')
- w_output_grad_t: float32 [1024, 1024], P('dom', 'head')
The draws below stay inside these ranges and needn't reach their ends.
Inputs may be any that keep to these rules, and one draw needn't show every extreme that they name: `cross_source`: row p names global blocks of partitions other than p; at most 2 entries of one row lie in any one partition, and some row has exactly 2 in one partition. `cross_target`: the entries of one row are distinct. `cross_count`: some partition has 16 live slots. `features`: entries lie within 10 in magnitude. `w_query`: entries lie within 5 / sqrt(1024) in magnitude. `w_key`: entries lie within 5 / sqrt(1024) in magnitude.
All inputs are finite; a program needn't handle non-finite values.
Results may differ from the reference program's by a relative error of at most 0.018.
Values may be sent and summed in bfloat16 or wider, within the bound.
A program may use at most 64 MiB of HBM per device.

```python
import math
import jax
import jax.numpy as jnp
from jax import lax

D = 1024
H = 16
HD = 64
BLK = 128
CAP = 2
PARTS_SIZE = 16
P_NODES = 2048
NBLK_P = 16
CMAX = 16
NODES = 32768


def cross_tables(key):
    lowest = CMAX - CMAX // 4
    counts = jax.random.randint(jax.random.fold_in(key, 501), (PARTS_SIZE,), lowest, CMAX + 1)
    full_part = jax.random.randint(jax.random.fold_in(key, 502), (), 0, PARTS_SIZE)
    counts = jnp.where(jnp.arange(PARTS_SIZE) == full_part, CMAX, counts)

    def shuffle_owners(subkey):
        return jax.random.permutation(subkey, PARTS_SIZE - 1)
    owner_order = jax.vmap(shuffle_owners)(jax.random.split(jax.random.fold_in(key, 503), PARTS_SIZE))
    slot_groups = jnp.arange(CMAX) // CAP
    owners = (jnp.arange(PARTS_SIZE)[:, None] + 1 + owner_order[:, slot_groups]) % PARTS_SIZE
    within = jax.random.randint(jax.random.fold_in(key, 504), (PARTS_SIZE, CMAX), 0, NBLK_P)
    source = owners * NBLK_P + within

    def shuffle_slots(subkey):
        return jax.random.permutation(subkey, CMAX)
    slot_order = jax.vmap(shuffle_slots)(jax.random.split(jax.random.fold_in(key, 505), PARTS_SIZE))
    source = jnp.take_along_axis(source, slot_order, axis=1)

    def shuffle_targets(subkey):
        return jax.random.permutation(subkey, NBLK_P)
    target = jax.vmap(shuffle_targets)(jax.random.split(jax.random.fold_in(key, 506), PARTS_SIZE))[:, :CMAX]
    return (source.astype(jnp.int32), target.astype(jnp.int32), counts.astype(jnp.int32))


def draw_cross_source(key, part):
    return cross_tables(key)[0]


def draw_cross_target(key, part):
    return cross_tables(key)[1]


def draw_cross_count(key, part):
    return cross_tables(key)[2]


def projection_pair(key):
    base = jnp.clip(jax.random.normal(jax.random.fold_in(key, 601), (D, D), jnp.float32), -4.0, 4.0) / math.sqrt(D)
    other = jnp.clip(jax.random.normal(jax.random.fold_in(key, 602), (D, D), jnp.float32), -4.0, 4.0) / math.sqrt(D)
    return (base, other)


def draw_w_query(key, part):
    return projection_pair(key)[0].astype(jnp.bfloat16)


def draw_w_key(key, part):
    return projection_pair(key)[1].astype(jnp.bfloat16)


def draw_features(key, part):
    drawn = jax.random.normal(jax.random.fold_in(key, 704), (NODES, D), jnp.float32)
    return jnp.clip(drawn, -4.0, 4.0).astype(jnp.bfloat16)


def strengthened(values, rng, source, target, parts, factor):
    owner, partner = [(jnp.arange(values.shape[dim]) // (values.shape[dim] // parts)).reshape([-1 if axis == dim else 1 for axis in range(values.ndim)]) for dim in (source, target)]
    chosen = jax.random.permutation(rng, parts)[partner]
    strong = (owner == chosen) | (owner == (partner + parts // 2) % parts)
    return jnp.where(strong, factor * values, values)


def steps_of(rng, extent, cuts, smallest, largest):
    def one(dim, blocks):
        steps = jax.random.uniform(jax.random.fold_in(jax.random.fold_in(rng, 6), dim), (blocks,), jnp.float32, smallest / len(cuts), largest / len(cuts))
        return jnp.repeat(jnp.exp(steps), extent[dim] // blocks).reshape((-1,) + (1,) * (len(extent) - dim - 1))

    gain = one(*cuts[0])
    for cut in cuts[1:]:
        gain = gain * one(*cut)
    return gain


def scatter_about(key, dims, scale, reach, cuts=(), held_as=jnp.bfloat16):
    values = jax.random.normal(key, dims, jnp.float32) * scale
    if len(cuts) > 0:
        values = steps_of(key, dims, cuts, -0.22, 0.18) * values
    return jnp.clip(values, min=-reach, max=reach).astype(held_as)


def noise_with(stream_key, dims, scale, limit, shards, heavy, kind=jnp.bfloat16):
    entries = scale * jax.random.normal(stream_key, dims, jnp.float32)
    if shards:
        entries = entries * steps_of(stream_key, dims, shards, -0.22, 0.18)
    return jnp.clip(strengthened(entries, jax.random.fold_in(stream_key, 3), *heavy), -limit, limit).astype(kind)


def setup_inputs(seed: int = 0) -> dict:
    splits = jax.random.split(jax.random.key(seed), 10)
    features = draw_features(jax.random.fold_in(splits[9], 71), 0)
    w_query = draw_w_query(jax.random.fold_in(splits[9], 71), 0)
    w_key = draw_w_key(jax.random.fold_in(splits[9], 71), 0)
    w_value = scatter_about(splits[3], (D, D), D ** -0.5, 0.1875, ((1, 16),))
    w_output = scatter_about(splits[4], (D, D), D ** -0.5, 0.1875, ((0, 16),))
    cotangent = noise_with(splits[5], (NODES, D), 1.0, 24.0, ((0, 256),), (0, 1, 256, 6.0))
    cross_source = draw_cross_source(jax.random.fold_in(splits[9], 71), 0)
    cross_target = draw_cross_target(jax.random.fold_in(splits[9], 71), 0)
    cross_count = draw_cross_count(jax.random.fold_in(splits[9], 71), 0)
    return dict(features=features, w_query=w_query, w_key=w_key, w_value=w_value, w_output=w_output, cotangent=cotangent, cross_source=cross_source, cross_target=cross_target, cross_count=cross_count)


NEG_FILL = -1e+30

def rounded(array):
    return lax.optimization_barrier(array.astype(jnp.bfloat16)).astype(jnp.float32)

def select_table(target, live_count):
    slot_ids = jnp.arange(CMAX, dtype=jnp.int32)
    block_ids = jnp.arange(NBLK_P, dtype=jnp.int32)
    return (target[None, :] == block_ids[:, None]) & (slot_ids < live_count)[None, :]

def gather_extra(chosen, source, key_blocks, value_blocks):
    picker = chosen.astype(jnp.float32)
    extra_keys = jnp.einsum('tj,jbhd->tbhd', picker, key_blocks[source].astype(jnp.float32), precision=lax.Precision.HIGHEST)
    extra_values = jnp.einsum('tj,jbhd->tbhd', picker, value_blocks[source].astype(jnp.float32), precision=lax.Precision.HIGHEST)
    return (extra_keys.astype(jnp.bfloat16), extra_values.astype(jnp.bfloat16))

def part_probs(part_queries, part_keys, extra_keys, usable):
    scaling = 1.0 / math.sqrt(HD)
    query_f = part_queries.astype(jnp.float32)
    local_scores = jnp.einsum('tbhd,nhd->thbn', query_f, part_keys.astype(jnp.float32)) * scaling
    extra_scores = jnp.einsum('tbhd,tehd->thbe', query_f, extra_keys.astype(jnp.float32)) * scaling
    extra_scores = jnp.where(usable[:, None, None, None], extra_scores, NEG_FILL)
    highest = jnp.maximum(lax.optimization_barrier(jnp.max(local_scores, -1)), lax.optimization_barrier(jnp.max(extra_scores, -1)))[..., None]
    local_exp = jnp.exp(local_scores - highest)
    extra_exp = jnp.exp(extra_scores - highest)
    denominator = lax.optimization_barrier(jnp.sum(local_exp, -1, keepdims=True)) + lax.optimization_barrier(jnp.sum(extra_exp, -1, keepdims=True))
    return (local_exp / denominator, extra_exp / denominator)

def reference(features, w_query, w_key, w_value, w_output, cotangent, cross_source, cross_target, cross_count):
    scaling = 1.0 / math.sqrt(HD)
    queries = jnp.dot(features, w_query, preferred_element_type=jnp.float32).astype(jnp.bfloat16)
    keys = jnp.dot(features, w_key, preferred_element_type=jnp.float32).astype(jnp.bfloat16)
    values = jnp.dot(features, w_value, preferred_element_type=jnp.float32).astype(jnp.bfloat16)
    shape_five = (PARTS_SIZE, NBLK_P, BLK, H, HD)
    queries_five = queries.reshape(shape_five)
    keys_part = keys.reshape(PARTS_SIZE, P_NODES, H, HD)
    values_part = values.reshape(PARTS_SIZE, P_NODES, H, HD)
    key_blocks = keys.reshape(PARTS_SIZE * NBLK_P, BLK, H, HD)
    value_blocks = values.reshape(PARTS_SIZE * NBLK_P, BLK, H, HD)

    def part_forward(inputs):
        part_queries, part_keys, part_values, source, target, live_count = inputs
        chosen = select_table(target, live_count)
        extra_keys, extra_values = gather_extra(chosen, source, key_blocks, value_blocks)
        usable = jnp.any(chosen, 1)
        local_probs, extra_probs = part_probs(part_queries, part_keys, extra_keys, usable)
        attended_part = jnp.einsum('thbn,nhd->tbhd', rounded(local_probs), part_values.astype(jnp.float32))
        attended_part = attended_part + jnp.einsum('thbe,tehd->tbhd', rounded(extra_probs), extra_values.astype(jnp.float32))
        return attended_part.astype(jnp.bfloat16)
    attended = lax.map(part_forward, (queries_five, keys_part, values_part, cross_source, cross_target, cross_count))
    attended_flat = attended.reshape(NODES, D)
    layer_out = (features.astype(jnp.float32) + jnp.dot(attended_flat, w_output, preferred_element_type=jnp.float32)).astype(jnp.bfloat16)
    w_output_grad_t = jnp.dot(cotangent.T, attended_flat, preferred_element_type=jnp.float32)
    grad_attended = jnp.dot(cotangent, w_output.T, preferred_element_type=jnp.float32).astype(jnp.bfloat16)
    grad_attended_five = grad_attended.reshape(shape_five)

    def part_backward(inputs):
        part_queries, part_keys, part_values, source, target, live_count, attended_part, grad_part = inputs
        chosen = select_table(target, live_count)
        extra_keys, extra_values = gather_extra(chosen, source, key_blocks, value_blocks)
        usable = jnp.any(chosen, 1)
        local_probs, extra_probs = part_probs(part_queries, part_keys, extra_keys, usable)
        grad_f = grad_part.astype(jnp.float32)
        query_f = part_queries.astype(jnp.float32)
        row_delta = lax.optimization_barrier(jnp.sum(grad_f * attended_part.astype(jnp.float32), -1))
        row_delta = jnp.transpose(row_delta, (0, 2, 1))[..., None]
        local_dprob = jnp.einsum('tbhd,nhd->thbn', grad_f, part_values.astype(jnp.float32))
        extra_dprob = jnp.einsum('tbhd,tehd->thbe', grad_f, extra_values.astype(jnp.float32))
        local_dscore = rounded(local_probs * (local_dprob - row_delta) * scaling)
        extra_dscore = rounded(extra_probs * (extra_dprob - row_delta) * scaling)
        grad_q = jnp.einsum('thbn,nhd->tbhd', local_dscore, part_keys.astype(jnp.float32))
        grad_q = (grad_q + jnp.einsum('thbe,tehd->tbhd', extra_dscore, extra_keys.astype(jnp.float32))).astype(jnp.bfloat16)
        key_local = jnp.einsum('thbn,tbhd->nhd', local_dscore, query_f)
        value_local = jnp.einsum('thbn,tbhd->nhd', rounded(local_probs), grad_f)
        extra_dkey = jnp.einsum('thbe,tbhd->tehd', extra_dscore, query_f)
        extra_dvalue = jnp.einsum('thbe,tbhd->tehd', rounded(extra_probs), grad_f)
        picker = chosen.astype(jnp.float32)
        slot_dkey = jnp.einsum('tj,tehd->jehd', picker, extra_dkey, precision=lax.Precision.HIGHEST)
        slot_dvalue = jnp.einsum('tj,tehd->jehd', picker, extra_dvalue, precision=lax.Precision.HIGHEST)
        return (grad_q, key_local, value_local, slot_dkey, slot_dvalue)
    grad_q, key_local, value_local, slot_dkey, slot_dvalue = lax.map(part_backward, (queries_five, keys_part, values_part, cross_source, cross_target, cross_count, attended, grad_attended_five))
    flat_source = cross_source.reshape(-1)
    key_total = key_local.reshape(PARTS_SIZE * NBLK_P, BLK, H, HD).at[flat_source].add(slot_dkey.reshape(PARTS_SIZE * CMAX, BLK, H, HD))
    value_total = value_local.reshape(PARTS_SIZE * NBLK_P, BLK, H, HD).at[flat_source].add(slot_dvalue.reshape(PARTS_SIZE * CMAX, BLK, H, HD))
    grad_queries = grad_q.reshape(NODES, D)
    grad_keys = key_total.reshape(NODES, D).astype(jnp.bfloat16)
    grad_values = value_total.reshape(NODES, D).astype(jnp.bfloat16)
    back_sum = jnp.dot(grad_queries, w_query.T, preferred_element_type=jnp.float32)
    back_sum = back_sum + jnp.dot(grad_keys, w_key.T, preferred_element_type=jnp.float32)
    back_sum = back_sum + jnp.dot(grad_values, w_value.T, preferred_element_type=jnp.float32)
    grad_features = (cotangent.astype(jnp.float32) + back_sum).astype(jnp.bfloat16)
    w_query_grad = jnp.dot(features.T, grad_queries, preferred_element_type=jnp.float32)
    w_key_grad = jnp.dot(features.T, grad_keys, preferred_element_type=jnp.float32)
    w_value_grad = jnp.dot(features.T, grad_values, preferred_element_type=jnp.float32)
    return (layer_out, grad_features, w_query_grad, w_key_grad, w_value_grad, w_output_grad_t)
```

```python
import functools
import math

import jax
import jax.numpy as jnp
from jax import lax
from jax.experimental import pallas as pl
from jax.experimental.pallas import tpu as pltpu
from jax.sharding import PartitionSpec as P

HD = 64
BLK = 128
CAP = 2
X = 4
Y = 4
Z = 8
PARTS = 16
NBLK = 16
WIDTH = 1024
GROUP = 256
CHUNK = 512
NEG_FILL = -1e30
MESH = pl.DeviceIdType.MESH
BF = jnp.bfloat16
F32 = jnp.float32


def mm(a, b):
    return jnp.dot(a, b, preferred_element_type=F32)


def mm_nt(a, b):
    return lax.dot_general(a, b, (((1,), (1,)), ((), ())), preferred_element_type=F32)


def place():
    d = lax.axis_index("dom")
    h = lax.axis_index("head")
    return d, lax.div(h, Y), lax.rem(h, Y)


def greet(peers):
    barrier = pltpu.get_barrier_semaphore()
    for peer in peers:
        pl.semaphore_signal(barrier, inc=1, device_id=peer, device_id_type=MESH)
    pl.semaphore_wait(barrier, len(peers))


def lanes(shape):
    return lax.broadcasted_iota(jnp.int32, shape, len(shape) - 1)


def gather_kernel(
    feat, cot, w, req, qkvg, feat_t, cot_t, w_all, asked, feat_all, cot_all, stage,
    xs, xr, ys, yr, ds, dr, as_, ar,
):
    d, x, y = place()

    def dev(dd, xx, yy):
        return (dd, xx * Y + yy)

    xp, xm = lax.rem(x + 1, X), lax.rem(x + 3, X)
    yp, ym = lax.rem(y + 1, Y), lax.rem(y + 3, Y)
    x2, y2 = lax.rem(x + 2, X), lax.rem(y + 2, Y)
    right, left = dev(d, xp, y), dev(d, xm, y)
    up, down = dev(d, x, yp), dev(d, x, ym)
    across = dev(d, x, y2)
    doms = [lax.rem(d + k, PARTS) for k in range(1, PARTS)]
    greet([right, left, up, down, across] + [dev(q, x, y) for q in doms])

    def send(src, dst, s, r, to):
        c = pltpu.make_async_remote_copy(
            src_ref=src, dst_ref=dst, send_sem=s, recv_sem=r, device_id=to, device_id_type=MESH
        )
        c.start()
        return c

    pend = []
    for k, q in enumerate(doms):
        pend.append(send(req.at[q], asked.at[d], ds.at[k], dr.at[k], dev(q, x, y)))
    tables = list(pend)
    first = []
    for i, (own, full) in enumerate(((feat, feat_all), (cot, cot_all))):
        first.append(
            (
                send(own, full.at[x], xs.at[4 * i], xr.at[4 * i], right),
                send(own, full.at[x], xs.at[4 * i + 1], xr.at[4 * i + 1], left),
            )
        )
    wfirst = (
        send(w, w_all.at[y], ys.at[0], yr.at[0], up),
        send(w, w_all.at[y], ys.at[1], yr.at[1], down),
    )
    asked[d] = jnp.zeros((8, 128), jnp.int32)
    feat_all[x] = feat[...]
    cot_all[x] = cot[...]
    w_all[y] = w[...]
    rows, half = BLK // 2, WIDTH // 2
    second = []
    for i, full in enumerate((feat_all, cot_all)):
        a, b = first[i]
        a.wait_recv()
        second.append(
            send(
                full.at[xm, pl.ds(0, rows)], full.at[xm, pl.ds(0, rows)],
                xs.at[4 * i + 2], xr.at[4 * i + 2], right,
            )
        )
        b.wait_recv()
        second.append(
            send(
                full.at[xp, pl.ds(rows, rows)], full.at[xp, pl.ds(rows, rows)],
                xs.at[4 * i + 3], xr.at[4 * i + 3], left,
            )
        )
        pend += [a, b]
    wfirst[0].wait_recv()
    second.append(
        send(w_all.at[ym, pl.ds(0, half)], w_all.at[ym, pl.ds(0, half)], ys.at[2], yr.at[2], up)
    )
    wfirst[1].wait_recv()
    second.append(
        send(
            w_all.at[yp, pl.ds(half, half)], w_all.at[yp, pl.ds(half, half)],
            ys.at[3], yr.at[3], down,
        )
    )
    pend += list(wfirst)
    for c in second:
        c.wait_recv()
    pend += second
    fa = feat_all[...].reshape(X * BLK, WIDTH)
    ca = cot_all[...].reshape(X * BLK, WIDTH)
    picked = lanes((X * BLK, 256)) < 192

    def project(h):
        return jnp.where(picked, mm(fa, w_all[h]), mm(ca, w_all[h])).astype(BF).reshape(X, BLK, 256)

    back = []
    for k, (yy, to) in enumerate(((y2, across), (yp, up), (ym, down))):
        stage[k] = project(yy)
        back.append(send(stage.at[k], qkvg.at[y], as_.at[k], ar.at[k], to))
    qkvg[y] = project(y)
    for i in range(X):
        cols = pl.ds(i * BLK, BLK)
        feat_t[:, cols] = jnp.transpose(feat_all[i])
        cot_t[:, cols] = jnp.transpose(cot_all[i])
    for c in back + tables:
        c.wait_recv()
    pend += back
    for c in pend:
        c.wait_send()


def attention_kernel(
    asked, tab, qkvg, gqa, dkv, returned,
    outgoing, incoming, sending, probs, scores, kvt, qd, accq, outl, att, mrow, lrow, rl_s, rd_s,
    egrad, ks, kr, gs, gr,
):
    d, x, y = place()
    doms = [lax.rem(d + k, PARTS) for k in range(1, PARTS)]
    head = x * Y + y
    greet([(q, head) for q in doms])

    def send(src, dst, s, r, to):
        c = pltpu.make_async_remote_copy(
            src_ref=src, dst_ref=dst, send_sem=s, recv_sem=r, device_id=to, device_id_type=MESH
        )
        c.start()
        return c

    going = []
    for k, q in enumerate(doms):
        for c in range(CAP):
            outgoing[k, c] = qkvg[asked[q * CAP + c], :, :128]
        going.append(
            send(outgoing.at[k], incoming.at[pl.ds(d * CAP, CAP)], ks.at[k], kr.at[k], (q, head))
        )
    incoming[pl.ds(d * CAP, CAP)] = jnp.zeros((CAP, BLK, 128), BF)
    returned[pl.ds(d * CAP, CAP)] = jnp.zeros((CAP, BLK, 128), BF)
    low1 = lanes((BLK, 128)) < HD
    low2 = lanes((GROUP, 128)) < HD
    for s in range(NBLK):
        c, i = s // 4, s % 4
        kvt[c, :, pl.ds(i * 128, 128)] = jnp.transpose(qkvg[s, :, :128])
        part = qkvg[s, :, 128:]
        qd[s] = jnp.where(low1, part * 0.125, part)
    dkv[...] = jnp.zeros_like(dkv)

    nchunk = NBLK * BLK // CHUNK

    def fold(v, op):
        out = v[:, 0:128]
        for j in range(1, CHUNK // 128):
            out = op(out, v[:, j * 128 : (j + 1) * 128])
        return out

    def forward(g, _):
        part = qd[pl.ds(2 * g, 2)].reshape(GROUP, 128)
        qs = jnp.where(low2, part, jnp.zeros_like(part))
        top = None
        for c in range(nchunk):
            s = mm(qs, kvt[c])
            scores[c] = s
            t = fold(s, jnp.maximum)
            top = t if top is None else jnp.maximum(top, t)
        m = jnp.max(top, 1, keepdims=True)
        total, out = None, None
        for c in range(nchunk):
            e = jnp.exp(scores[c] - m)
            t = fold(e, jnp.add)
            total = t if total is None else total + t
            eb = e.astype(BF)
            probs[g, c] = eb
            o = mm(eb, qkvg[4 * c : 4 * c + 4, :, :128].reshape(CHUNK, 128))
            out = o if out is None else out + o
        l = jnp.sum(total, 1, keepdims=True)
        outl[pl.ds(2 * g, 2)] = out.reshape(2, BLK, 128)
        mrow[pl.ds(2 * g, 2)] = jnp.broadcast_to(m, (GROUP, 128)).reshape(2, BLK, 128)
        lrow[pl.ds(2 * g, 2)] = jnp.broadcast_to(l, (GROUP, 128)).reshape(2, BLK, 128)
        return 0

    lax.fori_loop(0, NBLK // 2, forward, 0)
    for c in going:
        c.wait_recv()

    def extra(s, _):
        blk = qd[s]
        zero = jnp.zeros_like(blk)
        ekv = incoming[tab[s]]
        se = mm_nt(jnp.where(low1, blk, zero), ekv)
        se = jnp.where(tab[NBLK + s] > 0, se, NEG_FILL)
        ml, ll = mrow[s], lrow[s]
        big = jnp.maximum(ml, jnp.max(se, 1, keepdims=True))
        c = jnp.exp(ml - big)
        ee = jnp.exp(se - big)
        l = c * ll + jnp.sum(ee, 1, keepdims=True)
        r = 1.0 / l
        pe = ee * r
        peb = pe.astype(BF)
        rl = c * r
        a = (outl[s] * rl + mm(peb, ekv)).astype(BF)
        go = jnp.where(low1, zero, blk)
        delta = jnp.sum(go.astype(F32) * a.astype(F32), 1, keepdims=True)
        dse = (pe * (mm_nt(go, ekv) - delta)).astype(BF)
        accq[s] = mm(dse, ekv)
        att[s] = a
        rl_s[s] = rl
        rd_s[s] = rl * delta
        bt = jnp.transpose(blk)
        egrad[s, 0:HD] = mm(bt[0:HD], dse).astype(BF)
        egrad[s, HD:128] = mm(bt[HD:128], peb).astype(BF)
        return 0

    lax.fori_loop(0, NBLK, extra, 0)
    home = []
    for k, q in enumerate(doms):
        for c in range(CAP):
            slot = q * CAP + c
            got = egrad[tab[2 * NBLK + slot]]
            sending[k, c] = jnp.where(
                tab[2 * NBLK + PARTS * CAP + slot] > 0, got, jnp.zeros_like(got)
            )
        home.append(
            send(sending.at[k], returned.at[pl.ds(d * CAP, CAP)], gs.at[k], gr.at[k], (q, head))
        )

    def backward(g, _):
        part = qd[pl.ds(2 * g, 2)].reshape(GROUP, 128)
        rl = rl_s[pl.ds(2 * g, 2)].reshape(GROUP, 128)
        rd = rd_s[pl.ds(2 * g, 2)].reshape(GROUP, 128)[:, :1]
        z = jnp.where(low2, part, (part.astype(F32) * rl).astype(BF))
        zt = jnp.transpose(z)
        go = jnp.where(low2, jnp.zeros_like(z), z)
        dq = accq[pl.ds(2 * g, 2)].reshape(GROUP, 128)
        for c in range(nchunk):
            dp = mm(go, kvt[c])
            eb = probs[g, c]
            dsc = eb * (dp - rd).astype(BF)
            dq = dq + mm(dsc, qkvg[4 * c : 4 * c + 4, :, :128].reshape(CHUNK, 128))
            dk = mm(zt[0:HD], dsc)
            dv = mm(zt[HD:128], eb)
            for i in range(CHUNK // 128):
                dkv[4 * c + i, 0:HD] += dk[:, i * 128 : (i + 1) * 128]
                dkv[4 * c + i, HD:128] += dv[:, i * 128 : (i + 1) * 128]
        both = jnp.where(low2, (dq * 0.125).astype(BF), att[pl.ds(2 * g, 2)].reshape(GROUP, 128))
        gqa[pl.ds(2 * g, 2)] = both.reshape(2, BLK, 128)
        return 0

    lax.fori_loop(0, NBLK // 2, backward, 0)
    for c in home:
        c.wait_recv()
    for c in going + home:
        c.wait_send()


def scatter_kernel(asked, dkv, returned, gkv, acc):
    acc[...] = dkv[...]

    def add(r, _):
        acc[asked[r]] += returned[r].astype(F32)
        return 0

    lax.fori_loop(0, PARTS * CAP, add, 0)

    def turn(s, _):
        gkv[s] = jnp.transpose(acc[s]).astype(BF)
        return 0

    lax.fori_loop(0, NBLK, turn, 0)


def reduce_kernel(
    gkv, gqa, feat, cot, w_all, feat_t, cot_t, lo, gf, wg,
    g_kv, g_qa, own, part, rs, wgf, sibs, sibr, ysend, yrecv, zsend, zrecv,
    as_, ar, xs, xr, ss, sr, ys, yr, zs, zr,
):
    d, x, y = place()
    core = lax.rem(d, 2)
    z = lax.div(d, 2)

    def dev(dd, xx, yy):
        return (dd, xx * Y + yy)

    ysteps = [lax.rem(y + k, Y) for k in (2, 1, 3)]
    xsteps = [lax.rem(x + k, X) for k in (2, 1, 3)]
    zsteps = [lax.rem(z + k, Z) for k in (4, 3, 5, 2, 6, 1, 7)]
    sibling = dev(d + 1 - 2 * core, x, y)
    greet(
        [dev(d, x, yy) for yy in ysteps]
        + [dev(d, xx, y) for xx in xsteps]
        + [dev(zz * 2 + core, x, y) for zz in zsteps]
        + [sibling]
    )

    def send(src, dst, s, r, to):
        c = pltpu.make_async_remote_copy(
            src_ref=src, dst_ref=dst, send_sem=s, recv_sem=r, device_id=to, device_id_type=MESH
        )
        c.start()
        return c

    a2a = []
    for k, yy in enumerate(ysteps):
        a2a.append(send(gkv.at[yy], g_kv.at[y], as_.at[2 * k], ar.at[2 * k], dev(d, x, yy)))
        a2a.append(
            send(gqa.at[yy], g_qa.at[y], as_.at[2 * k + 1], ar.at[2 * k + 1], dev(d, x, yy))
        )
    g_kv[y] = gkv[y]
    g_qa[y] = gqa[y]
    for c in a2a:
        c.wait_recv()
    rows = X * BLK
    picked = lanes((rows, 256)) < 192
    for n in range(4):
        f, o = None, None
        for h in range(Y):
            g = jnp.concatenate([g_kv[h].reshape(rows, 128), g_qa[h].reshape(rows, 128)], 1)
            wn = w_all[h, n * 256 : (n + 1) * 256, :]
            zero = jnp.zeros_like(g)
            f1 = mm_nt(jnp.where(picked, g, zero), wn)
            o1 = mm_nt(jnp.where(picked, zero, g), wn)
            f, o = (f1, o1) if f is None else (f + f1, o + o1)
        cols = pl.ds(n * 256, 256)
        part[:, 0, :, cols] = o.astype(BF).reshape(X, BLK, 256)
        part[:, 1, :, cols] = f.astype(BF).reshape(X, BLK, 256)
    rsum = []
    for k, xx in enumerate(xsteps):
        rsum.append(send(part.at[xx], rs.at[k], xs.at[k], xr.at[k], dev(d, xx, y)))
    picked_w = lanes((WIDTH, 256)) < 192
    sib = []
    for h in range(Y):
        g = jnp.concatenate([g_kv[h].reshape(rows, 128), g_qa[h].reshape(rows, 128)], 1)
        full = jnp.where(picked_w, mm(feat_t[...], g), mm(cot_t[...], g)).reshape(Z, 2, 64, 256)
        wgf[h] = full
        sibs[h] = wgf[h, :, 1 - core].astype(BF)
        sib.append(send(sibs.at[h], sibr.at[h], ss.at[h], sr.at[h], sibling))
    for c in sib:
        c.wait_recv()
    ysum = []
    for k, yy in enumerate(ysteps):
        ysend[k] = (wgf[yy, :, core] + sibr[yy].astype(F32)).astype(BF)
        ysum.append(send(ysend.at[k], yrecv.at[k], ys.at[k], yr.at[k], dev(d, x, yy)))
    total = wgf[y, :, core] + sibr[y].astype(F32)
    for c in rsum:
        c.wait_recv()
    base = part[x].astype(F32)
    for k in range(3):
        base = base + rs[k].astype(F32)
    lo[...] = (feat[...].astype(F32) + base[0]).astype(BF)
    gf[...] = (cot[...].astype(F32) + base[1]).astype(BF)
    for k in range(3):
        ysum[k].wait_recv()
        total = total + yrecv[k].astype(F32)
    zsend[...] = total.astype(BF)
    own[...] = total
    zsum = []
    for k, zz in enumerate(zsteps):
        zsum.append(
            send(zsend.at[zz], zrecv.at[k], zs.at[k], zr.at[k], dev(zz * 2 + core, x, y))
        )
    res = own[z]
    for k in range(7):
        zsum[k].wait_recv()
        res = res + zrecv[k].astype(F32)
    wg[...] = res
    for c in a2a + rsum + sib + ysum + zsum:
        c.wait_send()


VM = pl.BlockSpec(memory_space=pltpu.VMEM)
SM = pl.BlockSpec(memory_space=pltpu.SMEM)


def dma(n):
    return pltpu.SemaphoreType.DMA((n,))


def sds(shape, dtype):
    return jax.ShapeDtypeStruct(shape, dtype)


def params(cid):
    return pltpu.CompilerParams(
        collective_id=cid, has_side_effects=True, vmem_limit_bytes=56 * 1024 * 1024
    )


def turned(t):
    return (t % 4) * 4 + t // 4


def local(
    features, w_query, w_key, w_value, w_output, cotangent, cross_source, cross_target, cross_count
):
    source, target, live_count = cross_source[0], cross_target[0], cross_count[0]
    owners = source // NBLK
    slot_ids = jnp.arange(16, dtype=jnp.int32)
    earlier = (owners[:, None] == owners[None, :]) & (slot_ids[None, :] < slot_ids[:, None])
    position = jnp.sum(earlier.astype(jnp.int32), 1)
    slot = owners * CAP + position
    placed = slot[:, None] == jnp.arange(PARTS * CAP, dtype=jnp.int32)[None, :]
    live = slot_ids < live_count
    request = jnp.sum(jnp.where(placed, turned(source % NBLK)[:, None], 0), 0)
    req = jnp.pad(request.reshape(PARTS, 1, CAP), ((0, 0), (0, 7), (0, 126)))
    tpos = turned(target)
    chosen = (tpos[:, None] == slot_ids[None, :]) & live[:, None]
    alive = placed & live[:, None]
    tab = jnp.concatenate(
        [
            jnp.sum(jnp.where(chosen, slot[:, None], 0), 0),
            jnp.sum(chosen.astype(jnp.int32), 0),
            jnp.sum(jnp.where(alive, tpos[:, None], 0), 0),
            jnp.sum(alive.astype(jnp.int32), 0),
        ]
    )
    w = jnp.concatenate([w_key, w_value, w_query, w_output.T], 1)

    qkvg, feat_t, cot_t, w_all, asked = pl.pallas_call(
        gather_kernel,
        out_shape=(
            sds((Y, X, BLK, 256), BF),
            sds((WIDTH, X * BLK), BF),
            sds((WIDTH, X * BLK), BF),
            sds((Y, WIDTH, 256), BF),
            sds((PARTS, 8, 128), jnp.int32),
        ),
        in_specs=[VM] * 4,
        out_specs=(VM,) * 5,
        scratch_shapes=[
            pltpu.VMEM((X, BLK, WIDTH), BF),
            pltpu.VMEM((X, BLK, WIDTH), BF),
            pltpu.VMEM((3, X, BLK, 256), BF),
            dma(8), dma(8), dma(4), dma(4), dma(15), dma(15), dma(3), dma(3),
        ],
        compiler_params=params(1),
        name="gather_project",
    )(features, cotangent, w, req)
    asked = asked[:, 0, :CAP].reshape(PARTS * CAP)

    gqa, dkv, returned = pl.pallas_call(
        attention_kernel,
        out_shape=(
            sds((NBLK, BLK, 128), BF),
            sds((NBLK, 128, BLK), F32),
            sds((PARTS * CAP, 128, BLK), BF),
        ),
        in_specs=[SM, SM, VM],
        out_specs=(VM,) * 3,
        scratch_shapes=[
            pltpu.VMEM((15, CAP, BLK, 128), BF),
            pltpu.VMEM((PARTS * CAP, BLK, 128), BF),
            pltpu.VMEM((15, CAP, 128, BLK), BF),
            pltpu.VMEM((NBLK // 2, 4, GROUP, CHUNK), BF),
            pltpu.VMEM((4, GROUP, CHUNK), F32),
            pltpu.VMEM((4, 128, CHUNK), BF),
            pltpu.VMEM((NBLK, BLK, 128), BF),
            pltpu.VMEM((NBLK, BLK, 128), F32),
            pltpu.VMEM((NBLK, BLK, 128), F32),
            pltpu.VMEM((NBLK, BLK, 128), BF),
            pltpu.VMEM((NBLK, BLK, 128), F32),
            pltpu.VMEM((NBLK, BLK, 128), F32),
            pltpu.VMEM((NBLK, BLK, 128), F32),
            pltpu.VMEM((NBLK, BLK, 128), F32),
            pltpu.VMEM((NBLK, 128, BLK), BF),
            dma(15), dma(15), dma(15), dma(15),
        ],
        compiler_params=params(2),
        name="attention",
    )(asked, tab, qkvg.reshape(NBLK, BLK, 256))

    gkv = pl.pallas_call(
        scatter_kernel,
        out_shape=sds((NBLK, BLK, 128), BF),
        in_specs=[SM, VM, VM],
        out_specs=VM,
        scratch_shapes=[pltpu.VMEM((NBLK, 128, BLK), F32)],
        name="scatter_add",
    )(asked, dkv, returned)

    four = (Y, X, BLK, 128)
    layer_out, grad_features, wg = pl.pallas_call(
        reduce_kernel,
        out_shape=(
            sds((BLK, WIDTH), BF),
            sds((BLK, WIDTH), BF),
            sds((64, 256), F32),
        ),
        in_specs=[VM] * 7,
        out_specs=(VM,) * 3,
        scratch_shapes=[
            pltpu.VMEM(four, BF),
            pltpu.VMEM(four, BF),
            pltpu.VMEM((Z, 64, 256), F32),
            pltpu.VMEM((X, 2, BLK, WIDTH), BF),
            pltpu.VMEM((3, 2, BLK, WIDTH), BF),
            pltpu.VMEM((Y, Z, 2, 64, 256), F32),
            pltpu.VMEM((Y, Z, 64, 256), BF),
            pltpu.VMEM((Y, Z, 64, 256), BF),
            pltpu.VMEM((3, Z, 64, 256), BF),
            pltpu.VMEM((3, Z, 64, 256), BF),
            pltpu.VMEM((Z, 64, 256), BF),
            pltpu.VMEM((7, 64, 256), BF),
            dma(6), dma(6), dma(3), dma(3), dma(4), dma(4), dma(3), dma(3), dma(7), dma(7),
        ],
        compiler_params=params(3),
        name="project_reduce",
    )(gkv.reshape(four), gqa.reshape(four), features, cotangent, w_all, feat_t, cot_t)
    return (
        layer_out,
        grad_features,
        wg[:, 128:192],
        wg[:, 0:64],
        wg[:, 64:128],
        wg[:, 192:256],
    )


def solution(mesh):
    return jax.shard_map(
        local,
        mesh=mesh,
        in_specs=(
            P(("dom", "head"), None),
            P(None, "head"),
            P(None, "head"),
            P(None, "head"),
            P("head", None),
            P(("dom", "head"), None),
            P("dom", None),
            P("dom", None),
            P("dom"),
        ),
        out_specs=(
            P(("dom", "head"), None),
            P(("dom", "head"), None),
            P("dom", "head"),
            P("dom", "head"),
            P("dom", "head"),
            P("dom", "head"),
        ),
        check_vma=False,
    )
```

```python
import jax
import jax.numpy as jnp
from jax import lax
from jax.experimental import pallas as pl
from jax.experimental.pallas import tpu as pltpu
from jax.sharding import PartitionSpec as P

HD = 64
BLK = 128
CAP = 2
X = 4
Y = 4
Z = 8
PARTS = 16
NBLK = 16
WIDTH = 1024
GROUP = 256
CHUNK = 512
NEG_FILL = -1e30
MESH = pl.DeviceIdType.MESH
BF = jnp.bfloat16
F32 = jnp.float32


def mm(a, b):
    return jnp.dot(a, b, preferred_element_type=F32)


def mm_nt(a, b):
    return lax.dot_general(a, b, (((1,), (1,)), ((), ())), preferred_element_type=F32)


def place():
    d = lax.axis_index("dom")
    h = lax.axis_index("head")
    return d, lax.div(h, Y), lax.rem(h, Y)


def greet(peers):
    barrier = pltpu.get_barrier_semaphore()
    for peer in peers:
        pl.semaphore_signal(barrier, inc=1, device_id=peer, device_id_type=MESH)
    pl.semaphore_wait(barrier, len(peers))


def lanes(shape):
    return lax.broadcasted_iota(jnp.int32, shape, len(shape) - 1)


class Sems:
    def __init__(self, send, recv):
        self.send, self.recv, self.n, self.all = send, recv, 0, []

    def start(self, src, dst, to):
        c = pltpu.make_async_remote_copy(
            src_ref=src, dst_ref=dst, send_sem=self.send.at[self.n], recv_sem=self.recv.at[self.n],
            device_id=to, device_id_type=MESH,
        )
        c.start()
        self.n += 1
        self.all.append(c)
        return c


def order_tables(asked, table):
    sub = lax.broadcasted_iota(jnp.int32, (128, 128), 0)
    lane = lax.broadcasted_iota(jnp.int32, (128, 128), 1)
    a = jnp.where((sub & 7) < CAP, asked[...].reshape(128, 128), 99.0)
    b = jnp.transpose(a)
    one, zero = jnp.ones((128, 128), F32), jnp.zeros((128, 128), F32)
    lanef = lane.astype(F32)
    less = jnp.where((b < a) | ((b == a) & (lane < sub)), one, zero)
    rank = jnp.sum(less, 1, keepdims=True)
    hot = jnp.where(rank == lanef, one, zero)
    where_from = ((sub >> 3) * CAP + (sub & 7)).astype(F32)
    order = jnp.sum(hot * where_from, 0, keepdims=True)
    value = jnp.sum(hot * a, 0, keepdims=True)
    end = jnp.sum(jnp.where(a <= lanef, one, zero), 0, keepdims=True) - 1.0
    has = jnp.sum(jnp.where(a == lanef, one, zero), 0, keepdims=True)
    wide = jnp.broadcast_to(value, (8, 128))
    same = jnp.where(wide == pltpu.roll(wide, 1, 1), one[:8], zero[:8])
    row = sub[:8]
    out = jnp.where(row == 0, jnp.minimum(b[:8], 15.0), zero[:8])
    for i, v in ((1, order), (2, same), (3, jnp.maximum(end, 0.0)), (4, has)):
        out = jnp.where(row == i, jnp.broadcast_to(v, (8, 128)), out)
    table[...] = out.astype(jnp.int32)


def layer_kernel(
    tab, feat, cot, wk, wv, wq, wo, req,
    lo, gf, wg,
    feat_all, cot_all, wkv, wqo, feat_t, cot_t, asked, table, smem, kst, qst, kv_l, qg_l,
    outgoing, incoming, sending, returned, probs, scores, kvt, qd, accq, outl, mrow, lrow, rl_s, rd_s,
    dkv, egrad, runs, gkv, attp, gqp, g_kv, at_l, gq_l, part, rs, g2, wgf, sibs, sibr, ysend, yrecv,
    own, zsend, zrecv, send_sems, recv_sems, local_sem,
):
    d, x, y = place()
    core, z = lax.rem(d, 2), lax.div(d, 2)

    def dev(dd, xx, yy):
        return (dd, xx * Y + yy)

    xp, xm, x2 = [lax.rem(x + k, X) for k in (1, 3, 2)]
    yp, ym, y2 = [lax.rem(y + k, Y) for k in (1, 3, 2)]
    right, left, xopp = dev(d, xp, y), dev(d, xm, y), dev(d, x2, y)
    up, down, yopp = dev(d, x, yp), dev(d, x, ym), dev(d, x, y2)
    doms = [lax.rem(d + k, PARTS) for k in range(1, PARTS)]
    sibling = dev(d + 1 - 2 * core, x, y)
    greet([right, left, xopp, up, down, yopp] + [dev(q, x, y) for q in doms])
    net = Sems(send_sems, recv_sems)
    start = net.start
    ysteps = [(y2, yopp), (yp, up), (ym, down)]

    fl = start(feat, feat_all.at[x], right)
    fr = start(feat, feat_all.at[x], left)
    for i, (w, o) in enumerate(((wkv, (wk, wv)), (wqo, (wq, wo)))):
        w[y, 0:HD] = o[0][...]
        w[y, HD:128] = o[1][...]
    mine = pl.multiple_of(core * HD, HD)
    whole = pl.ds(mine, HD)
    upper, lower = pl.ds(mine, 32), pl.ds(mine + 32, 32)
    wown = []
    for w in (wkv, wqo):
        piece = w.at[y, whole]
        wown.append((start(piece, piece, up), start(piece, piece, down)))
    tables = [start(req.at[q], asked.at[d], dev(q, x, y)) for q in doms]
    asked[d] = jnp.full((8, 128), 99.0, F32)
    feat_all[x] = feat[...]
    cot_all[x] = cot[...]

    def wmiddle(i):
        w = (wkv, wqo)[i]
        a, b = wown[i]
        a.wait_recv()
        p = w.at[ym, upper]
        f1 = start(p, p, up)
        p = w.at[ym, whole]
        s1 = start(p, p, sibling)
        b.wait_recv()
        p = w.at[yp, lower]
        f2 = start(p, p, down)
        p = w.at[yp, whole]
        s2 = start(p, p, sibling)
        return f1, f2, s1, s2

    def wlast(i, mid):
        w = (wkv, wqo)[i]
        mid[0].wait_recv()
        mid[1].wait_recv()
        p = w.at[y2, whole]
        s3 = start(p, p, sibling)
        mid[2].wait_recv()
        mid[3].wait_recv()
        s3.wait_recv()

    def xmiddle(full, a, b):
        a.wait_recv()
        p = full.at[xm, pl.ds(0, HD)]
        f1 = start(p, p, right)
        b.wait_recv()
        p = full.at[xp, pl.ds(HD, HD)]
        f2 = start(p, p, left)
        return f1, f2

    mkv = wmiddle(0)
    ffwd = xmiddle(feat_all, fl, fr)
    cl = start(cot, cot_all.at[x], right)
    cr = start(cot, cot_all.at[x], left)
    mqo = wmiddle(1)
    wlast(0, mkv)
    low4 = (lanes((BLK, 512)) & 127) < HD

    def project_kv(b):
        r = mm_nt(feat_all[b], wkv[...].reshape(Y * 128, WIDTH)).astype(BF)
        for h in range(Y):
            kst[h, b] = r[:, h * 128 : (h + 1) * 128]
        kv_l[y, b] = kst[y, b]
        return [start(kst.at[yy, b], kv_l.at[y, b], to) for yy, to in ysteps]

    def project_qo(b):
        w = wqo[...].reshape(Y * 128, WIDTH)
        r = jnp.where(low4, mm_nt(feat_all[b], w), mm_nt(cot_all[b], w)).astype(BF)
        for h in range(Y):
            qst[h, b] = r[:, h * 128 : (h + 1) * 128]
        qg_l[y, b] = qst[y, b]
        return [start(qst.at[yy, b], qg_l.at[y, b], to) for yy, to in ysteps]

    def turn(full, b, out):
        out[b] = jnp.transpose(full[b])

    kvs = project_kv(x)
    kvs += project_kv(xm)
    kvs += project_kv(xp)
    for c in tables:
        c.wait_recv()
    order_tables(asked, table)
    cp = pltpu.make_async_copy(table, smem, local_sem)
    cp.start()
    for c in ffwd:
        c.wait_recv()
    kvs += project_kv(x2)
    wlast(1, mqo)
    qgs = project_qo(x)
    cfwd = xmiddle(cot_all, cl, cr)
    qgs += project_qo(xm)
    qgs += project_qo(xp)
    cp.wait()
    for c in kvs:
        c.wait_recv()

    going = []
    for k, q in enumerate(doms):
        for c in range(CAP):
            at = jnp.clip(smem[0, q * 8 + c], 0, NBLK - 1)
            outgoing[k, c] = kv_l[lax.div(at, 4), lax.rem(at, 4)]
        going.append(start(outgoing.at[k], incoming.at[pl.ds(d * CAP, CAP)], dev(q, x, y)))
    for c in cfwd:
        c.wait_recv()
    qgs += project_qo(x2)
    incoming[pl.ds(d * CAP, CAP)] = jnp.zeros((CAP, BLK, 128), BF)
    returned[pl.ds(d * CAP, CAP)] = jnp.zeros((CAP, BLK, 128), BF)
    for b in range(X):
        turn(feat_all, b, feat_t)
        turn(cot_all, b, cot_t)
    low1 = lanes((BLK, 128)) < HD
    low2 = lanes((GROUP, 128)) < HD
    for s in range(NBLK):
        kvt[s // 4, :, pl.ds((s % 4) * 128, 128)] = jnp.transpose(kv_l[s // 4, s % 4])
    for c in qgs:
        c.wait_recv()
    for s in range(NBLK):
        p = qg_l[s // 4, s % 4]
        qd[s] = jnp.where(low1, p * 0.125, p)
    dkv[...] = jnp.zeros_like(dkv)

    nchunk = NBLK * BLK // CHUNK

    def fold(v, op):
        out = v[:, 0:128]
        for j in range(1, CHUNK // 128):
            out = op(out, v[:, j * 128 : (j + 1) * 128])
        return out

    def forward(g, _):
        p = qd[pl.ds(2 * g, 2)].reshape(GROUP, 128)
        qs = jnp.where(low2, p, jnp.zeros_like(p))
        top = None
        for c in range(nchunk):
            s = mm(qs, kvt[c])
            scores[c] = s
            t = fold(s, jnp.maximum)
            top = t if top is None else jnp.maximum(top, t)
        m = jnp.max(top, 1, keepdims=True)
        total, out = None, None
        for c in range(nchunk):
            e = jnp.exp(scores[c] - m)
            t = fold(e, jnp.add)
            total = t if total is None else total + t
            eb = e.astype(BF)
            probs[g, c] = eb
            o = mm(eb, kv_l[c].reshape(CHUNK, 128))
            out = o if out is None else out + o
        l = jnp.sum(total, 1, keepdims=True)
        outl[pl.ds(2 * g, 2)] = out.reshape(2, BLK, 128)
        mrow[pl.ds(2 * g, 2)] = jnp.broadcast_to(m, (GROUP, 128)).reshape(2, BLK, 128)
        lrow[pl.ds(2 * g, 2)] = jnp.broadcast_to(l, (GROUP, 128)).reshape(2, BLK, 128)
        return 0

    lax.fori_loop(0, NBLK // 2, forward, 0)
    for c in going:
        c.wait_recv()

    def extra(s):
        blk = qd[s]
        zero = jnp.zeros_like(blk)
        ekv = incoming[tab[s]]
        se = mm_nt(jnp.where(low1, blk, zero), ekv)
        se = jnp.where(tab[NBLK + s] > 0, se, NEG_FILL)
        ml, ll = mrow[s], lrow[s]
        big = jnp.maximum(ml, jnp.max(se, 1, keepdims=True))
        c = jnp.exp(ml - big)
        ee = jnp.exp(se - big)
        l = c * ll + jnp.sum(ee, 1, keepdims=True)
        r = 1.0 / l
        pe = ee * r
        peb = pe.astype(BF)
        rl = c * r
        out = (outl[s] * rl + mm(peb, ekv)).astype(BF).astype(F32)
        go = jnp.where(low1, zero, blk)
        delta = jnp.sum(go.astype(F32) * out, 1, keepdims=True)
        dse = (pe * (mm_nt(go, ekv) - delta)).astype(BF)
        accq[s] = mm(dse, ekv)
        rl_s[s] = rl
        rd_s[s] = rl * delta
        bt = jnp.transpose(blk)
        egrad[s, 0:HD] = mm(bt[0:HD], dse).astype(BF)
        egrad[s, HD:128] = mm(bt[HD:128], peb).astype(BF)
        return out

    def extras(g, _):
        a, b = extra(2 * g), extra(2 * g + 1)
        attp[lax.div(g, 2), lax.rem(g, 2)] = jnp.where(low1, pltpu.roll(a, HD, 1), b).astype(BF)
        return 0

    lax.fori_loop(0, NBLK // 2, extras, 0)
    home = []
    for k, q in enumerate(doms):
        for c in range(CAP):
            slot = q * CAP + c
            got = egrad[tab[2 * NBLK + slot]]
            sending[k, c] = jnp.where(
                tab[2 * NBLK + PARTS * CAP + slot] > 0, got, jnp.zeros_like(got)
            )
        home.append(start(sending.at[k], returned.at[pl.ds(d * CAP, CAP)], dev(q, x, y)))
    ats = [start(attp.at[yy], at_l.at[y], to) for yy, to in ysteps]
    at_l[y] = attp[y]

    def backward(g, _):
        p = qd[pl.ds(2 * g, 2)].reshape(GROUP, 128)
        rl = rl_s[pl.ds(2 * g, 2)].reshape(GROUP, 128)
        rd = rd_s[pl.ds(2 * g, 2)].reshape(GROUP, 128)[:, :1]
        zz = jnp.where(low2, p, (p.astype(F32) * rl).astype(BF))
        zt = jnp.transpose(zz)
        go = jnp.where(low2, jnp.zeros_like(zz), zz)
        dq = accq[pl.ds(2 * g, 2)].reshape(GROUP, 128)
        for c in range(nchunk):
            dp = mm(go, kvt[c])
            eb = probs[g, c]
            dsc = eb * (dp - rd).astype(BF)
            dq = dq + mm(dsc, kv_l[c].reshape(CHUNK, 128))
            dk = mm(zt[0:HD], dsc)
            dv = mm(zt[HD:128], eb)
            for i in range(CHUNK // 128):
                dkv[4 * c + i, 0:HD] += dk[:, i * 128 : (i + 1) * 128]
                dkv[4 * c + i, HD:128] += dv[:, i * 128 : (i + 1) * 128]
        dq = dq * 0.125
        gqp[lax.div(g, 2), lax.rem(g, 2)] = jnp.where(
            low1, dq[0:BLK], pltpu.roll(dq[BLK:GROUP], HD, 1)
        ).astype(BF)
        return 0

    lax.fori_loop(0, NBLK // 2, backward, 0)
    gqs = [start(gqp.at[yy], gq_l.at[y], to) for yy, to in ysteps]
    gq_l[y] = gqp[y]

    rows = X * BLK
    for c in ats:
        c.wait_recv()
    for h in range(Y):
        for j in range(2):
            p = at_l[h, j].astype(F32)
            zero = jnp.zeros_like(p)
            g2[1, h, 2 * j] = jnp.where(low1, zero, pltpu.roll(p, HD, 1)).astype(BF)
            g2[1, h, 2 * j + 1] = jnp.where(low1, zero, p).astype(BF)
    for n in range(4):
        cols = pl.ds(n * 256, 256)
        o = None
        for h in range(Y):
            t = mm(g2[1, h].reshape(rows, 128), wqo[h, :, cols])
            o = t if o is None else o + t
        part[:, 0, :, cols] = o.astype(BF).reshape(X, BLK, 256)
    xsteps = [(x2, xopp), (xp, right), (xm, left)]
    los = [start(part.at[xx, 0], rs.at[k, 0], to) for k, (xx, to) in enumerate(xsteps)]

    def tmm(t, g):
        r = None
        for b in range(X):
            v = mm(t[b], g[b])
            r = v if r is None else r + v
        return r

    def weights(i, left_of):
        out = []
        for h in range(Y):
            wgf[i, h] = left_of(h).reshape(Z, 2, 64, 128)
            sibs[i, h] = wgf[i, h, :, 1 - core].astype(BF)
            out.append(start(sibs.at[i, h], sibr.at[i, h], sibling))
        return out

    def along_y(i, sib):
        for c in sib:
            c.wait_recv()
        out = []
        for k, (yy, to) in enumerate(ysteps):
            ysend[i, k] = (wgf[i, yy, :, core] + sibr[i, yy].astype(F32)).astype(BF)
            out.append(start(ysend.at[i, k], yrecv.at[i, k], to))
        return out

    zsteps = [lax.rem(z + k, Z) for k in (4, 3, 5, 2, 6, 1, 7)]

    def along_z(i, ys):
        total = wgf[i, y, :, core] + sibr[i, y].astype(F32)
        for k in range(3):
            ys[k].wait_recv()
            total = total + yrecv[i, k].astype(F32)
        own[i] = total
        zsend[i] = total.astype(BF)
        return [
            start(zsend.at[i, zz], zrecv.at[i, k], dev(zz * 2 + core, x, y))
            for k, zz in enumerate(zsteps)
        ]

    def finish(i, zsum):
        res = own[i, z]
        for k in range(7):
            zsum[k].wait_recv()
            res = res + zrecv[i, k].astype(F32)
        wg[:, i * 128 : (i + 1) * 128] = res

    for c in gqs:
        c.wait_recv()
    for h in range(Y):
        for j in range(2):
            p = gq_l[h, j].astype(F32)
            zero = jnp.zeros_like(p)
            g2[0, h, 2 * j] = jnp.where(low1, p, zero).astype(BF)
            g2[0, h, 2 * j + 1] = jnp.where(low1, pltpu.roll(p, HD, 1), zero).astype(BF)
    sib1 = weights(1, lambda h: tmm(feat_t, g2[0, h]) + tmm(cot_t, g2[1, h]))
    y1 = along_y(1, sib1)
    for c in home:
        c.wait_recv()
    running = None
    for k in range(CAP * (PARTS - 1)):
        got = returned[jnp.clip(smem[1, k], 0, PARTS * CAP - 1)].astype(F32)
        running = got if k == 0 else got + running * smem[2, k].astype(F32)
        runs[k] = running
    for s in range(NBLK):
        more = jnp.where(smem[4, s] > 0, runs[jnp.clip(smem[3, s], 0, CAP * (PARTS - 1) - 1)], jnp.zeros((128, BLK), F32))
        gkv[s // 4, s % 4] = jnp.transpose(dkv[s] + more).astype(BF)
    gks = [start(gkv.at[yy], g_kv.at[y], to) for yy, to in ysteps]
    g_kv[y] = gkv[y]
    z1 = along_z(1, y1)
    for c in gks:
        c.wait_recv()
    for n in range(4):
        cols = pl.ds(n * 256, 256)
        o = None
        for h in range(Y):
            t = mm(g2[0, h].reshape(rows, 128), wqo[h, :, cols])
            t = t + mm(g_kv[h].reshape(rows, 128), wkv[h, :, cols])
            o = t if o is None else o + t
        part[:, 1, :, cols] = o.astype(BF).reshape(X, BLK, 256)
    gfs = [start(part.at[xx, 1], rs.at[k, 1], to) for k, (xx, to) in enumerate(xsteps)]
    sib0 = weights(0, lambda h: tmm(feat_t, g_kv[h]))
    y0 = along_y(0, sib0)
    for i, (copies, base, out) in enumerate(((los, feat, lo), (gfs, cot, gf))):
        if i == 1:
            finish(1, z1)
            z0 = along_z(0, y0)
        total = part[x, i].astype(F32)
        for k in range(3):
            copies[k].wait_recv()
            total = total + rs[k, i].astype(F32)
        out[...] = (base[...].astype(F32) + total).astype(BF)
    finish(0, z0)
    for c in net.all:
        c.wait_send()


VM = pl.BlockSpec(memory_space=pltpu.VMEM)
SM = pl.BlockSpec(memory_space=pltpu.SMEM)
COPIES = 134


def sds(shape, dtype):
    return jax.ShapeDtypeStruct(shape, dtype)


def params(cid):
    return pltpu.CompilerParams(
        collective_id=cid, has_side_effects=True, vmem_limit_bytes=60 * 1024 * 1024
    )


def turned(t):
    return (t % 4) * 4 + t // 4


def local(
    features, w_query, w_key, w_value, w_output, cotangent, cross_source, cross_target, cross_count
):
    source, target, live_count = cross_source[0], cross_target[0], cross_count[0]
    owners = source // NBLK
    slot_ids = jnp.arange(16, dtype=jnp.int32)
    earlier = (owners[:, None] == owners[None, :]) & (slot_ids[None, :] < slot_ids[:, None])
    position = jnp.sum(earlier.astype(jnp.int32), 1)
    slot = owners * CAP + position
    placed = slot[:, None] == jnp.arange(PARTS * CAP, dtype=jnp.int32)[None, :]
    live = slot_ids < live_count
    row_slot = jnp.arange(PARTS * 8, dtype=jnp.int32)
    row_slot = jnp.where(row_slot % 8 < CAP, (row_slot // 8) * CAP + row_slot % 8, -1)
    placed_row = slot[:, None] == row_slot[None, :]
    request = jnp.sum(jnp.where(placed_row, turned(source % NBLK)[:, None], 0), 0)
    req = jnp.broadcast_to(request.astype(F32).reshape(PARTS, 8, 1), (PARTS, 8, 128))
    tpos = turned(target)
    chosen = (tpos[:, None] == slot_ids[None, :]) & live[:, None]
    alive = placed & live[:, None]
    tab = jnp.concatenate(
        [
            jnp.sum(jnp.where(chosen, slot[:, None], 0), 0),
            jnp.sum(chosen.astype(jnp.int32), 0),
            jnp.sum(jnp.where(alive, tpos[:, None], 0), 0),
            jnp.sum(alive.astype(jnp.int32), 0),
        ]
    )
    v = pltpu.VMEM
    full = (X, BLK, WIDTH)
    four = (Y, X, BLK, 128)
    pair = (Y, 2, BLK, 128)
    blocks = (NBLK, BLK, 128)
    layer_out, grad_features, wg = pl.pallas_call(
        layer_kernel,
        out_shape=(sds((BLK, WIDTH), BF), sds((BLK, WIDTH), BF), sds((64, 256), F32)),
        in_specs=[SM] + [VM] * 7,
        out_specs=(VM,) * 3,
        scratch_shapes=[
            v(full, BF), v(full, BF), v((Y, 128, WIDTH), BF), v((Y, 128, WIDTH), BF),
            v((X, WIDTH, BLK), BF), v((X, WIDTH, BLK), BF),
            v((PARTS, 8, 128), F32), v((8, 128), jnp.int32), pltpu.SMEM((8, 128), jnp.int32),
            v(four, BF), v(four, BF), v(four, BF), v(four, BF),
            v((15, CAP, BLK, 128), BF), v((PARTS * CAP, BLK, 128), BF),
            v((15, CAP, BLK, 128), BF), v((PARTS * CAP, BLK, 128), BF),
            v((NBLK // 2, 4, GROUP, CHUNK), BF), v((4, GROUP, CHUNK), F32), v((4, 128, CHUNK), BF),
            v(blocks, BF), v(blocks, F32), v(blocks, F32), v(blocks, F32), v(blocks, F32),
            v(blocks, F32), v(blocks, F32),
            v(blocks, F32), v(blocks, BF), v((30, 128, BLK), F32), v(four, BF),
            v(pair, BF), v(pair, BF), v(four, BF), v(pair, BF), v(pair, BF),
            v((X, 2, BLK, WIDTH), BF), v((3, 2, BLK, WIDTH), BF), v((2,) + four, BF),
            v((2, Y, Z, 2, 64, 128), F32), v((2, Y, Z, 64, 128), BF), v((2, Y, Z, 64, 128), BF),
            v((2, 3, Z, 64, 128), BF), v((2, 3, Z, 64, 128), BF),
            v((2, Z, 64, 128), F32), v((2, Z, 64, 128), BF), v((2, 7, 64, 128), BF),
            pltpu.SemaphoreType.DMA((COPIES,)), pltpu.SemaphoreType.DMA((COPIES,)),
            pltpu.SemaphoreType.DMA,
        ],
        compiler_params=params(1),
        name="layer",
    )(tab, features, cotangent, w_key.T, w_value.T, w_query.T, w_output, req)
    return (
        layer_out,
        grad_features,
        wg[:, 128:192],
        wg[:, 0:64],
        wg[:, 64:128],
        wg[:, 192:256],
    )


def solution(mesh):
    return jax.shard_map(
        local,
        mesh=mesh,
        in_specs=(
            P(("dom", "head"), None),
            P(None, "head"),
            P(None, "head"),
            P(None, "head"),
            P("head", None),
            P(("dom", "head"), None),
            P("dom", None),
            P("dom", None),
            P("dom"),
        ),
        out_specs=(
            P(("dom", "head"), None),
            P(("dom", "head"), None),
            P("dom", "head"),
            P("dom", "head"),
            P("dom", "head"),
            P("dom", "head"),
        ),
        check_vma=False,
    )
```

```python
import jax
import jax.numpy as jnp
from jax import lax
from jax.experimental import pallas as pl
from jax.experimental.pallas import tpu as pltpu
from jax.sharding import PartitionSpec as P

HD = 64
BLK = 128
CAP = 2
X = 4
Y = 4
Z = 8
PARTS = 16
NBLK = 16
WIDTH = 1024
GROUP = 256
CHUNK = 512
NEG_FILL = -1e30
MESH = pl.DeviceIdType.MESH
BF = jnp.bfloat16
F32 = jnp.float32


def mm(a, b):
    return jnp.dot(a, b, preferred_element_type=F32)


def mm_nt(a, b):
    return lax.dot_general(a, b, (((1,), (1,)), ((), ())), preferred_element_type=F32)


def place():
    d = lax.axis_index("dom")
    h = lax.axis_index("head")
    return d, lax.div(h, Y), lax.rem(h, Y)


def greet(peers, meanwhile):
    barrier = pltpu.get_barrier_semaphore()
    for peer in peers:
        pl.semaphore_signal(barrier, inc=1, device_id=peer, device_id_type=MESH)
    meanwhile()
    pl.semaphore_wait(barrier, len(peers))


def lanes(shape):
    return lax.broadcasted_iota(jnp.int32, shape, len(shape) - 1)


def turned(t):
    return lax.rem(t, 4) * 4 + lax.div(t, 4)


class Sems:
    def __init__(self, send, recv):
        self.send, self.recv, self.n, self.all = send, recv, 0, []

    def start(self, src, dst, to):
        c = pltpu.make_async_remote_copy(
            src_ref=src, dst_ref=dst, send_sem=self.send.at[self.n], recv_sem=self.recv.at[self.n],
            device_id=to, device_id_type=MESH,
        )
        c.start()
        self.n += 1
        self.all.append(c)
        return c


def slot_tables(source, target, count, req, table):
    sub = lax.broadcasted_iota(jnp.int32, (128, 128), 0)
    row = lax.broadcasted_iota(jnp.int32, (8, 128), 0)
    lane = lax.broadcasted_iota(jnp.int32, (8, 128), 1)
    ask = jnp.zeros((128, 128), jnp.int32)
    tab = jnp.zeros((8, 128), jnp.int32)
    owners = []
    for j in range(16):
        src, tgt = source[0, j], target[0, j]
        owner, block = lax.div(src, NBLK), lax.rem(src, NBLK)
        position = jnp.int32(0)
        for o in owners:
            position = position + jnp.where(o == owner, 1, 0)
        owners.append(owner)
        position = jnp.minimum(position, CAP - 1)
        ask = ask + jnp.where(sub == owner * 8 + position, turned(block), 0)
        slot, pos = owner * CAP + position, turned(tgt)
        live = jnp.where(count[0] > j, 1, 0)
        here, there = lane == pos, lane == slot
        tab = tab + jnp.where((row == 0) & here, slot * live, 0)
        tab = tab + jnp.where((row == 1) & here, live, 0)
        tab = tab + jnp.where((row == 2) & there, pos * live, 0)
        tab = tab + jnp.where((row == 3) & there, live, 0)
    req[...] = ask.astype(F32).reshape(PARTS, 8, 128)
    table[...] = tab


def order_tables(asked, table):
    sub = lax.broadcasted_iota(jnp.int32, (128, 128), 0)
    lane = lax.broadcasted_iota(jnp.int32, (128, 128), 1)
    a = jnp.where((sub & 7) < CAP, asked[...].reshape(128, 128), 99.0)
    b = jnp.transpose(a)
    one, zero = jnp.ones((128, 128), F32), jnp.zeros((128, 128), F32)
    lanef = lane.astype(F32)
    less = jnp.where((b < a) | ((b == a) & (lane < sub)), one, zero)
    rank = jnp.sum(less, 1, keepdims=True)
    hot = jnp.where(rank == lanef, one, zero)
    where_from = ((sub >> 3) * CAP + (sub & 7)).astype(F32)
    order = jnp.sum(hot * where_from, 0, keepdims=True)
    value = jnp.sum(hot * a, 0, keepdims=True)
    end = jnp.sum(jnp.where(a <= lanef, one, zero), 0, keepdims=True) - 1.0
    has = jnp.sum(jnp.where(a == lanef, one, zero), 0, keepdims=True)
    wide = jnp.broadcast_to(value, (8, 128))
    same = jnp.where(wide == pltpu.roll(wide, 1, 1), one[:8], zero[:8])
    row = sub[:8]
    out = jnp.where(row == 0, jnp.minimum(b[:8], 15.0), zero[:8])
    for i, v in ((1, order), (2, same), (3, jnp.maximum(end, 0.0)), (4, has)):
        out = jnp.where(row == i, jnp.broadcast_to(v, (8, 128)), out)
    table[...] = out.astype(jnp.int32)


def layer_kernel(
    source, target, count, feat, cot, wk, wv, wq, wo,
    lo, gf, wg,
    req, tab_v, tab, feat_all, cot_all, wkv, wqo, feat_t, cot_t, asked, table, smem, kst, qst, kv_l, qg_l,
    outgoing, incoming, sending, returned, probs, scores, kvt, qd, outl, mrow, lrow, rl_s, rd_s,
    dkv, egrad, dses, qdt, runs, gkv, attp, gqp, g_kv, at_l, gq_l, part, gfq, rs, g2, wgf, sibs, sibr, ysend, yrecv,
    own, zsend, zrecv, send_sems, recv_sems, local_sem, tab_sem,
):
    d, x, y = place()
    core, z = lax.rem(d, 2), lax.div(d, 2)

    def dev(dd, xx, yy):
        return (dd, xx * Y + yy)

    xp, xm, x2 = [lax.rem(x + k, X) for k in (1, 3, 2)]
    yp, ym, y2 = [lax.rem(y + k, Y) for k in (1, 3, 2)]
    right, left, xopp = dev(d, xp, y), dev(d, xm, y), dev(d, x2, y)
    up, down, yopp = dev(d, x, yp), dev(d, x, ym), dev(d, x, y2)
    doms = [lax.rem(d + k, PARTS) for k in range(1, PARTS)]
    sibling = dev(d + 1 - 2 * core, x, y)

    def prepare():
        slot_tables(source, target, count, req, tab_v)
        for w, o in ((wkv, (wk, wv)), (wqo, (wq, wo))):
            w[y, 0:HD] = o[0][...]
            w[y, HD:128] = o[1][...]
        asked[d] = jnp.full((8, 128), 99.0, F32)
        feat_all[x] = feat[...]
        cot_all[x] = cot[...]

    greet([right, left, xopp, up, down, yopp] + [dev(q, x, y) for q in doms], prepare)
    tp = pltpu.make_async_copy(tab_v, tab, tab_sem)
    tp.start()
    net = Sems(send_sems, recv_sems)
    start = net.start
    ysteps = [(y2, yopp), (yp, up), (ym, down)]

    fl = start(feat, feat_all.at[x], right)
    fr = start(feat, feat_all.at[x], left)
    mine = pl.multiple_of(core * HD, HD)
    whole = pl.ds(mine, HD)
    upper, lower = pl.ds(mine, 32), pl.ds(mine + 32, 32)
    wown = []
    for w in (wkv, wqo):
        piece = w.at[y, whole]
        wown.append((start(piece, piece, up), start(piece, piece, down)))
    tables = [start(req.at[q], asked.at[d], dev(q, x, y)) for q in doms]

    def wmiddle(i):
        w = (wkv, wqo)[i]
        a, b = wown[i]
        a.wait_recv()
        p = w.at[ym, upper]
        f1 = start(p, p, up)
        p = w.at[ym, whole]
        s1 = start(p, p, sibling)
        b.wait_recv()
        p = w.at[yp, lower]
        f2 = start(p, p, down)
        p = w.at[yp, whole]
        s2 = start(p, p, sibling)
        return f1, f2, s1, s2

    def wlast(i, mid):
        w = (wkv, wqo)[i]
        mid[0].wait_recv()
        mid[1].wait_recv()
        p = w.at[y2, whole]
        s3 = start(p, p, sibling)
        mid[2].wait_recv()
        mid[3].wait_recv()
        s3.wait_recv()

    def xmiddle(full, a, b):
        a.wait_recv()
        p = full.at[xm, pl.ds(0, HD)]
        f1 = start(p, p, right)
        b.wait_recv()
        p = full.at[xp, pl.ds(HD, HD)]
        f2 = start(p, p, left)
        return f1, f2

    mkv = wmiddle(0)
    ffwd = xmiddle(feat_all, fl, fr)
    mqo = wmiddle(1)
    wlast(0, mkv)
    low4 = (lanes((BLK, 512)) & 127) < HD

    def project_kv(b):
        r = mm_nt(feat_all[b], wkv[...].reshape(Y * 128, WIDTH)).astype(BF)
        for h in range(Y):
            kst[h, b] = r[:, h * 128 : (h + 1) * 128]
        kv_l[y, b] = kst[y, b]
        return [start(kst.at[yy, b], kv_l.at[y, b], to) for yy, to in ysteps]

    def project_qo(b):
        w = wqo[...].reshape(Y * 128, WIDTH)
        r = jnp.where(low4, mm_nt(feat_all[b], w), mm_nt(cot_all[b], w)).astype(BF)
        for h in range(Y):
            qst[h, b] = r[:, h * 128 : (h + 1) * 128]
        qg_l[y, b] = qst[y, b]
        return [start(qst.at[yy, b], qg_l.at[y, b], to) for yy, to in ysteps]

    kvs = project_kv(x)
    kvs += project_kv(xm)
    kvs += project_kv(xp)
    for c in tables:
        c.wait_recv()
    order_tables(asked, table)
    cp = pltpu.make_async_copy(table, smem, local_sem)
    cp.start()
    for c in ffwd:
        c.wait_recv()
    cl = start(cot, cot_all.at[x], right)
    cr = start(cot, cot_all.at[x], left)
    kvs += project_kv(x2)
    wlast(1, mqo)
    cp.wait()
    tp.wait()
    for c in kvs:
        c.wait_recv()

    going = []
    for k, q in enumerate(doms):
        for c in range(CAP):
            at = jnp.clip(smem[0, q * 8 + c], 0, NBLK - 1)
            outgoing[k, c] = kv_l[lax.div(at, 4), lax.rem(at, 4)]
        going.append(start(outgoing.at[k], incoming.at[pl.ds(d * CAP, CAP)], dev(q, x, y)))
    qgs = project_qo(x)
    cfwd = xmiddle(cot_all, cl, cr)
    qgs += project_qo(xm)
    qgs += project_qo(xp)
    for c in cfwd:
        c.wait_recv()
    qgs += project_qo(x2)
    incoming[pl.ds(d * CAP, CAP)] = jnp.zeros((CAP, BLK, 128), BF)
    returned[pl.ds(d * CAP, CAP)] = jnp.zeros((CAP, BLK, 128), BF)
    for b in range(X):
        feat_t[:, b * BLK : (b + 1) * BLK] = jnp.transpose(feat_all[b])
        cot_t[:, b * BLK : (b + 1) * BLK] = jnp.transpose(cot_all[b])
    low1 = lanes((BLK, 128)) < HD
    low2 = lanes((GROUP, 128)) < HD
    for s in range(NBLK):
        kvt[s // 4, :, pl.ds((s % 4) * 128, 128)] = jnp.transpose(kv_l[s // 4, s % 4])
    for c in qgs:
        c.wait_recv()
    for s in range(NBLK):
        p = qg_l[s // 4, s % 4]
        p = jnp.where(low1, p * 0.125, p)
        qd[s] = p
        qdt[s] = jnp.transpose(p)
    dkv[...] = jnp.zeros_like(dkv)

    nchunk = NBLK * BLK // CHUNK

    def fold(v, op):
        out = v[:, 0:128]
        for j in range(1, CHUNK // 128):
            out = op(out, v[:, j * 128 : (j + 1) * 128])
        return out

    def forward(g, _):
        p = qd[pl.ds(2 * g, 2)].reshape(GROUP, 128)
        qs = jnp.where(low2, p, jnp.zeros_like(p))
        top = None
        for c in range(nchunk):
            s = mm(qs, kvt[c])
            scores[c] = s
            t = fold(s, jnp.maximum)
            top = t if top is None else jnp.maximum(top, t)
        m = jnp.max(top, 1, keepdims=True)
        total, out = None, None
        for c in range(nchunk):
            e = jnp.exp(scores[c] - m)
            t = fold(e, jnp.add)
            total = t if total is None else total + t
            eb = e.astype(BF)
            probs[g, c] = eb
            o = mm(eb, kv_l[c].reshape(CHUNK, 128))
            out = o if out is None else out + o
        l = jnp.sum(total, 1, keepdims=True)
        outl[pl.ds(2 * g, 2)] = out.reshape(2, BLK, 128)
        mrow[pl.ds(2 * g, 2)] = jnp.broadcast_to(m, (GROUP, 128)).reshape(2, BLK, 128)
        lrow[pl.ds(2 * g, 2)] = jnp.broadcast_to(l, (GROUP, 128)).reshape(2, BLK, 128)
        return 0

    lax.fori_loop(0, NBLK // 2, forward, 0)
    for c in going:
        c.wait_recv()

    batch = 8

    def extras(g, _):
        ids = [batch * g + i for i in range(batch)]
        blks = [qd[i] for i in ids]
        ekvs = [incoming[jnp.clip(tab[0, i], 0, PARTS * CAP - 1)] for i in ids]
        zero = jnp.zeros((BLK, 128), BF)
        ses = [mm_nt(jnp.where(low1, b, zero), e) for b, e in zip(blks, ekvs)]
        gos = [jnp.where(low1, zero, b) for b in blks]
        dps = [mm_nt(o, e) for o, e in zip(gos, ekvs)]
        ses = [jnp.where(tab[1, i] > 0, e, NEG_FILL) for i, e in zip(ids, ses)]
        mls = [mrow[i] for i in ids]
        bigs = [jnp.maximum(m, jnp.max(e, 1, keepdims=True)) for m, e in zip(mls, ses)]
        cs = [jnp.exp(m - b) for m, b in zip(mls, bigs)]
        ees = [jnp.exp(e - b) for e, b in zip(ses, bigs)]
        ls = [c * lrow[i] + jnp.sum(e, 1, keepdims=True) for c, i, e in zip(cs, ids, ees)]
        rs_ = [1.0 / v for v in ls]
        pes = [e * r for e, r in zip(ees, rs_)]
        pbs = [p.astype(BF) for p in pes]
        rls = [c * r for c, r in zip(cs, rs_)]
        outs = [
            (outl[i] * r + mm(p, e)).astype(BF).astype(F32)
            for i, r, p, e in zip(ids, rls, pbs, ekvs)
        ]
        deltas = [
            jnp.sum(o.astype(F32) * a, 1, keepdims=True) for o, a in zip(gos, outs)
        ]
        dss = [(p * (dp - dl)).astype(BF) for p, dp, dl in zip(pes, dps, deltas)]
        for n, i in enumerate(ids):
            bt = qdt[i]
            egrad[i, 0:HD] = mm(bt[0:HD], dss[n]).astype(BF)
            egrad[i, HD:128] = mm(bt[HD:128], pbs[n]).astype(BF)
        for n, i in enumerate(ids):
            dses[i] = dss[n]
            rl_s[i] = rls[n]
            rd_s[i] = rls[n] * deltas[n]
        for n in range(0, batch, 2):
            attp[(batch // 4) * g + n // 4, (n // 2) % 2] = jnp.where(
                low1, pltpu.roll(outs[n], HD, 1), outs[n + 1]
            ).astype(BF)
        return 0

    lax.fori_loop(0, NBLK // batch, extras, 0)
    home = []
    for k, q in enumerate(doms):
        for c in range(CAP):
            slot = q * CAP + c
            got = egrad[jnp.clip(tab[2, slot], 0, NBLK - 1)]
            sending[k, c] = jnp.where(tab[3, slot] > 0, got, jnp.zeros_like(got))
        home.append(start(sending.at[k], returned.at[pl.ds(d * CAP, CAP)], dev(q, x, y)))
    ats = [start(attp.at[yy], at_l.at[y], to) for yy, to in ysteps]
    at_l[y] = attp[y]

    def backward(g, _):
        p = qd[pl.ds(2 * g, 2)].reshape(GROUP, 128)
        rl = rl_s[pl.ds(2 * g, 2)].reshape(GROUP, 128)
        rd = rd_s[pl.ds(2 * g, 2)].reshape(GROUP, 128)[:, :1]
        zz = jnp.where(low2, p, (p.astype(F32) * rl).astype(BF))
        zt = jnp.transpose(zz)
        go = jnp.where(low2, jnp.zeros_like(zz), zz)
        dq = jnp.concatenate(
            [
                mm(dses[2 * g + i], incoming[jnp.clip(tab[0, 2 * g + i], 0, PARTS * CAP - 1)])
                for i in range(2)
            ],
            0,
        )
        for c in range(nchunk):
            dp = mm(go, kvt[c])
            eb = probs[g, c]
            dsc = eb * (dp - rd).astype(BF)
            dq = dq + mm(dsc, kv_l[c].reshape(CHUNK, 128))
            dk = mm(zt[0:HD], dsc)
            dv = mm(zt[HD:128], eb)
            for i in range(CHUNK // 128):
                dkv[4 * c + i, 0:HD] += dk[:, i * 128 : (i + 1) * 128]
                dkv[4 * c + i, HD:128] += dv[:, i * 128 : (i + 1) * 128]
        dq = dq * 0.125
        gqp[lax.div(g, 2), lax.rem(g, 2)] = jnp.where(
            low1, dq[0:BLK], pltpu.roll(dq[BLK:GROUP], HD, 1)
        ).astype(BF)
        return 0

    lax.fori_loop(0, NBLK // 2, backward, 0)
    gqs = [start(gqp.at[yy], gq_l.at[y], to) for yy, to in ysteps]
    gq_l[y] = gqp[y]

    def two(ref, h):
        return jnp.concatenate([ref[h].reshape(rows, 128), ref[h + 1].reshape(rows, 128)], 1)

    rows = X * BLK
    for c in ats:
        c.wait_recv()
    for h in range(Y):
        for j in range(2):
            p = at_l[h, j].astype(F32)
            zero = jnp.zeros_like(p)
            g2[1, h, 2 * j] = jnp.where(low1, zero, pltpu.roll(p, HD, 1)).astype(BF)
            g2[1, h, 2 * j + 1] = jnp.where(low1, zero, p).astype(BF)
    for n in range(4):
        cols = pl.ds(n * 256, 256)
        o = None
        for h in range(0, Y, 2):
            t = mm(two(g2.at[1], h), wqo[h : h + 2, :, cols].reshape(256, 256))
            o = t if o is None else o + t
        part[:, 0, :, cols] = o.astype(BF).reshape(X, BLK, 256)
    xsteps = [(x2, xopp), (xp, right), (xm, left)]
    los = [start(part.at[xx, 0], rs.at[k, 0], to) for k, (xx, to) in enumerate(xsteps)]

    def weights(i, left_of):
        out = []
        for h in range(Y):
            if h % 2 == 0:
                both = left_of(h)
                for j in range(2):
                    wgf[i, h + j] = both[:, j * 128 : (j + 1) * 128].reshape(Z, 2, 64, 128)
            sibs[i, h] = wgf[i, h, :, 1 - core].astype(BF)
            out.append(start(sibs.at[i, h], sibr.at[i, h], sibling))
        return out

    def along_y(i, sib):
        for c in sib:
            c.wait_recv()
        out = []
        for k, (yy, to) in enumerate(ysteps):
            ysend[i, k] = (wgf[i, yy, :, core] + sibr[i, yy].astype(F32)).astype(BF)
            out.append(start(ysend.at[i, k], yrecv.at[i, k], to))
        return out

    zsteps = [lax.rem(z + k, Z) for k in (4, 3, 5, 2, 6, 1, 7)]

    def along_z(i, ys):
        total = wgf[i, y, :, core] + sibr[i, y].astype(F32)
        for k in range(3):
            ys[k].wait_recv()
            total = total + yrecv[i, k].astype(F32)
        own[i] = total
        zsend[i] = total.astype(BF)
        return [
            start(zsend.at[i, zz], zrecv.at[i, k], dev(zz * 2 + core, x, y))
            for k, zz in enumerate(zsteps)
        ]

    def finish(i, zsum):
        res = own[i, z]
        for k in range(7):
            zsum[k].wait_recv()
            res = res + zrecv[i, k].astype(F32)
        wg[:, i * 128 : (i + 1) * 128] = res

    for c in gqs:
        c.wait_recv()
    for h in range(Y):
        for j in range(2):
            p = gq_l[h, j].astype(F32)
            zero = jnp.zeros_like(p)
            g2[0, h, 2 * j] = jnp.where(low1, p, zero).astype(BF)
            g2[0, h, 2 * j + 1] = jnp.where(low1, pltpu.roll(p, HD, 1), zero).astype(BF)
    sib1 = weights(1, lambda h: mm(feat_t[...], two(g2.at[0], h)) + mm(cot_t[...], two(g2.at[1], h)))
    y1 = along_y(1, sib1)
    for n in range(4):
        cols = pl.ds(n * 256, 256)
        o = None
        for h in range(0, Y, 2):
            t = mm(two(g2.at[0], h), wqo[h : h + 2, :, cols].reshape(256, 256))
            o = t if o is None else o + t
        gfq[:, cols] = o
    for c in home:
        c.wait_recv()
    running = None
    for k in range(CAP * (PARTS - 1)):
        got = returned[jnp.clip(smem[1, k], 0, PARTS * CAP - 1)].astype(F32)
        running = got if k == 0 else got + running * smem[2, k].astype(F32)
        runs[k] = running
    for s in range(NBLK):
        more = jnp.where(
            smem[4, s] > 0,
            runs[jnp.clip(smem[3, s], 0, CAP * (PARTS - 1) - 1)],
            jnp.zeros((128, BLK), F32),
        )
        gkv[s // 4, s % 4] = jnp.transpose(dkv[s] + more).astype(BF)
    gks = [start(gkv.at[yy], g_kv.at[y], to) for yy, to in ysteps]
    g_kv[y] = gkv[y]
    z1 = along_z(1, y1)
    for c in gks:
        c.wait_recv()
    sib0 = weights(0, lambda h: mm(feat_t[...], two(g_kv, h)))
    for n in range(4):
        cols = pl.ds(n * 256, 256)
        o = gfq[:, cols]
        for h in range(0, Y, 2):
            o = o + mm(two(g_kv, h), wkv[h : h + 2, :, cols].reshape(256, 256))
        part[:, 1, :, cols] = o.astype(BF).reshape(X, BLK, 256)
    gfs = [start(part.at[xx, 1], rs.at[k, 1], to) for k, (xx, to) in enumerate(xsteps)]
    y0 = along_y(0, sib0)
    for i, (copies, base, out) in enumerate(((los, feat, lo), (gfs, cot, gf))):
        if i == 1:
            finish(1, z1)
            z0 = along_z(0, y0)
        total = part[x, i].astype(F32)
        for k in range(3):
            copies[k].wait_recv()
            total = total + rs[k, i].astype(F32)
        out[...] = (base[...].astype(F32) + total).astype(BF)
    finish(0, z0)
    for c in net.all:
        c.wait_send()


def hand_over_kernel(lo, gf, wg, lo_o, gf_o, q_o, k_o, v_o, o_o):
    lo_o[...] = lo[...]
    gf_o[...] = gf[...]
    for i, o in enumerate((k_o, v_o, q_o, o_o)):
        o[...] = wg[:, i * HD : (i + 1) * HD]


VM = pl.BlockSpec(memory_space=pltpu.VMEM)
SM = pl.BlockSpec(memory_space=pltpu.SMEM)
COPIES = 134


def sds(shape, dtype):
    return jax.ShapeDtypeStruct(shape, dtype)


def params(cid):
    return pltpu.CompilerParams(
        collective_id=cid, has_side_effects=True, vmem_limit_bytes=60 * 1024 * 1024
    )


def local(
    features, w_query, w_key, w_value, w_output, cotangent, cross_source, cross_target, cross_count
):
    v = pltpu.VMEM
    full = (X, BLK, WIDTH)
    four = (Y, X, BLK, 128)
    pair = (Y, 2, BLK, 128)
    blocks = (NBLK, BLK, 128)
    layer_out, grad_features, wg = pl.pallas_call(
        layer_kernel,
        out_shape=(sds((BLK, WIDTH), BF), sds((BLK, WIDTH), BF), sds((64, 256), F32)),
        in_specs=[SM] * 3 + [VM] * 6,
        out_specs=(VM,) * 3,
        scratch_shapes=[
            v((PARTS, 8, 128), F32), v((8, 128), jnp.int32), pltpu.SMEM((8, 128), jnp.int32),
            v(full, BF), v(full, BF), v((Y, 128, WIDTH), BF), v((Y, 128, WIDTH), BF),
            v((WIDTH, X * BLK), BF), v((WIDTH, X * BLK), BF),
            v((PARTS, 8, 128), F32), v((8, 128), jnp.int32), pltpu.SMEM((8, 128), jnp.int32),
            v(four, BF), v(four, BF), v(four, BF), v(four, BF),
            v((15, CAP, BLK, 128), BF), v((PARTS * CAP, BLK, 128), BF),
            v((15, CAP, BLK, 128), BF), v((PARTS * CAP, BLK, 128), BF),
            v((NBLK // 2, 4, GROUP, CHUNK), BF), v((4, GROUP, CHUNK), F32), v((4, 128, CHUNK), BF),
            v(blocks, BF), v(blocks, F32), v(blocks, F32), v(blocks, F32), v(blocks, F32),
            v(blocks, F32),
            v(blocks, F32), v(blocks, BF), v(blocks, BF), v(blocks, BF), v((30, 128, BLK), F32), v(four, BF),
            v(pair, BF), v(pair, BF), v(four, BF), v(pair, BF), v(pair, BF),
            v((X, 2, BLK, WIDTH), BF), v((X * BLK, WIDTH), F32), v((3, 2, BLK, WIDTH), BF), v((2,) + four, BF),
            v((2, Y, Z, 2, 64, 128), F32), v((2, Y, Z, 64, 128), BF), v((2, Y, Z, 64, 128), BF),
            v((2, 3, Z, 64, 128), BF), v((2, 3, Z, 64, 128), BF),
            v((2, Z, 64, 128), F32), v((2, Z, 64, 128), BF), v((2, 7, 64, 128), BF),
            pltpu.SemaphoreType.DMA((COPIES,)), pltpu.SemaphoreType.DMA((COPIES,)),
            pltpu.SemaphoreType.DMA, pltpu.SemaphoreType.DMA,
        ],
        compiler_params=params(1),
        name="layer",
    )(
        cross_source, cross_target, cross_count, features, cotangent,
        w_key.T, w_value.T, w_query.T, w_output,
    )
    square = sds((HD, HD), F32)
    return pl.pallas_call(
        hand_over_kernel,
        out_shape=(sds((BLK, WIDTH), BF), sds((BLK, WIDTH), BF), square, square, square, square),
        in_specs=[VM] * 3,
        out_specs=(VM,) * 6,
        name="hand_over",
    )(layer_out, grad_features, wg)


def solution(mesh):
    return jax.shard_map(
        local,
        mesh=mesh,
        in_specs=(
            P(("dom", "head"), None),
            P(None, "head"),
            P(None, "head"),
            P(None, "head"),
            P("head", None),
            P(("dom", "head"), None),
            P("dom", None),
            P("dom", None),
            P("dom"),
        ),
        out_specs=(
            P(("dom", "head"), None),
            P(("dom", "head"), None),
            P("dom", "head"),
            P("dom", "head"),
            P("dom", "head"),
            P("dom", "head"),
        ),
        check_vma=False,
    )
```

```python
import jax
import jax.numpy as jnp
from jax import lax
from jax.experimental import pallas as pl
from jax.experimental.pallas import tpu as pltpu
from jax.sharding import PartitionSpec as P

HD = 64
BLK = 128
CAP = 2
X = 4
Y = 4
Z = 8
PARTS = 16
NBLK = 16
WIDTH = 1024
GROUP = 256
CHUNK = 512
NEG_FILL = -1e30
MESH = pl.DeviceIdType.MESH
BF = jnp.bfloat16
F32 = jnp.float32


def mm(a, b):
    return jnp.dot(a, b, preferred_element_type=F32)


def mm_nt(a, b):
    return lax.dot_general(a, b, (((1,), (1,)), ((), ())), preferred_element_type=F32)


def place():
    d = lax.axis_index("dom")
    h = lax.axis_index("head")
    return d, lax.div(h, Y), lax.rem(h, Y)


def greet(peers, meanwhile):
    barrier = pltpu.get_barrier_semaphore()
    for peer in peers:
        pl.semaphore_signal(barrier, inc=1, device_id=peer, device_id_type=MESH)
    meanwhile()
    pl.semaphore_wait(barrier, len(peers))


def lanes(shape):
    return lax.broadcasted_iota(jnp.int32, shape, len(shape) - 1)


def turned(t):
    return lax.rem(t, 4) * 4 + lax.div(t, 4)


class Sems:
    def __init__(self, send, recv):
        self.send, self.recv, self.n, self.all = send, recv, 0, []

    def start(self, src, dst, to):
        c = pltpu.make_async_remote_copy(
            src_ref=src, dst_ref=dst, send_sem=self.send.at[self.n], recv_sem=self.recv.at[self.n],
            device_id=to, device_id_type=MESH,
        )
        c.start()
        self.n += 1
        self.all.append(c)
        return c

    def group(self, landing):
        g = Group(self, self.n, landing)
        self.n += 1
        self.all.append(g)
        return g


class Group:
    def __init__(self, net, n, landing):
        self.net, self.n, self.landing, self.to = net, n, landing, None

    def copy(self, src, dst, to):
        return pltpu.make_async_remote_copy(
            src_ref=src, dst_ref=dst, send_sem=self.net.send.at[self.n],
            recv_sem=self.net.recv.at[self.n], device_id=to, device_id_type=MESH,
        )

    def start(self, src, dst, to):
        self.to = to
        self.copy(src, dst, to).start()

    def wait_recv(self):
        self.copy(self.landing, self.landing, self.to).wait_recv()

    def wait_send(self):
        self.copy(self.landing, self.landing, self.to).wait_send()


def slot_tables(source, target, count, req, table):
    sub = lax.broadcasted_iota(jnp.int32, (128, 128), 0)
    row = lax.broadcasted_iota(jnp.int32, (8, 128), 0)
    lane = lax.broadcasted_iota(jnp.int32, (8, 128), 1)
    ask = jnp.zeros((128, 128), jnp.int32)
    tab = jnp.zeros((8, 128), jnp.int32)
    owners = []
    for j in range(16):
        src, tgt = source[0, j], target[0, j]
        owner, block = lax.div(src, NBLK), lax.rem(src, NBLK)
        position = jnp.int32(0)
        for o in owners:
            position = position + jnp.where(o == owner, 1, 0)
        owners.append(owner)
        position = jnp.minimum(position, CAP - 1)
        ask = ask + jnp.where(sub == owner * 8 + position, turned(block), 0)
        slot, pos = owner * CAP + position, turned(tgt)
        live = jnp.where(count[0] > j, 1, 0)
        here, there = lane == pos, lane == slot
        tab = tab + jnp.where((row == 0) & here, slot * live, 0)
        tab = tab + jnp.where((row == 1) & here, live, 0)
        tab = tab + jnp.where((row == 2) & there, pos * live, 0)
        tab = tab + jnp.where((row == 3) & there, live, 0)
    req[...] = ask.astype(F32).reshape(PARTS, 8, 128)
    table[...] = tab


def order_tables(asked, table):
    sub = lax.broadcasted_iota(jnp.int32, (128, 128), 0)
    lane = lax.broadcasted_iota(jnp.int32, (128, 128), 1)
    a = jnp.where((sub & 7) < CAP, asked[...].reshape(128, 128), 99.0)
    b = jnp.transpose(a)
    one, zero = jnp.ones((128, 128), F32), jnp.zeros((128, 128), F32)
    lanef = lane.astype(F32)
    less = jnp.where((b < a) | ((b == a) & (lane < sub)), one, zero)
    rank = jnp.sum(less, 1, keepdims=True)
    hot = jnp.where(rank == lanef, one, zero)
    where_from = ((sub >> 3) * CAP + (sub & 7)).astype(F32)
    order = jnp.sum(hot * where_from, 0, keepdims=True)
    value = jnp.sum(hot * a, 0, keepdims=True)
    end = jnp.sum(jnp.where(a <= lanef, one, zero), 0, keepdims=True) - 1.0
    has = jnp.sum(jnp.where(a == lanef, one, zero), 0, keepdims=True)
    wide = jnp.broadcast_to(value, (8, 128))
    same = jnp.where(wide == pltpu.roll(wide, 1, 1), one[:8], zero[:8])
    row = sub[:8]
    out = jnp.where(row == 0, jnp.minimum(b[:8], 15.0), zero[:8])
    for i, v in ((1, order), (2, same), (3, jnp.maximum(end, 0.0)), (4, has)):
        out = jnp.where(row == i, jnp.broadcast_to(v, (8, 128)), out)
    table[...] = out.astype(jnp.int32)


def layer_kernel(
    source, target, count, feat, cot, wk, wv, wq, wo,
    lo, gf, wg,
    req, tab_v, tab, feat_all, cot_all, wkv, wqo, feat_t, cot_t, asked, table, smem, kst, qst, kv_l, qg_l,
    outgoing, incoming, sending, returned, probs, scores, kvt, qd, outl, mrow, lrow, rl_s, rd_s,
    dkv, egrad, dses, qdt, runs, gkv, attp, gqp, g_kv, at_l, gq_l, part, gfq, rs, g2, wgf, sibs, sibr, ysend, yrecv,
    own, zsend, zrecv, send_sems, recv_sems, local_sem, tab_sem,
):
    d, x, y = place()
    core, z = lax.rem(d, 2), lax.div(d, 2)

    def dev(dd, xx, yy):
        return (dd, xx * Y + yy)

    xp, xm, x2 = [lax.rem(x + k, X) for k in (1, 3, 2)]
    yp, ym, y2 = [lax.rem(y + k, Y) for k in (1, 3, 2)]
    right, left, xopp = dev(d, xp, y), dev(d, xm, y), dev(d, x2, y)
    up, down, yopp = dev(d, x, yp), dev(d, x, ym), dev(d, x, y2)
    doms = [lax.rem(d + k, PARTS) for k in range(1, PARTS)]
    sibling = dev(d + 1 - 2 * core, x, y)

    def prepare():
        slot_tables(source, target, count, req, tab_v)
        for w, o in ((wkv, (wk, wv)), (wqo, (wq, wo))):
            w[y, 0:HD] = o[0][...]
            w[y, HD:128] = o[1][...]
        asked[d] = jnp.full((8, 128), 99.0, F32)
        feat_all[x] = feat[...]
        cot_all[x] = cot[...]

    greet([right, left, xopp, up, down, yopp] + [dev(q, x, y) for q in doms], prepare)
    tp = pltpu.make_async_copy(tab_v, tab, tab_sem)
    tp.start()
    net = Sems(send_sems, recv_sems)
    start = net.start
    ysteps = [(y2, yopp), (yp, up), (ym, down)]

    def along_x(own_rows, full):
        top, bottom = pl.ds(0, HD), pl.ds(HD, HD)
        out = []
        for first, second, to in ((top, bottom, right), (bottom, top, left)):
            out.append([start(own_rows.at[h], full.at[x, h], to) for h in (first, second)])
        return out

    fx = along_x(feat, feat_all)
    mine = pl.multiple_of(core * HD, HD)
    whole = pl.ds(mine, HD)
    upper, lower = pl.ds(mine, 32), pl.ds(mine + 32, 32)
    wown = []
    for w in (wkv, wqo):
        piece = w.at[y, whole]
        wown.append((start(piece, piece, up), start(piece, piece, down)))
    tables = net.group(asked.at[pl.ds(0, PARTS - 1)])
    for q in doms:
        tables.start(req.at[q], asked.at[d], dev(q, x, y))

    def wmiddle(i):
        w = (wkv, wqo)[i]
        a, b = wown[i]
        a.wait_recv()
        p = w.at[ym, upper]
        f1 = start(p, p, up)
        p = w.at[ym, whole]
        s1 = start(p, p, sibling)
        b.wait_recv()
        p = w.at[yp, lower]
        f2 = start(p, p, down)
        p = w.at[yp, whole]
        s2 = start(p, p, sibling)
        return f1, f2, s1, s2

    def wlast(i, mid):
        w = (wkv, wqo)[i]
        mid[0].wait_recv()
        mid[1].wait_recv()
        p = w.at[y2, whole]
        s3 = start(p, p, sibling)
        mid[2].wait_recv()
        mid[3].wait_recv()
        s3.wait_recv()

    def xmiddle(full, halves):
        (a0, a1), (b0, b1) = halves
        a0.wait_recv()
        p = full.at[xm, pl.ds(0, HD)]
        f1 = start(p, p, right)
        b0.wait_recv()
        p = full.at[xp, pl.ds(HD, HD)]
        f2 = start(p, p, left)
        a1.wait_recv()
        b1.wait_recv()
        return f1, f2

    mkv = wmiddle(0)
    ffwd = xmiddle(feat_all, fx)
    mqo = wmiddle(1)
    wlast(0, mkv)
    low4 = (lanes((BLK, 512)) & 127) < HD

    def project_kv(b):
        r = mm_nt(feat_all[b], wkv[...].reshape(Y * 128, WIDTH)).astype(BF)
        for h in range(Y):
            kst[h, b] = r[:, h * 128 : (h + 1) * 128]
        kv_l[y, b] = kst[y, b]
        for yy, to in ysteps:
            kvs.start(kst.at[yy, b], kv_l.at[y, b], to)

    def project_qo(b):
        w = wqo[...].reshape(Y * 128, WIDTH)
        r = jnp.where(low4, mm_nt(feat_all[b], w), mm_nt(cot_all[b], w)).astype(BF)
        for h in range(Y):
            qst[h, b] = r[:, h * 128 : (h + 1) * 128]
        qg_l[y, b] = qst[y, b]
        for yy, to in ysteps:
            qgs.start(qst.at[yy, b], qg_l.at[y, b], to)

    kvs, qgs = net.group(kv_l.at[pl.ds(0, 3)]), net.group(qg_l.at[pl.ds(0, 3)])
    project_kv(x)
    project_kv(xm)
    project_kv(xp)
    tables.wait_recv()
    order_tables(asked, table)
    cp = pltpu.make_async_copy(table, smem, local_sem)
    cp.start()
    for c in ffwd:
        c.wait_recv()
    cx = along_x(cot, cot_all)
    project_kv(x2)
    cp.wait()
    tp.wait()
    kvs.wait_recv()

    going = net.group(incoming.at[pl.ds(0, CAP * (PARTS - 1))])
    for k, q in enumerate(doms):
        for c in range(CAP):
            at = jnp.clip(smem[0, q * 8 + c], 0, NBLK - 1)
            outgoing[k, c] = kv_l[lax.div(at, 4), lax.rem(at, 4)]
        going.start(outgoing.at[k], incoming.at[pl.ds(d * CAP, CAP)], dev(q, x, y))
    wlast(1, mqo)
    project_qo(x)
    cfwd = xmiddle(cot_all, cx)
    project_qo(xm)
    project_qo(xp)
    for c in cfwd:
        c.wait_recv()
    project_qo(x2)
    incoming[pl.ds(d * CAP, CAP)] = jnp.zeros((CAP, BLK, 128), BF)
    returned[pl.ds(d * CAP, CAP)] = jnp.zeros((CAP, BLK, 128), BF)
    for b in range(X):
        feat_t[:, b * BLK : (b + 1) * BLK] = jnp.transpose(feat_all[b])
        cot_t[:, b * BLK : (b + 1) * BLK] = jnp.transpose(cot_all[b])
    low1 = lanes((BLK, 128)) < HD
    low2 = lanes((GROUP, 128)) < HD
    for s in range(NBLK):
        kvt[s // 4, :, pl.ds((s % 4) * 128, 128)] = jnp.transpose(kv_l[s // 4, s % 4])
    qgs.wait_recv()
    for s in range(NBLK):
        p = qg_l[s // 4, s % 4]
        p = jnp.where(low1, p * 0.125, p)
        qd[s] = p
        qdt[s] = jnp.transpose(p)
    dkv[...] = jnp.zeros_like(dkv)

    nchunk = NBLK * BLK // CHUNK

    def fold(v, op):
        out = v[:, 0:128]
        for j in range(1, CHUNK // 128):
            out = op(out, v[:, j * 128 : (j + 1) * 128])
        return out

    def forward(g, _):
        p = qd[pl.ds(2 * g, 2)].reshape(GROUP, 128)
        qs = jnp.where(low2, p, jnp.zeros_like(p))
        top = None
        for c in range(nchunk):
            s = mm(qs, kvt[c])
            scores[c] = s
            t = fold(s, jnp.maximum)
            top = t if top is None else jnp.maximum(top, t)
        m = jnp.max(top, 1, keepdims=True)
        total, out = None, None
        for c in range(nchunk):
            e = jnp.exp(scores[c] - m)
            t = fold(e, jnp.add)
            total = t if total is None else total + t
            eb = e.astype(BF)
            probs[g, c] = eb
            o = mm(eb, kv_l[c].reshape(CHUNK, 128))
            out = o if out is None else out + o
        l = jnp.sum(total, 1, keepdims=True)
        outl[pl.ds(2 * g, 2)] = out.reshape(2, BLK, 128)
        mrow[pl.ds(2 * g, 2)] = jnp.broadcast_to(m, (GROUP, 128)).reshape(2, BLK, 128)
        lrow[pl.ds(2 * g, 2)] = jnp.broadcast_to(l, (GROUP, 128)).reshape(2, BLK, 128)
        return 0

    lax.fori_loop(0, NBLK // 2, forward, 0)
    going.wait_recv()

    batch = 8

    def extras(g, _):
        ids = [batch * g + i for i in range(batch)]
        blks = [qd[i] for i in ids]
        ekvs = [incoming[jnp.clip(tab[0, i], 0, PARTS * CAP - 1)] for i in ids]
        zero = jnp.zeros((BLK, 128), BF)
        ses = [mm_nt(jnp.where(low1, b, zero), e) for b, e in zip(blks, ekvs)]
        gos = [jnp.where(low1, zero, b) for b in blks]
        dps = [mm_nt(o, e) for o, e in zip(gos, ekvs)]
        ses = [jnp.where(tab[1, i] > 0, e, NEG_FILL) for i, e in zip(ids, ses)]
        mls = [mrow[i] for i in ids]
        bigs = [jnp.maximum(m, jnp.max(e, 1, keepdims=True)) for m, e in zip(mls, ses)]
        cs = [jnp.exp(m - b) for m, b in zip(mls, bigs)]
        ees = [jnp.exp(e - b) for e, b in zip(ses, bigs)]
        ls = [c * lrow[i] + jnp.sum(e, 1, keepdims=True) for c, i, e in zip(cs, ids, ees)]
        rs_ = [1.0 / v for v in ls]
        pes = [e * r for e, r in zip(ees, rs_)]
        pbs = [p.astype(BF) for p in pes]
        rls = [c * r for c, r in zip(cs, rs_)]
        outs = [
            (outl[i] * r + mm(p, e)).astype(BF).astype(F32)
            for i, r, p, e in zip(ids, rls, pbs, ekvs)
        ]
        deltas = [
            jnp.sum(o.astype(F32) * a, 1, keepdims=True) for o, a in zip(gos, outs)
        ]
        dss = [(p * (dp - dl)).astype(BF) for p, dp, dl in zip(pes, dps, deltas)]
        for n, i in enumerate(ids):
            bt = qdt[i]
            egrad[i, 0:HD] = mm(bt[0:HD], dss[n]).astype(BF)
            egrad[i, HD:128] = mm(bt[HD:128], pbs[n]).astype(BF)
        for n, i in enumerate(ids):
            dses[i] = dss[n]
            rl_s[i] = rls[n]
            rd_s[i] = rls[n] * deltas[n]
        for n in range(0, batch, 2):
            attp[(batch // 4) * g + n // 4, (n // 2) % 2] = jnp.where(
                low1, pltpu.roll(outs[n], HD, 1), outs[n + 1]
            ).astype(BF)
        return 0

    lax.fori_loop(0, NBLK // batch, extras, 0)
    home = net.group(returned.at[pl.ds(0, CAP * (PARTS - 1))])
    for k, q in enumerate(doms):
        for c in range(CAP):
            slot = q * CAP + c
            got = egrad[jnp.clip(tab[2, slot], 0, NBLK - 1)]
            sending[k, c] = jnp.where(tab[3, slot] > 0, got, jnp.zeros_like(got))
        home.start(sending.at[k], returned.at[pl.ds(d * CAP, CAP)], dev(q, x, y))
    ats = net.group(at_l.at[pl.ds(0, 3)])
    for yy, to in ysteps:
        ats.start(attp.at[yy], at_l.at[y], to)
    at_l[y] = attp[y]

    def backward(g, _):
        p = qd[pl.ds(2 * g, 2)].reshape(GROUP, 128)
        rl = rl_s[pl.ds(2 * g, 2)].reshape(GROUP, 128)
        rd = rd_s[pl.ds(2 * g, 2)].reshape(GROUP, 128)[:, :1]
        zz = jnp.where(low2, p, (p.astype(F32) * rl).astype(BF))
        zt = jnp.transpose(zz)
        go = jnp.where(low2, jnp.zeros_like(zz), zz)
        dq = jnp.concatenate(
            [
                mm(dses[2 * g + i], incoming[jnp.clip(tab[0, 2 * g + i], 0, PARTS * CAP - 1)])
                for i in range(2)
            ],
            0,
        )
        for c in range(nchunk):
            dp = mm(go, kvt[c])
            eb = probs[g, c]
            dsc = eb * (dp - rd).astype(BF)
            dq = dq + mm(dsc, kv_l[c].reshape(CHUNK, 128))
            dk = mm(zt[0:HD], dsc)
            dv = mm(zt[HD:128], eb)
            for i in range(CHUNK // 128):
                dkv[4 * c + i, 0:HD] += dk[:, i * 128 : (i + 1) * 128]
                dkv[4 * c + i, HD:128] += dv[:, i * 128 : (i + 1) * 128]
        dq = dq * 0.125
        gqp[lax.div(g, 2), lax.rem(g, 2)] = jnp.where(
            low1, dq[0:BLK], pltpu.roll(dq[BLK:GROUP], HD, 1)
        ).astype(BF)
        return 0

    lax.fori_loop(0, NBLK // 2, backward, 0)
    gqs = net.group(gq_l.at[pl.ds(0, 3)])
    for yy, to in ysteps:
        gqs.start(gqp.at[yy], gq_l.at[y], to)
    gq_l[y] = gqp[y]

    def two(ref, h, h2=None):
        h2 = h + 1 if h2 is None else h2
        return jnp.concatenate([ref[h].reshape(rows, 128), ref[h2].reshape(rows, 128)], 1)

    rows = X * BLK
    ats.wait_recv()
    for h in range(Y):
        for j in range(2):
            p = at_l[h, j].astype(F32)
            zero = jnp.zeros_like(p)
            g2[1, h, 2 * j] = jnp.where(low1, zero, pltpu.roll(p, HD, 1)).astype(BF)
            g2[1, h, 2 * j + 1] = jnp.where(low1, zero, p).astype(BF)
    for n in range(4):
        cols = pl.ds(n * 256, 256)
        o = None
        for h in range(0, Y, 2):
            t = mm(two(g2.at[1], h), wqo[h : h + 2, :, cols].reshape(256, 256))
            o = t if o is None else o + t
        part[:, 0, :, cols] = o.astype(BF).reshape(X, BLK, 256)
    xsteps = [(x2, xopp), (xp, right), (xm, left)]
    los, gfs = net.group(rs.at[:, 0]), net.group(rs.at[:, 1])
    for k, (xx, to) in enumerate(xsteps):
        los.start(part.at[xx, 0], rs.at[k, 0], to)

    yorder = [yy for yy, _ in ysteps] + [y]

    def weights(i, left_of):
        out = []
        for n in (0, 2):
            pick = yorder[n : n + 2]
            both = left_of(*pick)
            c = net.group(sibr.at[i, pl.ds(0, 2)])
            for j, h in enumerate(pick):
                wgf[i, h] = both[:, j * 128 : (j + 1) * 128].reshape(Z, 2, 64, 128)
                sibs[i, h] = wgf[i, h, :, 1 - core].astype(BF)
                c.start(sibs.at[i, h], sibr.at[i, h], sibling)
            out.append(c)
        return out

    def along_y(i, sib):
        out = net.group(yrecv.at[i])
        for k, (yy, to) in enumerate(ysteps):
            if k != 1:
                sib[k // 2].wait_recv()
            ysend[i, k] = (wgf[i, yy, :, core] + sibr[i, yy].astype(F32)).astype(BF)
            out.start(ysend.at[i, k], yrecv.at[i, k], to)
        return out

    zsteps = [lax.rem(z + k, Z) for k in (4, 3, 5, 2, 6, 1, 7)]

    def along_z(i, ys):
        total = wgf[i, y, :, core] + sibr[i, y].astype(F32)
        ys.wait_recv()
        for k in range(3):
            total = total + yrecv[i, k].astype(F32)
        own[i] = total
        zsend[i] = total.astype(BF)
        out = net.group(zrecv.at[i])
        for k, zz in enumerate(zsteps):
            out.start(zsend.at[i, zz], zrecv.at[i, k], dev(zz * 2 + core, x, y))
        return out

    def finish(i, zsum):
        res = own[i, z]
        zsum.wait_recv()
        for k in range(7):
            res = res + zrecv[i, k].astype(F32)
        wg[:, i * 128 : (i + 1) * 128] = res

    gqs.wait_recv()
    for h in range(Y):
        for j in range(2):
            p = gq_l[h, j].astype(F32)
            zero = jnp.zeros_like(p)
            g2[0, h, 2 * j] = jnp.where(low1, p, zero).astype(BF)
            g2[0, h, 2 * j + 1] = jnp.where(low1, pltpu.roll(p, HD, 1), zero).astype(BF)
    sib1 = weights(1, lambda h, h2: mm(feat_t[...], two(g2.at[0], h, h2)) + mm(cot_t[...], two(g2.at[1], h, h2)))
    y1 = along_y(1, sib1)
    for n in range(4):
        cols = pl.ds(n * 256, 256)
        o = None
        for h in range(0, Y, 2):
            t = mm(two(g2.at[0], h), wqo[h : h + 2, :, cols].reshape(256, 256))
            o = t if o is None else o + t
        gfq[:, :, cols] = o.reshape(X, BLK, 256)
    home.wait_recv()
    running = None
    for k in range(CAP * (PARTS - 1)):
        got = returned[jnp.clip(smem[1, k], 0, PARTS * CAP - 1)].astype(F32)
        running = got if k == 0 else got + running * smem[2, k].astype(F32)
        runs[k] = running
    for s in range(NBLK):
        more = jnp.where(
            smem[4, s] > 0,
            runs[jnp.clip(smem[3, s], 0, CAP * (PARTS - 1) - 1)],
            jnp.zeros((128, BLK), F32),
        )
        gkv[s // 4, s % 4] = jnp.transpose(dkv[s] + more).astype(BF)
    xorder = [(x2, xopp), (xp, right), (xm, left), (x, None)]
    gks = []
    for b, _ in xorder:
        c = net.group(g_kv.at[pl.ds(0, 3), b])
        for yy, to in ysteps:
            c.start(gkv.at[yy, b], g_kv.at[y, b], to)
        gks.append(c)
    g_kv[y] = gkv[y]
    z1 = along_z(1, y1)

    def feature_part(b):
        o = gfq[b]
        for h in range(0, Y, 2):
            g = jnp.concatenate([g_kv[h, b], g_kv[h + 1, b]], 1)
            o = o + mm(g, wkv[h : h + 2].reshape(256, WIDTH))
        part[b, 1] = o.astype(BF)

    for k, (b, to) in enumerate(xorder):
        gks[k].wait_recv()
        if k < 3:
            feature_part(b)
            gfs.start(part.at[b, 1], rs.at[k, 1], to)
    sib0 = weights(0, lambda h, h2: mm(feat_t[...], two(g_kv, h, h2)))
    feature_part(x)
    y0 = along_y(0, sib0)
    for i, (copies, base, out) in enumerate(((los, feat, lo), (gfs, cot, gf))):
        if i == 1:
            finish(1, z1)
            z0 = along_z(0, y0)
        total = part[x, i].astype(F32)
        copies.wait_recv()
        for k in range(3):
            total = total + rs[k, i].astype(F32)
        out[...] = (base[...].astype(F32) + total).astype(BF)
    finish(0, z0)
    for c in net.all:
        c.wait_send()


def hand_over_kernel(lo, gf, wg, lo_o, gf_o, q_o, k_o, v_o, o_o):
    lo_o[...] = lo[...]
    gf_o[...] = gf[...]
    for i, o in enumerate((k_o, v_o, q_o, o_o)):
        o[...] = wg[:, i * HD : (i + 1) * HD]


VM = pl.BlockSpec(memory_space=pltpu.VMEM)
SM = pl.BlockSpec(memory_space=pltpu.SMEM)
COPIES = 47


def sds(shape, dtype):
    return jax.ShapeDtypeStruct(shape, dtype)


def params(cid):
    return pltpu.CompilerParams(
        collective_id=cid, has_side_effects=True, vmem_limit_bytes=60 * 1024 * 1024
    )


def local(
    features, w_query, w_key, w_value, w_output, cotangent, cross_source, cross_target, cross_count
):
    v = pltpu.VMEM
    full = (X, BLK, WIDTH)
    four = (Y, X, BLK, 128)
    pair = (Y, 2, BLK, 128)
    blocks = (NBLK, BLK, 128)
    layer_out, grad_features, wg = pl.pallas_call(
        layer_kernel,
        out_shape=(sds((BLK, WIDTH), BF), sds((BLK, WIDTH), BF), sds((64, 256), F32)),
        in_specs=[SM] * 3 + [VM] * 6,
        out_specs=(VM,) * 3,
        scratch_shapes=[
            v((PARTS, 8, 128), F32), v((8, 128), jnp.int32), pltpu.SMEM((8, 128), jnp.int32),
            v(full, BF), v(full, BF), v((Y, 128, WIDTH), BF), v((Y, 128, WIDTH), BF),
            v((WIDTH, X * BLK), BF), v((WIDTH, X * BLK), BF),
            v((PARTS, 8, 128), F32), v((8, 128), jnp.int32), pltpu.SMEM((8, 128), jnp.int32),
            v(four, BF), v(four, BF), v(four, BF), v(four, BF),
            v((15, CAP, BLK, 128), BF), v((PARTS * CAP, BLK, 128), BF),
            v((15, CAP, BLK, 128), BF), v((PARTS * CAP, BLK, 128), BF),
            v((NBLK // 2, 4, GROUP, CHUNK), BF), v((4, GROUP, CHUNK), F32), v((4, 128, CHUNK), BF),
            v(blocks, BF), v(blocks, F32), v(blocks, F32), v(blocks, F32), v(blocks, F32),
            v(blocks, F32),
            v(blocks, F32), v(blocks, BF), v(blocks, BF), v(blocks, BF), v((30, 128, BLK), F32), v(four, BF),
            v(pair, BF), v(pair, BF), v(four, BF), v(pair, BF), v(pair, BF),
            v((X, 2, BLK, WIDTH), BF), v((X, BLK, WIDTH), F32), v((3, 2, BLK, WIDTH), BF), v((2,) + four, BF),
            v((2, Y, Z, 2, 64, 128), F32), v((2, Y, Z, 64, 128), BF), v((2, Y, Z, 64, 128), BF),
            v((2, 3, Z, 64, 128), BF), v((2, 3, Z, 64, 128), BF),
            v((2, Z, 64, 128), F32), v((2, Z, 64, 128), BF), v((2, 7, 64, 128), BF),
            pltpu.SemaphoreType.DMA((COPIES,)), pltpu.SemaphoreType.DMA((COPIES,)),
            pltpu.SemaphoreType.DMA, pltpu.SemaphoreType.DMA,
        ],
        compiler_params=params(1),
        name="layer",
    )(
        cross_source, cross_target, cross_count, features, cotangent,
        w_key.T, w_value.T, w_query.T, w_output,
    )
    square = sds((HD, HD), F32)
    return pl.pallas_call(
        hand_over_kernel,
        out_shape=(sds((BLK, WIDTH), BF), sds((BLK, WIDTH), BF), square, square, square, square),
        in_specs=[VM] * 3,
        out_specs=(VM,) * 6,
        name="hand_over",
    )(layer_out, grad_features, wg)


def solution(mesh):
    return jax.shard_map(
        local,
        mesh=mesh,
        in_specs=(
            P(("dom", "head"), None),
            P(None, "head"),
            P(None, "head"),
            P(None, "head"),
            P("head", None),
            P(("dom", "head"), None),
            P("dom", None),
            P("dom", None),
            P("dom"),
        ),
        out_specs=(
            P(("dom", "head"), None),
            P(("dom", "head"), None),
            P("dom", "head"),
            P("dom", "head"),
            P("dom", "head"),
            P("dom", "head"),
        ),
        check_vma=False,
    )
```

```python
import jax
import jax.numpy as jnp
from jax import lax
from jax.experimental import pallas as pl
from jax.experimental.pallas import tpu as pltpu
from jax.sharding import PartitionSpec as P

HD = 64
BLK = 128
CAP = 2
X = 4
Y = 4
Z = 8
PARTS = 16
NBLK = 16
WIDTH = 1024
GROUP = 256
CHUNK = 512
NEG_FILL = -1e30
MESH = pl.DeviceIdType.MESH
BF = jnp.bfloat16
F32 = jnp.float32


def mm(a, b):
    return jnp.dot(a, b, preferred_element_type=F32)


def mm_nt(a, b):
    return lax.dot_general(a, b, (((1,), (1,)), ((), ())), preferred_element_type=F32)


def place():
    d = lax.axis_index("dom")
    h = lax.axis_index("head")
    return d, lax.div(h, Y), lax.rem(h, Y)


def greet(peers, meanwhile):
    barrier = pltpu.get_barrier_semaphore()
    for peer in peers:
        pl.semaphore_signal(barrier, inc=1, device_id=peer, device_id_type=MESH)
    meanwhile()
    pl.semaphore_wait(barrier, len(peers))


def lanes(shape):
    return lax.broadcasted_iota(jnp.int32, shape, len(shape) - 1)


def turned(t):
    return lax.rem(t, 4) * 4 + lax.div(t, 4)


class Sems:
    def __init__(self, send, recv):
        self.send, self.recv, self.n, self.all = send, recv, 0, []

    def start(self, src, dst, to):
        c = pltpu.make_async_remote_copy(
            src_ref=src, dst_ref=dst, send_sem=self.send.at[self.n], recv_sem=self.recv.at[self.n],
            device_id=to, device_id_type=MESH,
        )
        c.start()
        self.n += 1
        self.all.append(c)
        return c

    def group(self, landing):
        g = Group(self, self.n, landing)
        self.n += 1
        self.all.append(g)
        return g


class Group:
    def __init__(self, net, n, landing):
        self.net, self.n, self.landing, self.to = net, n, landing, None

    def copy(self, src, dst, to):
        return pltpu.make_async_remote_copy(
            src_ref=src, dst_ref=dst, send_sem=self.net.send.at[self.n],
            recv_sem=self.net.recv.at[self.n], device_id=to, device_id_type=MESH,
        )

    def start(self, src, dst, to):
        self.to = to
        self.copy(src, dst, to).start()

    def wait_recv(self):
        self.copy(self.landing, self.landing, self.to).wait_recv()

    def wait_send(self):
        self.copy(self.landing, self.landing, self.to).wait_send()


def slot_tables(source, target, count, req, table):
    sub = lax.broadcasted_iota(jnp.int32, (128, 128), 0)
    row = lax.broadcasted_iota(jnp.int32, (8, 128), 0)
    lane = lax.broadcasted_iota(jnp.int32, (8, 128), 1)
    ask = jnp.zeros((128, 128), jnp.int32)
    tab = jnp.zeros((8, 128), jnp.int32)
    owners = []
    for j in range(16):
        src, tgt = source[0, j], target[0, j]
        owner, block = lax.div(src, NBLK), lax.rem(src, NBLK)
        position = jnp.int32(0)
        for o in owners:
            position = position + jnp.where(o == owner, 1, 0)
        owners.append(owner)
        position = jnp.minimum(position, CAP - 1)
        ask = ask + jnp.where(sub == owner * 8 + position, turned(block), 0)
        slot, pos = owner * CAP + position, turned(tgt)
        live = jnp.where(count[0] > j, 1, 0)
        here, there = lane == pos, lane == slot
        tab = tab + jnp.where((row == 0) & here, slot * live, 0)
        tab = tab + jnp.where((row == 1) & here, live, 0)
        tab = tab + jnp.where((row == 2) & there, pos * live, 0)
        tab = tab + jnp.where((row == 3) & there, live, 0)
    req[...] = ask.astype(F32).reshape(PARTS, 8, 128)
    table[...] = tab


def order_tables(asked, table):
    sub = lax.broadcasted_iota(jnp.int32, (128, 128), 0)
    lane = lax.broadcasted_iota(jnp.int32, (128, 128), 1)
    a = jnp.where((sub & 7) < CAP, asked[...].reshape(128, 128), 99.0)
    b = jnp.transpose(a)
    one, zero = jnp.ones((128, 128), F32), jnp.zeros((128, 128), F32)
    lanef = lane.astype(F32)
    less = jnp.where((b < a) | ((b == a) & (lane < sub)), one, zero)
    rank = jnp.sum(less, 1, keepdims=True)
    hot = jnp.where(rank == lanef, one, zero)
    where_from = ((sub >> 3) * CAP + (sub & 7)).astype(F32)
    order = jnp.sum(hot * where_from, 0, keepdims=True)
    value = jnp.sum(hot * a, 0, keepdims=True)
    end = jnp.sum(jnp.where(a <= lanef, one, zero), 0, keepdims=True) - 1.0
    has = jnp.sum(jnp.where(a == lanef, one, zero), 0, keepdims=True)
    wide = jnp.broadcast_to(value, (8, 128))
    same = jnp.where(wide == pltpu.roll(wide, 1, 1), one[:8], zero[:8])
    row = sub[:8]
    out = jnp.where(row == 0, jnp.minimum(b[:8], 15.0), zero[:8])
    for i, v in ((1, order), (2, same), (3, jnp.maximum(end, 0.0)), (4, has)):
        out = jnp.where(row == i, jnp.broadcast_to(v, (8, 128)), out)
    table[...] = out.astype(jnp.int32)


def layer_kernel(
    source, target, count, feat, cot, wk, wv, wq, wo,
    lo, gf, wg,
    req, tab_v, tab, feat_all, cot_all, wkv, wqo, feat_t, cot_t, asked, table, smem, kst, qst, kv_l, qg_l,
    outgoing, incoming, sending, returned, probs, scores, kvt, qd, outl, mrow, lrow, rl_s, rd_s,
    dkv, egrad, dses, qdt, runs, gkv, attp, gqp, g_kv, at_l, gq_l, part, gfq, rs, g2, wgf, sibs, sibr, ysend, yrecv,
    own, zsend, zrecv, send_sems, recv_sems, local_sem, tab_sem,
):
    d, x, y = place()
    core, z = lax.rem(d, 2), lax.div(d, 2)

    def dev(dd, xx, yy):
        return (dd, xx * Y + yy)

    xp, xm, x2 = [lax.rem(x + k, X) for k in (1, 3, 2)]
    yp, ym, y2 = [lax.rem(y + k, Y) for k in (1, 3, 2)]
    right, left, xopp = dev(d, xp, y), dev(d, xm, y), dev(d, x2, y)
    up, down, yopp = dev(d, x, yp), dev(d, x, ym), dev(d, x, y2)
    doms = [lax.rem(d + k, PARTS) for k in range(1, PARTS)]
    sibling = dev(d + 1 - 2 * core, x, y)

    def prepare():
        slot_tables(source, target, count, req, tab_v)
        for w, o in ((wkv, (wk, wv)), (wqo, (wq, wo))):
            w[y, 0:HD] = o[0][...]
            w[y, HD:128] = o[1][...]
        asked[d] = jnp.full((8, 128), 99.0, F32)
        feat_all[x] = feat[...]
        cot_all[x] = cot[...]

    greet([right, left, xopp, up, down, yopp] + [dev(q, x, y) for q in doms], prepare)
    tp = pltpu.make_async_copy(tab_v, tab, tab_sem)
    tp.start()
    net = Sems(send_sems, recv_sems)
    start = net.start
    ysteps = [(y2, yopp), (yp, up), (ym, down)]

    def along_x(own_rows, full):
        top, bottom = pl.ds(0, HD), pl.ds(HD, HD)
        out = []
        for first, second, to in ((top, bottom, right), (bottom, top, left)):
            out.append([start(own_rows.at[h], full.at[x, h], to) for h in (first, second)])
        return out

    fx = along_x(feat, feat_all)
    mine = pl.multiple_of(core * HD, HD)
    whole = pl.ds(mine, HD)
    upper, lower = pl.ds(mine, 32), pl.ds(mine + 32, 32)

    def wfirst(w):
        piece = w.at[y, whole]
        return start(piece, piece, up), start(piece, piece, down)

    wown = [wfirst(wkv)]
    tables = net.group(asked.at[pl.ds(0, PARTS - 1)])
    for q in doms:
        tables.start(req.at[q], asked.at[d], dev(q, x, y))

    def wmiddle(i):
        w = (wkv, wqo)[i]
        a, b = wown[i]
        a.wait_recv()
        p = w.at[ym, upper]
        f1 = start(p, p, up)
        p = w.at[ym, whole]
        s1 = start(p, p, sibling)
        b.wait_recv()
        p = w.at[yp, lower]
        f2 = start(p, p, down)
        p = w.at[yp, whole]
        s2 = start(p, p, sibling)
        return f1, f2, s1, s2

    def wlast(i, mid):
        w = (wkv, wqo)[i]
        mid[0].wait_recv()
        mid[1].wait_recv()
        p = w.at[y2, whole]
        s3 = start(p, p, sibling)
        mid[2].wait_recv()
        mid[3].wait_recv()
        s3.wait_recv()

    def xmiddle(full, halves):
        (a0, a1), (b0, b1) = halves
        a0.wait_recv()
        p = full.at[xm, pl.ds(0, HD)]
        f1 = start(p, p, right)
        b0.wait_recv()
        p = full.at[xp, pl.ds(HD, HD)]
        f2 = start(p, p, left)
        a1.wait_recv()
        b1.wait_recv()
        return f1, f2

    mkv = wmiddle(0)
    ffwd = xmiddle(feat_all, fx)
    wlast(0, mkv)
    low4 = (lanes((BLK, 512)) & 127) < HD

    def project_kv(b):
        r = mm_nt(feat_all[b], wkv[...].reshape(Y * 128, WIDTH)).astype(BF)
        for h in range(Y):
            kst[h, b] = r[:, h * 128 : (h + 1) * 128]
        kv_l[y, b] = kst[y, b]
        for yy, to in ysteps:
            kvs.start(kst.at[yy, b], kv_l.at[y, b], to)

    def project_qo(b):
        w = wqo[...].reshape(Y * 128, WIDTH)
        r = jnp.where(low4, mm_nt(feat_all[b], w), mm_nt(cot_all[b], w)).astype(BF)
        for h in range(Y):
            qst[h, b] = r[:, h * 128 : (h + 1) * 128]
        qg_l[y, b] = qst[y, b]
        for yy, to in ysteps:
            qgs.start(qst.at[yy, b], qg_l.at[y, b], to)

    kvs, qgs = net.group(kv_l.at[pl.ds(0, 3)]), net.group(qg_l.at[pl.ds(0, 3)])
    project_kv(x)
    project_kv(xm)
    project_kv(xp)
    tables.wait_recv()
    order_tables(asked, table)
    cp = pltpu.make_async_copy(table, smem, local_sem)
    cp.start()
    for c in ffwd:
        c.wait_recv()
    project_kv(x2)
    wown.append(wfirst(wqo))
    cx = along_x(cot, cot_all)
    cp.wait()
    tp.wait()
    kvs.wait_recv()

    going = net.group(incoming.at[pl.ds(0, CAP * (PARTS - 1))])
    for k, q in enumerate(doms):
        for c in range(CAP):
            at = jnp.clip(smem[0, q * 8 + c], 0, NBLK - 1)
            outgoing[k, c] = kv_l[lax.div(at, 4), lax.rem(at, 4)]
        going.start(outgoing.at[k], incoming.at[pl.ds(d * CAP, CAP)], dev(q, x, y))
    mqo = wmiddle(1)
    cfwd = xmiddle(cot_all, cx)
    wlast(1, mqo)
    project_qo(x)
    project_qo(xm)
    project_qo(xp)
    for c in cfwd:
        c.wait_recv()
    project_qo(x2)
    incoming[pl.ds(d * CAP, CAP)] = jnp.zeros((CAP, BLK, 128), BF)
    returned[pl.ds(d * CAP, CAP)] = jnp.zeros((CAP, BLK, 128), BF)
    for b in range(X):
        feat_t[:, b * BLK : (b + 1) * BLK] = jnp.transpose(feat_all[b])
        cot_t[:, b * BLK : (b + 1) * BLK] = jnp.transpose(cot_all[b])
    low1 = lanes((BLK, 128)) < HD
    low2 = lanes((GROUP, 128)) < HD
    for s in range(NBLK):
        kvt[s // 4, :, pl.ds((s % 4) * 128, 128)] = jnp.transpose(kv_l[s // 4, s % 4])
    qgs.wait_recv()
    for s in range(NBLK):
        p = qg_l[s // 4, s % 4]
        p = jnp.where(low1, p * 0.125, p)
        qd[s] = p
        qdt[s] = jnp.transpose(p)
    dkv[...] = jnp.zeros_like(dkv)

    nchunk = NBLK * BLK // CHUNK

    def fold(v, op):
        out = v[:, 0:128]
        for j in range(1, CHUNK // 128):
            out = op(out, v[:, j * 128 : (j + 1) * 128])
        return out

    def forward(g, _):
        p = qd[pl.ds(2 * g, 2)].reshape(GROUP, 128)
        qs = jnp.where(low2, p, jnp.zeros_like(p))
        top = None
        for c in range(nchunk):
            s = mm(qs, kvt[c])
            scores[c] = s
            t = fold(s, jnp.maximum)
            top = t if top is None else jnp.maximum(top, t)
        m = jnp.max(top, 1, keepdims=True)
        total, out = None, None
        for c in range(nchunk):
            e = jnp.exp(scores[c] - m)
            t = fold(e, jnp.add)
            total = t if total is None else total + t
            eb = e.astype(BF)
            probs[g, c] = eb
            o = mm(eb, kv_l[c].reshape(CHUNK, 128))
            out = o if out is None else out + o
        l = jnp.sum(total, 1, keepdims=True)
        outl[pl.ds(2 * g, 2)] = out.reshape(2, BLK, 128)
        mrow[pl.ds(2 * g, 2)] = jnp.broadcast_to(m, (GROUP, 128)).reshape(2, BLK, 128)
        lrow[pl.ds(2 * g, 2)] = jnp.broadcast_to(l, (GROUP, 128)).reshape(2, BLK, 128)
        return 0

    lax.fori_loop(0, NBLK // 2, forward, 0)
    going.wait_recv()

    batch = 8

    def extras(g, _):
        ids = [batch * g + i for i in range(batch)]
        blks = [qd[i] for i in ids]
        ekvs = [incoming[jnp.clip(tab[0, i], 0, PARTS * CAP - 1)] for i in ids]
        zero = jnp.zeros((BLK, 128), BF)
        ses = [mm_nt(jnp.where(low1, b, zero), e) for b, e in zip(blks, ekvs)]
        gos = [jnp.where(low1, zero, b) for b in blks]
        dps = [mm_nt(o, e) for o, e in zip(gos, ekvs)]
        ses = [jnp.where(tab[1, i] > 0, e, NEG_FILL) for i, e in zip(ids, ses)]
        mls = [mrow[i] for i in ids]
        bigs = [jnp.maximum(m, jnp.max(e, 1, keepdims=True)) for m, e in zip(mls, ses)]
        cs = [jnp.exp(m - b) for m, b in zip(mls, bigs)]
        ees = [jnp.exp(e - b) for e, b in zip(ses, bigs)]
        ls = [c * lrow[i] + jnp.sum(e, 1, keepdims=True) for c, i, e in zip(cs, ids, ees)]
        rs_ = [1.0 / v for v in ls]
        pes = [e * r for e, r in zip(ees, rs_)]
        pbs = [p.astype(BF) for p in pes]
        rls = [c * r for c, r in zip(cs, rs_)]
        outs = [
            (outl[i] * r + mm(p, e)).astype(BF).astype(F32)
            for i, r, p, e in zip(ids, rls, pbs, ekvs)
        ]
        deltas = [
            jnp.sum(o.astype(F32) * a, 1, keepdims=True) for o, a in zip(gos, outs)
        ]
        dss = [(p * (dp - dl)).astype(BF) for p, dp, dl in zip(pes, dps, deltas)]
        for n, i in enumerate(ids):
            bt = qdt[i]
            egrad[i, 0:HD] = mm(bt[0:HD], dss[n]).astype(BF)
            egrad[i, HD:128] = mm(bt[HD:128], pbs[n]).astype(BF)
        for n, i in enumerate(ids):
            dses[i] = dss[n]
            rl_s[i] = rls[n]
            rd_s[i] = rls[n] * deltas[n]
        for n in range(0, batch, 2):
            attp[(batch // 4) * g + n // 4, (n // 2) % 2] = jnp.where(
                low1, pltpu.roll(outs[n], HD, 1), outs[n + 1]
            ).astype(BF)
        return 0

    lax.fori_loop(0, NBLK // batch, extras, 0)
    home = net.group(returned.at[pl.ds(0, CAP * (PARTS - 1))])
    for k, q in enumerate(doms):
        for c in range(CAP):
            slot = q * CAP + c
            got = egrad[jnp.clip(tab[2, slot], 0, NBLK - 1)]
            sending[k, c] = jnp.where(tab[3, slot] > 0, got, jnp.zeros_like(got))
        home.start(sending.at[k], returned.at[pl.ds(d * CAP, CAP)], dev(q, x, y))
    ats = net.group(at_l.at[pl.ds(0, 3)])
    for yy, to in ysteps:
        ats.start(attp.at[yy], at_l.at[y], to)
    at_l[y] = attp[y]

    def backward(g, _):
        p = qd[pl.ds(2 * g, 2)].reshape(GROUP, 128)
        rl = rl_s[pl.ds(2 * g, 2)].reshape(GROUP, 128)
        rd = rd_s[pl.ds(2 * g, 2)].reshape(GROUP, 128)[:, :1]
        zz = jnp.where(low2, p, (p.astype(F32) * rl).astype(BF))
        zt = jnp.transpose(zz)
        go = jnp.where(low2, jnp.zeros_like(zz), zz)
        dq = jnp.concatenate(
            [
                mm(dses[2 * g + i], incoming[jnp.clip(tab[0, 2 * g + i], 0, PARTS * CAP - 1)])
                for i in range(2)
            ],
            0,
        )
        for c in range(nchunk):
            dp = mm(go, kvt[c])
            eb = probs[g, c]
            dsc = eb * (dp - rd).astype(BF)
            dq = dq + mm(dsc, kv_l[c].reshape(CHUNK, 128))
            dk = mm(zt[0:HD], dsc)
            dv = mm(zt[HD:128], eb)
            for i in range(CHUNK // 128):
                dkv[4 * c + i, 0:HD] += dk[:, i * 128 : (i + 1) * 128]
                dkv[4 * c + i, HD:128] += dv[:, i * 128 : (i + 1) * 128]
        dq = dq * 0.125
        gqp[lax.div(g, 2), lax.rem(g, 2)] = jnp.where(
            low1, dq[0:BLK], pltpu.roll(dq[BLK:GROUP], HD, 1)
        ).astype(BF)
        return 0

    lax.fori_loop(0, NBLK // 2, backward, 0)
    gqs = net.group(gq_l.at[pl.ds(0, 3)])
    for yy, to in ysteps:
        gqs.start(gqp.at[yy], gq_l.at[y], to)
    gq_l[y] = gqp[y]

    def two(ref, h, h2=None):
        h2 = h + 1 if h2 is None else h2
        return jnp.concatenate([ref[h].reshape(rows, 128), ref[h2].reshape(rows, 128)], 1)

    rows = X * BLK
    ats.wait_recv()
    for h in range(Y):
        for j in range(2):
            p = at_l[h, j].astype(F32)
            zero = jnp.zeros_like(p)
            g2[1, h, 2 * j] = jnp.where(low1, zero, pltpu.roll(p, HD, 1)).astype(BF)
            g2[1, h, 2 * j + 1] = jnp.where(low1, zero, p).astype(BF)
    for n in range(4):
        cols = pl.ds(n * 256, 256)
        o = None
        for h in range(0, Y, 2):
            t = mm(two(g2.at[1], h), wqo[h : h + 2, :, cols].reshape(256, 256))
            o = t if o is None else o + t
        part[:, 0, :, cols] = o.astype(BF).reshape(X, BLK, 256)
    xsteps = [(x2, xopp), (xp, right), (xm, left)]
    los, gfs = net.group(rs.at[:, 0]), net.group(rs.at[:, 1])
    for k, (xx, to) in enumerate(xsteps):
        los.start(part.at[xx, 0], rs.at[k, 0], to)

    yorder = [yy for yy, _ in ysteps] + [y]

    def weights(i, left_of):
        out = []
        for n in (0, 2):
            pick = yorder[n : n + 2]
            both = left_of(*pick)
            c = net.group(sibr.at[i, pl.ds(0, 2)])
            for j, h in enumerate(pick):
                wgf[i, h] = both[:, j * 128 : (j + 1) * 128].reshape(Z, 2, 64, 128)
                sibs[i, h] = wgf[i, h, :, 1 - core].astype(BF)
                c.start(sibs.at[i, h], sibr.at[i, h], sibling)
            out.append(c)
        return out

    def along_y(i, sib):
        out = net.group(yrecv.at[i])
        for k, (yy, to) in enumerate(ysteps):
            if k != 1:
                sib[k // 2].wait_recv()
            ysend[i, k] = (wgf[i, yy, :, core] + sibr[i, yy].astype(F32)).astype(BF)
            out.start(ysend.at[i, k], yrecv.at[i, k], to)
        return out

    zsteps = [lax.rem(z + k, Z) for k in (4, 3, 5, 2, 6, 1, 7)]

    def along_z(i, ys):
        total = wgf[i, y, :, core] + sibr[i, y].astype(F32)
        ys.wait_recv()
        for k in range(3):
            total = total + yrecv[i, k].astype(F32)
        own[i] = total
        zsend[i] = total.astype(BF)
        out = net.group(zrecv.at[i])
        for k, zz in enumerate(zsteps):
            out.start(zsend.at[i, zz], zrecv.at[i, k], dev(zz * 2 + core, x, y))
        return out

    def finish(i, zsum):
        res = own[i, z]
        zsum.wait_recv()
        for k in range(7):
            res = res + zrecv[i, k].astype(F32)
        wg[:, i * 128 : (i + 1) * 128] = res

    gqs.wait_recv()
    for h in range(Y):
        for j in range(2):
            p = gq_l[h, j].astype(F32)
            zero = jnp.zeros_like(p)
            g2[0, h, 2 * j] = jnp.where(low1, p, zero).astype(BF)
            g2[0, h, 2 * j + 1] = jnp.where(low1, pltpu.roll(p, HD, 1), zero).astype(BF)
    sib1 = weights(1, lambda h, h2: mm(feat_t[...], two(g2.at[0], h, h2)) + mm(cot_t[...], two(g2.at[1], h, h2)))
    y1 = along_y(1, sib1)
    for n in range(4):
        cols = pl.ds(n * 256, 256)
        o = None
        for h in range(0, Y, 2):
            t = mm(two(g2.at[0], h), wqo[h : h + 2, :, cols].reshape(256, 256))
            o = t if o is None else o + t
        gfq[:, :, cols] = o.reshape(X, BLK, 256)
    home.wait_recv()
    running = None
    for k in range(CAP * (PARTS - 1)):
        got = returned[jnp.clip(smem[1, k], 0, PARTS * CAP - 1)].astype(F32)
        running = got if k == 0 else got + running * smem[2, k].astype(F32)
        runs[k] = running
    for s in range(NBLK):
        more = jnp.where(
            smem[4, s] > 0,
            runs[jnp.clip(smem[3, s], 0, CAP * (PARTS - 1) - 1)],
            jnp.zeros((128, BLK), F32),
        )
        gkv[s // 4, s % 4] = jnp.transpose(dkv[s] + more).astype(BF)
    xorder = [(x2, xopp), (xp, right), (xm, left), (x, None)]
    gks = []
    for b, _ in xorder:
        c = net.group(g_kv.at[pl.ds(0, 3), b])
        for yy, to in ysteps:
            c.start(gkv.at[yy, b], g_kv.at[y, b], to)
        gks.append(c)
    g_kv[y] = gkv[y]
    z1 = along_z(1, y1)

    def feature_part(b):
        o = gfq[b]
        for h in range(0, Y, 2):
            g = jnp.concatenate([g_kv[h, b], g_kv[h + 1, b]], 1)
            o = o + mm(g, wkv[h : h + 2].reshape(256, WIDTH))
        part[b, 1] = o.astype(BF)

    for k, (b, to) in enumerate(xorder):
        gks[k].wait_recv()
        if k < 3:
            feature_part(b)
            gfs.start(part.at[b, 1], rs.at[k, 1], to)
    sib0 = weights(0, lambda h, h2: mm(feat_t[...], two(g_kv, h, h2)))
    feature_part(x)
    y0 = along_y(0, sib0)
    for i, (copies, base, out) in enumerate(((los, feat, lo), (gfs, cot, gf))):
        if i == 1:
            finish(1, z1)
            z0 = along_z(0, y0)
        total = part[x, i].astype(F32)
        copies.wait_recv()
        for k in range(3):
            total = total + rs[k, i].astype(F32)
        out[...] = (base[...].astype(F32) + total).astype(BF)
    finish(0, z0)
    for c in net.all:
        c.wait_send()


def hand_over_kernel(lo, gf, wg, lo_o, gf_o, q_o, k_o, v_o, o_o):
    lo_o[...] = lo[...]
    gf_o[...] = gf[...]
    for i, o in enumerate((k_o, v_o, q_o, o_o)):
        o[...] = wg[:, i * HD : (i + 1) * HD]


VM = pl.BlockSpec(memory_space=pltpu.VMEM)
SM = pl.BlockSpec(memory_space=pltpu.SMEM)
COPIES = 47


def sds(shape, dtype):
    return jax.ShapeDtypeStruct(shape, dtype)


def params(cid):
    return pltpu.CompilerParams(
        collective_id=cid, has_side_effects=True, vmem_limit_bytes=60 * 1024 * 1024
    )


def local(
    features, w_query, w_key, w_value, w_output, cotangent, cross_source, cross_target, cross_count
):
    v = pltpu.VMEM
    full = (X, BLK, WIDTH)
    four = (Y, X, BLK, 128)
    pair = (Y, 2, BLK, 128)
    blocks = (NBLK, BLK, 128)
    layer_out, grad_features, wg = pl.pallas_call(
        layer_kernel,
        out_shape=(sds((BLK, WIDTH), BF), sds((BLK, WIDTH), BF), sds((64, 256), F32)),
        in_specs=[SM] * 3 + [VM] * 6,
        out_specs=(VM,) * 3,
        scratch_shapes=[
            v((PARTS, 8, 128), F32), v((8, 128), jnp.int32), pltpu.SMEM((8, 128), jnp.int32),
            v(full, BF), v(full, BF), v((Y, 128, WIDTH), BF), v((Y, 128, WIDTH), BF),
            v((WIDTH, X * BLK), BF), v((WIDTH, X * BLK), BF),
            v((PARTS, 8, 128), F32), v((8, 128), jnp.int32), pltpu.SMEM((8, 128), jnp.int32),
            v(four, BF), v(four, BF), v(four, BF), v(four, BF),
            v((15, CAP, BLK, 128), BF), v((PARTS * CAP, BLK, 128), BF),
            v((15, CAP, BLK, 128), BF), v((PARTS * CAP, BLK, 128), BF),
            v((NBLK // 2, 4, GROUP, CHUNK), BF), v((4, GROUP, CHUNK), F32), v((4, 128, CHUNK), BF),
            v(blocks, BF), v(blocks, F32), v(blocks, F32), v(blocks, F32), v(blocks, F32),
            v(blocks, F32),
            v(blocks, F32), v(blocks, BF), v(blocks, BF), v(blocks, BF), v((30, 128, BLK), F32), v(four, BF),
            v(pair, BF), v(pair, BF), v(four, BF), v(pair, BF), v(pair, BF),
            v((X, 2, BLK, WIDTH), BF), v((X, BLK, WIDTH), F32), v((3, 2, BLK, WIDTH), BF), v((2,) + four, BF),
            v((2, Y, Z, 2, 64, 128), F32), v((2, Y, Z, 64, 128), BF), v((2, Y, Z, 64, 128), BF),
            v((2, 3, Z, 64, 128), BF), v((2, 3, Z, 64, 128), BF),
            v((2, Z, 64, 128), F32), v((2, Z, 64, 128), BF), v((2, 7, 64, 128), BF),
            pltpu.SemaphoreType.DMA((COPIES,)), pltpu.SemaphoreType.DMA((COPIES,)),
            pltpu.SemaphoreType.DMA, pltpu.SemaphoreType.DMA,
        ],
        compiler_params=params(1),
        name="layer",
    )(
        cross_source, cross_target, cross_count, features, cotangent,
        w_key.T, w_value.T, w_query.T, w_output,
    )
    square = sds((HD, HD), F32)
    return pl.pallas_call(
        hand_over_kernel,
        out_shape=(sds((BLK, WIDTH), BF), sds((BLK, WIDTH), BF), square, square, square, square),
        in_specs=[VM] * 3,
        out_specs=(VM,) * 6,
        name="hand_over",
    )(layer_out, grad_features, wg)


def solution(mesh):
    return jax.shard_map(
        local,
        mesh=mesh,
        in_specs=(
            P(("dom", "head"), None),
            P(None, "head"),
            P(None, "head"),
            P(None, "head"),
            P("head", None),
            P(("dom", "head"), None),
            P("dom", None),
            P("dom", None),
            P("dom"),
        ),
        out_specs=(
            P(("dom", "head"), None),
            P(("dom", "head"), None),
            P("dom", "head"),
            P("dom", "head"),
            P("dom", "head"),
            P("dom", "head"),
        ),
        check_vma=False,
    )
```

```python
import jax
import jax.numpy as jnp
from jax import lax
from jax.experimental import pallas as pl
from jax.experimental.pallas import tpu as pltpu
from jax.sharding import PartitionSpec as P

HD = 64
BLK = 128
CAP = 2
X = 4
Y = 4
Z = 8
PARTS = 16
NBLK = 16
WIDTH = 1024
GROUP = 256
CHUNK = 512
NEG_FILL = -1e30
MESH = pl.DeviceIdType.MESH
BF = jnp.bfloat16
F32 = jnp.float32


def mm(a, b):
    return jnp.dot(a, b, preferred_element_type=F32)


def mm_nt(a, b):
    return lax.dot_general(a, b, (((1,), (1,)), ((), ())), preferred_element_type=F32)


def place():
    d = lax.axis_index("dom")
    h = lax.axis_index("head")
    return d, lax.div(h, Y), lax.rem(h, Y)


def greet(peers, meanwhile):
    barrier = pltpu.get_barrier_semaphore()
    for peer in peers:
        pl.semaphore_signal(barrier, inc=1, device_id=peer, device_id_type=MESH)
    meanwhile()
    pl.semaphore_wait(barrier, len(peers))


def lanes(shape):
    return lax.broadcasted_iota(jnp.int32, shape, len(shape) - 1)


def turned(t):
    return lax.rem(t, 4) * 4 + lax.div(t, 4)


class Sems:
    def __init__(self, send, recv):
        self.send, self.recv, self.n, self.all = send, recv, 0, []

    def start(self, src, dst, to):
        c = pltpu.make_async_remote_copy(
            src_ref=src, dst_ref=dst, send_sem=self.send.at[self.n], recv_sem=self.recv.at[self.n],
            device_id=to, device_id_type=MESH,
        )
        c.start()
        self.n += 1
        self.all.append(c)
        return c

    def group(self, landing):
        g = Group(self, self.n, landing)
        self.n += 1
        self.all.append(g)
        return g


class Group:
    def __init__(self, net, n, landing):
        self.net, self.n, self.landing, self.to = net, n, landing, None

    def copy(self, src, dst, to):
        return pltpu.make_async_remote_copy(
            src_ref=src, dst_ref=dst, send_sem=self.net.send.at[self.n],
            recv_sem=self.net.recv.at[self.n], device_id=to, device_id_type=MESH,
        )

    def start(self, src, dst, to):
        self.to = to
        self.copy(src, dst, to).start()

    def wait_recv(self):
        self.copy(self.landing, self.landing, self.to).wait_recv()

    def wait_send(self):
        self.copy(self.landing, self.landing, self.to).wait_send()


def slot_tables(source, target, count, req, table):
    sub = lax.broadcasted_iota(jnp.int32, (128, 128), 0)
    row = lax.broadcasted_iota(jnp.int32, (8, 128), 0)
    lane = lax.broadcasted_iota(jnp.int32, (8, 128), 1)
    ask = jnp.zeros((128, 128), jnp.int32)
    tab = jnp.zeros((8, 128), jnp.int32)
    owners = []
    for j in range(16):
        src, tgt = source[0, j], target[0, j]
        owner, block = lax.div(src, NBLK), lax.rem(src, NBLK)
        position = jnp.int32(0)
        for o in owners:
            position = position + jnp.where(o == owner, 1, 0)
        owners.append(owner)
        position = jnp.minimum(position, CAP - 1)
        ask = ask + jnp.where(sub == owner * 8 + position, turned(block), 0)
        slot, pos = owner * CAP + position, turned(tgt)
        live = jnp.where(count[0] > j, 1, 0)
        here, there = lane == pos, lane == slot
        tab = tab + jnp.where((row == 0) & here, slot * live, 0)
        tab = tab + jnp.where((row == 1) & here, live, 0)
        tab = tab + jnp.where((row == 2) & there, pos * live, 0)
        tab = tab + jnp.where((row == 3) & there, live, 0)
    req[...] = ask.astype(F32).reshape(PARTS, 8, 128)
    table[...] = tab


def order_tables(asked, table):
    sub = lax.broadcasted_iota(jnp.int32, (128, 128), 0)
    lane = lax.broadcasted_iota(jnp.int32, (128, 128), 1)
    a = jnp.where((sub & 7) < CAP, asked[...].reshape(128, 128), 99.0)
    b = jnp.transpose(a)
    one, zero = jnp.ones((128, 128), F32), jnp.zeros((128, 128), F32)
    lanef = lane.astype(F32)
    less = jnp.where((b < a) | ((b == a) & (lane < sub)), one, zero)
    rank = jnp.sum(less, 1, keepdims=True)
    hot = jnp.where(rank == lanef, one, zero)
    where_from = ((sub >> 3) * CAP + (sub & 7)).astype(F32)
    order = jnp.sum(hot * where_from, 0, keepdims=True)
    value = jnp.sum(hot * a, 0, keepdims=True)
    end = jnp.sum(jnp.where(a <= lanef, one, zero), 0, keepdims=True) - 1.0
    has = jnp.sum(jnp.where(a == lanef, one, zero), 0, keepdims=True)
    wide = jnp.broadcast_to(value, (8, 128))
    same = jnp.where(wide == pltpu.roll(wide, 1, 1), one[:8], zero[:8])
    row = sub[:8]
    out = jnp.where(row == 0, jnp.minimum(b[:8], 15.0), zero[:8])
    for i, v in ((1, order), (2, same), (3, jnp.maximum(end, 0.0)), (4, has)):
        out = jnp.where(row == i, jnp.broadcast_to(v, (8, 128)), out)
    table[...] = out.astype(jnp.int32)


def layer_kernel(
    source, target, count, feat, cot, wk, wv, wq, wo,
    lo, gf, wg,
    req, tab_v, tab, feat_all, cot_all, wkv, wqo, feat_t, cot_t, asked, table, smem, kst, qst, kv_l, qg_l,
    outgoing, incoming, sending, returned, probs, scores, kvt, qd, outl, mrow, lrow, rl_s, rd_s,
    dkv, egrad, dses, qdt, runs, gkv, attp, gqp, g_kv, at_l, gq_l, part, gfq, rs, g2, wgf, sibs, sibr, ysend, yrecv,
    own, zsend, zrecv, send_sems, recv_sems, local_sem, tab_sem,
):
    d, x, y = place()
    core, z = lax.rem(d, 2), lax.div(d, 2)

    def dev(dd, xx, yy):
        return (dd, xx * Y + yy)

    xp, xm, x2 = [lax.rem(x + k, X) for k in (1, 3, 2)]
    yp, ym, y2 = [lax.rem(y + k, Y) for k in (1, 3, 2)]
    right, left, xopp = dev(d, xp, y), dev(d, xm, y), dev(d, x2, y)
    up, down, yopp = dev(d, x, yp), dev(d, x, ym), dev(d, x, y2)
    doms = [lax.rem(d + k, PARTS) for k in range(1, PARTS)]
    sibling = dev(d + 1 - 2 * core, x, y)

    def prepare():
        slot_tables(source, target, count, req, tab_v)
        for w, o in ((wkv, (wk, wv)), (wqo, (wq, wo))):
            w[y, 0:HD] = o[0][...]
            w[y, HD:128] = o[1][...]
        asked[d] = jnp.full((8, 128), 99.0, F32)
        feat_all[x] = feat[...]
        cot_all[x] = cot[...]

    greet([right, left, xopp, up, down, yopp] + [dev(q, x, y) for q in doms], prepare)
    tp = pltpu.make_async_copy(tab_v, tab, tab_sem)
    tp.start()
    net = Sems(send_sems, recv_sems)
    start = net.start
    ysteps = [(y2, yopp), (yp, up), (ym, down)]

    def along_x(own_rows, full):
        top, bottom = pl.ds(0, HD), pl.ds(HD, HD)
        out = []
        for first, second, to in ((top, bottom, right), (bottom, top, left)):
            out.append([start(own_rows.at[h], full.at[x, h], to) for h in (first, second)])
        return out

    fx = along_x(feat, feat_all)
    mine = pl.multiple_of(core * HD, HD)
    whole = pl.ds(mine, HD)
    upper, lower = pl.ds(mine, 32), pl.ds(mine + 32, 32)

    def wfirst(w):
        piece = w.at[y, whole]
        return start(piece, piece, up), start(piece, piece, down)

    wown = [wfirst(wkv)]
    tables = net.group(asked.at[pl.ds(0, PARTS - 1)])
    for q in doms:
        tables.start(req.at[q], asked.at[d], dev(q, x, y))

    def wmiddle(i):
        w = (wkv, wqo)[i]
        a, b = wown[i]
        a.wait_recv()
        p = w.at[ym, upper]
        f1 = start(p, p, up)
        p = w.at[ym, whole]
        s1 = start(p, p, sibling)
        b.wait_recv()
        p = w.at[yp, lower]
        f2 = start(p, p, down)
        p = w.at[yp, whole]
        s2 = start(p, p, sibling)
        return f1, f2, s1, s2

    def wlast(i, mid):
        w = (wkv, wqo)[i]
        mid[0].wait_recv()
        mid[1].wait_recv()
        p = w.at[y2, whole]
        s3 = start(p, p, sibling)
        mid[2].wait_recv()
        mid[3].wait_recv()
        s3.wait_recv()

    def xmiddle(full, halves):
        a0, b0 = halves[0][0], halves[1][0]
        a0.wait_recv()
        p = full.at[xm, pl.ds(0, HD)]
        f1 = start(p, p, right)
        b0.wait_recv()
        p = full.at[xp, pl.ds(HD, HD)]
        f2 = start(p, p, left)
        return f1, f2

    mkv = wmiddle(0)
    ffwd = xmiddle(feat_all, fx)
    wlast(0, mkv)
    low4 = (lanes((BLK, 512)) & 127) < HD

    def project_kv(b):
        r = mm_nt(feat_all[b], wkv[...].reshape(Y * 128, WIDTH)).astype(BF)
        for h in range(Y):
            kst[h, b] = r[:, h * 128 : (h + 1) * 128]
        kv_l[y, b] = kst[y, b]
        for yy, to in ysteps:
            kvs.start(kst.at[yy, b], kv_l.at[y, b], to)

    def project_qo(b):
        w = wqo[...].reshape(Y * 128, WIDTH)
        r = jnp.where(low4, mm_nt(feat_all[b], w), mm_nt(cot_all[b], w)).astype(BF)
        for h in range(Y):
            qst[h, b] = r[:, h * 128 : (h + 1) * 128]
        qg_l[y, b] = qst[y, b]
        for yy, to in ysteps:
            qgs.start(qst.at[yy, b], qg_l.at[y, b], to)

    kvs, qgs = net.group(kv_l.at[pl.ds(0, 3)]), net.group(qg_l.at[pl.ds(0, 3)])
    project_kv(x)
    fx[0][1].wait_recv()
    project_kv(xm)
    fx[1][1].wait_recv()
    project_kv(xp)
    tables.wait_recv()
    order_tables(asked, table)
    cp = pltpu.make_async_copy(table, smem, local_sem)
    cp.start()
    for c in ffwd:
        c.wait_recv()
    project_kv(x2)
    wown.append(wfirst(wqo))
    cx = along_x(cot, cot_all)
    cp.wait()
    tp.wait()
    kvs.wait_recv()

    going = net.group(incoming.at[pl.ds(0, CAP * (PARTS - 1))])
    for k, q in enumerate(doms):
        for c in range(CAP):
            at = jnp.clip(smem[0, q * 8 + c], 0, NBLK - 1)
            outgoing[k, c] = kv_l[lax.div(at, 4), lax.rem(at, 4)]
        going.start(outgoing.at[k], incoming.at[pl.ds(d * CAP, CAP)], dev(q, x, y))
    mqo = wmiddle(1)
    cfwd = xmiddle(cot_all, cx)
    cx[0][1].wait_recv()
    cx[1][1].wait_recv()
    wlast(1, mqo)
    project_qo(x)
    project_qo(xm)
    project_qo(xp)
    for c in cfwd:
        c.wait_recv()
    project_qo(x2)
    incoming[pl.ds(d * CAP, CAP)] = jnp.zeros((CAP, BLK, 128), BF)
    returned[pl.ds(d * CAP, CAP)] = jnp.zeros((CAP, BLK, 128), BF)
    for b in range(X):
        feat_t[:, b * BLK : (b + 1) * BLK] = jnp.transpose(feat_all[b])
        cot_t[:, b * BLK : (b + 1) * BLK] = jnp.transpose(cot_all[b])
    low1 = lanes((BLK, 128)) < HD
    low2 = lanes((GROUP, 128)) < HD
    for s in range(NBLK):
        kvt[s // 4, :, pl.ds((s % 4) * 128, 128)] = jnp.transpose(kv_l[s // 4, s % 4])
    qgs.wait_recv()
    for s in range(NBLK):
        p = qg_l[s // 4, s % 4]
        p = jnp.where(low1, p * 0.125, p)
        qd[s] = p
        qdt[s] = jnp.transpose(p)
    dkv[...] = jnp.zeros_like(dkv)

    nchunk = NBLK * BLK // CHUNK

    def fold(v, op):
        out = v[:, 0:128]
        for j in range(1, CHUNK // 128):
            out = op(out, v[:, j * 128 : (j + 1) * 128])
        return out

    def forward(g, _):
        p = qd[pl.ds(2 * g, 2)].reshape(GROUP, 128)
        qs = jnp.where(low2, p, jnp.zeros_like(p))
        top = None
        for c in range(nchunk):
            s = mm(qs, kvt[c])
            scores[c] = s
            t = fold(s, jnp.maximum)
            top = t if top is None else jnp.maximum(top, t)
        m = jnp.max(top, 1, keepdims=True)
        total, out = None, None
        for c in range(nchunk):
            e = jnp.exp(scores[c] - m)
            t = fold(e, jnp.add)
            total = t if total is None else total + t
            eb = e.astype(BF)
            probs[g, c] = eb
            o = mm(eb, kv_l[c].reshape(CHUNK, 128))
            out = o if out is None else out + o
        l = jnp.sum(total, 1, keepdims=True)
        outl[pl.ds(2 * g, 2)] = out.reshape(2, BLK, 128)
        mrow[pl.ds(2 * g, 2)] = jnp.broadcast_to(m, (GROUP, 128)).reshape(2, BLK, 128)
        lrow[pl.ds(2 * g, 2)] = jnp.broadcast_to(l, (GROUP, 128)).reshape(2, BLK, 128)
        return 0

    lax.fori_loop(0, NBLK // 2, forward, 0)
    going.wait_recv()

    batch = 8

    def extras(g, _):
        ids = [batch * g + i for i in range(batch)]
        blks = [qd[i] for i in ids]
        ekvs = [incoming[jnp.clip(tab[0, i], 0, PARTS * CAP - 1)] for i in ids]
        zero = jnp.zeros((BLK, 128), BF)
        ses = [mm_nt(jnp.where(low1, b, zero), e) for b, e in zip(blks, ekvs)]
        gos = [jnp.where(low1, zero, b) for b in blks]
        dps = [mm_nt(o, e) for o, e in zip(gos, ekvs)]
        ses = [jnp.where(tab[1, i] > 0, e, NEG_FILL) for i, e in zip(ids, ses)]
        mls = [mrow[i] for i in ids]
        bigs = [jnp.maximum(m, jnp.max(e, 1, keepdims=True)) for m, e in zip(mls, ses)]
        cs = [jnp.exp(m - b) for m, b in zip(mls, bigs)]
        ees = [jnp.exp(e - b) for e, b in zip(ses, bigs)]
        ls = [c * lrow[i] + jnp.sum(e, 1, keepdims=True) for c, i, e in zip(cs, ids, ees)]
        rs_ = [1.0 / v for v in ls]
        pes = [e * r for e, r in zip(ees, rs_)]
        pbs = [p.astype(BF) for p in pes]
        rls = [c * r for c, r in zip(cs, rs_)]
        outs = [
            (outl[i] * r + mm(p, e)).astype(BF).astype(F32)
            for i, r, p, e in zip(ids, rls, pbs, ekvs)
        ]
        deltas = [
            jnp.sum(o.astype(F32) * a, 1, keepdims=True) for o, a in zip(gos, outs)
        ]
        dss = [(p * (dp - dl)).astype(BF) for p, dp, dl in zip(pes, dps, deltas)]
        for n, i in enumerate(ids):
            bt = qdt[i]
            egrad[i, 0:HD] = mm(bt[0:HD], dss[n]).astype(BF)
            egrad[i, HD:128] = mm(bt[HD:128], pbs[n]).astype(BF)
        for n, i in enumerate(ids):
            dses[i] = dss[n]
            rl_s[i] = rls[n]
            rd_s[i] = rls[n] * deltas[n]
        for n in range(0, batch, 2):
            attp[(batch // 4) * g + n // 4, (n // 2) % 2] = jnp.where(
                low1, pltpu.roll(outs[n], HD, 1), outs[n + 1]
            ).astype(BF)
        return 0

    lax.fori_loop(0, NBLK // batch, extras, 0)
    home = net.group(returned.at[pl.ds(0, CAP * (PARTS - 1))])
    for k, q in enumerate(doms):
        for c in range(CAP):
            slot = q * CAP + c
            got = egrad[jnp.clip(tab[2, slot], 0, NBLK - 1)]
            sending[k, c] = jnp.where(tab[3, slot] > 0, got, jnp.zeros_like(got))
        home.start(sending.at[k], returned.at[pl.ds(d * CAP, CAP)], dev(q, x, y))
    ats = net.group(at_l.at[pl.ds(0, 3)])
    for yy, to in ysteps:
        ats.start(attp.at[yy], at_l.at[y], to)
    at_l[y] = attp[y]

    def backward(g, _):
        p = qd[pl.ds(2 * g, 2)].reshape(GROUP, 128)
        rl = rl_s[pl.ds(2 * g, 2)].reshape(GROUP, 128)
        rd = rd_s[pl.ds(2 * g, 2)].reshape(GROUP, 128)[:, :1]
        zz = jnp.where(low2, p, (p.astype(F32) * rl).astype(BF))
        zt = jnp.transpose(zz)
        go = jnp.where(low2, jnp.zeros_like(zz), zz)
        dq = jnp.concatenate(
            [
                mm(dses[2 * g + i], incoming[jnp.clip(tab[0, 2 * g + i], 0, PARTS * CAP - 1)])
                for i in range(2)
            ],
            0,
        )
        for c in range(nchunk):
            dp = mm(go, kvt[c])
            eb = probs[g, c]
            dsc = eb * (dp - rd).astype(BF)
            dq = dq + mm(dsc, kv_l[c].reshape(CHUNK, 128))
            dk = mm(zt[0:HD], dsc)
            dv = mm(zt[HD:128], eb)
            for i in range(CHUNK // 128):
                dkv[4 * c + i, 0:HD] += dk[:, i * 128 : (i + 1) * 128]
                dkv[4 * c + i, HD:128] += dv[:, i * 128 : (i + 1) * 128]
        dq = dq * 0.125
        gqp[lax.div(g, 2), lax.rem(g, 2)] = jnp.where(
            low1, dq[0:BLK], pltpu.roll(dq[BLK:GROUP], HD, 1)
        ).astype(BF)
        return 0

    lax.fori_loop(0, NBLK // 2, backward, 0)
    gqs = net.group(gq_l.at[pl.ds(0, 3)])
    for yy, to in ysteps:
        gqs.start(gqp.at[yy], gq_l.at[y], to)
    gq_l[y] = gqp[y]

    def two(ref, h, h2=None):
        h2 = h + 1 if h2 is None else h2
        return jnp.concatenate([ref[h].reshape(rows, 128), ref[h2].reshape(rows, 128)], 1)

    rows = X * BLK
    ats.wait_recv()
    for h in range(Y):
        for j in range(2):
            p = at_l[h, j].astype(F32)
            zero = jnp.zeros_like(p)
            g2[1, h, 2 * j] = jnp.where(low1, zero, pltpu.roll(p, HD, 1)).astype(BF)
            g2[1, h, 2 * j + 1] = jnp.where(low1, zero, p).astype(BF)
    for n in range(4):
        cols = pl.ds(n * 256, 256)
        o = None
        for h in range(0, Y, 2):
            t = mm(two(g2.at[1], h), wqo[h : h + 2, :, cols].reshape(256, 256))
            o = t if o is None else o + t
        part[:, 0, :, cols] = o.astype(BF).reshape(X, BLK, 256)
    xsteps = [(x2, xopp), (xp, right), (xm, left)]
    los, gfs = net.group(rs.at[:, 0]), net.group(rs.at[:, 1])
    for k, (xx, to) in enumerate(xsteps):
        los.start(part.at[xx, 0], rs.at[k, 0], to)

    yorder = [yy for yy, _ in ysteps] + [y]

    def weights(i, left_of):
        out = []
        for n in (0, 2):
            pick = yorder[n : n + 2]
            both = left_of(*pick)
            c = net.group(sibr.at[i, pl.ds(0, 2)])
            for j, h in enumerate(pick):
                wgf[i, h] = both[:, j * 128 : (j + 1) * 128].reshape(Z, 2, 64, 128)
                sibs[i, h] = wgf[i, h, :, 1 - core].astype(BF)
                c.start(sibs.at[i, h], sibr.at[i, h], sibling)
            out.append(c)
        return out

    def along_y(i, sib):
        out = net.group(yrecv.at[i])
        for k, (yy, to) in enumerate(ysteps):
            if k != 1:
                sib[k // 2].wait_recv()
            ysend[i, k] = (wgf[i, yy, :, core] + sibr[i, yy].astype(F32)).astype(BF)
            out.start(ysend.at[i, k], yrecv.at[i, k], to)
        return out

    zsteps = [lax.rem(z + k, Z) for k in (4, 3, 5, 2, 6, 1, 7)]

    def along_z(i, ys):
        total = wgf[i, y, :, core] + sibr[i, y].astype(F32)
        ys.wait_recv()
        for k in range(3):
            total = total + yrecv[i, k].astype(F32)
        own[i] = total
        zsend[i] = total.astype(BF)
        out = net.group(zrecv.at[i])
        for k, zz in enumerate(zsteps):
            out.start(zsend.at[i, zz], zrecv.at[i, k], dev(zz * 2 + core, x, y))
        return out

    def finish(i, zsum):
        res = own[i, z]
        zsum.wait_recv()
        for k in range(7):
            res = res + zrecv[i, k].astype(F32)
        wg[:, i * 128 : (i + 1) * 128] = res

    gqs.wait_recv()
    for h in range(Y):
        for j in range(2):
            p = gq_l[h, j].astype(F32)
            zero = jnp.zeros_like(p)
            g2[0, h, 2 * j] = jnp.where(low1, p, zero).astype(BF)
            g2[0, h, 2 * j + 1] = jnp.where(low1, pltpu.roll(p, HD, 1), zero).astype(BF)
    sib1 = weights(1, lambda h, h2: mm(feat_t[...], two(g2.at[0], h, h2)) + mm(cot_t[...], two(g2.at[1], h, h2)))
    y1 = along_y(1, sib1)
    for n in range(4):
        cols = pl.ds(n * 256, 256)
        o = None
        for h in range(0, Y, 2):
            t = mm(two(g2.at[0], h), wqo[h : h + 2, :, cols].reshape(256, 256))
            o = t if o is None else o + t
        gfq[:, :, cols] = o.reshape(X, BLK, 256)
    home.wait_recv()
    running = None
    for k in range(CAP * (PARTS - 1)):
        got = returned[jnp.clip(smem[1, k], 0, PARTS * CAP - 1)].astype(F32)
        running = got if k == 0 else got + running * smem[2, k].astype(F32)
        runs[k] = running
    for s in range(NBLK):
        more = jnp.where(
            smem[4, s] > 0,
            runs[jnp.clip(smem[3, s], 0, CAP * (PARTS - 1) - 1)],
            jnp.zeros((128, BLK), F32),
        )
        gkv[s // 4, s % 4] = jnp.transpose(dkv[s] + more).astype(BF)
    xorder = [(x2, xopp), (xp, right), (xm, left), (x, None)]
    gks = []
    for b, _ in xorder:
        c = net.group(g_kv.at[pl.ds(0, 3), b])
        for yy, to in ysteps:
            c.start(gkv.at[yy, b], g_kv.at[y, b], to)
        gks.append(c)
    g_kv[y] = gkv[y]
    z1 = along_z(1, y1)

    def feature_part(b):
        o = gfq[b]
        for h in range(0, Y, 2):
            g = jnp.concatenate([g_kv[h, b], g_kv[h + 1, b]], 1)
            o = o + mm(g, wkv[h : h + 2].reshape(256, WIDTH))
        part[b, 1] = o.astype(BF)

    for k, (b, to) in enumerate(xorder):
        gks[k].wait_recv()
        if k < 3:
            feature_part(b)
            gfs.start(part.at[b, 1], rs.at[k, 1], to)
    sib0 = weights(0, lambda h, h2: mm(feat_t[...], two(g_kv, h, h2)))
    feature_part(x)
    y0 = along_y(0, sib0)
    for i, (copies, base, out) in enumerate(((los, feat, lo), (gfs, cot, gf))):
        if i == 1:
            finish(1, z1)
            z0 = along_z(0, y0)
        total = part[x, i].astype(F32)
        copies.wait_recv()
        for k in range(3):
            total = total + rs[k, i].astype(F32)
        out[...] = (base[...].astype(F32) + total).astype(BF)
    finish(0, z0)
    for c in net.all:
        c.wait_send()


def hand_over_kernel(lo, gf, wg, lo_o, gf_o, q_o, k_o, v_o, o_o):
    lo_o[...] = lo[...]
    gf_o[...] = gf[...]
    for i, o in enumerate((k_o, v_o, q_o, o_o)):
        o[...] = wg[:, i * HD : (i + 1) * HD]


VM = pl.BlockSpec(memory_space=pltpu.VMEM)
SM = pl.BlockSpec(memory_space=pltpu.SMEM)
COPIES = 47


def sds(shape, dtype):
    return jax.ShapeDtypeStruct(shape, dtype)


def params(cid):
    return pltpu.CompilerParams(
        collective_id=cid, has_side_effects=True, vmem_limit_bytes=60 * 1024 * 1024
    )


def local(
    features, w_query, w_key, w_value, w_output, cotangent, cross_source, cross_target, cross_count
):
    v = pltpu.VMEM
    full = (X, BLK, WIDTH)
    four = (Y, X, BLK, 128)
    pair = (Y, 2, BLK, 128)
    blocks = (NBLK, BLK, 128)
    layer_out, grad_features, wg = pl.pallas_call(
        layer_kernel,
        out_shape=(sds((BLK, WIDTH), BF), sds((BLK, WIDTH), BF), sds((64, 256), F32)),
        in_specs=[SM] * 3 + [VM] * 6,
        out_specs=(VM,) * 3,
        scratch_shapes=[
            v((PARTS, 8, 128), F32), v((8, 128), jnp.int32), pltpu.SMEM((8, 128), jnp.int32),
            v(full, BF), v(full, BF), v((Y, 128, WIDTH), BF), v((Y, 128, WIDTH), BF),
            v((WIDTH, X * BLK), BF), v((WIDTH, X * BLK), BF),
            v((PARTS, 8, 128), F32), v((8, 128), jnp.int32), pltpu.SMEM((8, 128), jnp.int32),
            v(four, BF), v(four, BF), v(four, BF), v(four, BF),
            v((15, CAP, BLK, 128), BF), v((PARTS * CAP, BLK, 128), BF),
            v((15, CAP, BLK, 128), BF), v((PARTS * CAP, BLK, 128), BF),
            v((NBLK // 2, 4, GROUP, CHUNK), BF), v((4, GROUP, CHUNK), F32), v((4, 128, CHUNK), BF),
            v(blocks, BF), v(blocks, F32), v(blocks, F32), v(blocks, F32), v(blocks, F32),
            v(blocks, F32),
            v(blocks, F32), v(blocks, BF), v(blocks, BF), v(blocks, BF), v((30, 128, BLK), F32), v(four, BF),
            v(pair, BF), v(pair, BF), v(four, BF), v(pair, BF), v(pair, BF),
            v((X, 2, BLK, WIDTH), BF), v((X, BLK, WIDTH), F32), v((3, 2, BLK, WIDTH), BF), v((2,) + four, BF),
            v((2, Y, Z, 2, 64, 128), F32), v((2, Y, Z, 64, 128), BF), v((2, Y, Z, 64, 128), BF),
            v((2, 3, Z, 64, 128), BF), v((2, 3, Z, 64, 128), BF),
            v((2, Z, 64, 128), F32), v((2, Z, 64, 128), BF), v((2, 7, 64, 128), BF),
            pltpu.SemaphoreType.DMA((COPIES,)), pltpu.SemaphoreType.DMA((COPIES,)),
            pltpu.SemaphoreType.DMA, pltpu.SemaphoreType.DMA,
        ],
        compiler_params=params(1),
        name="layer",
    )(
        cross_source, cross_target, cross_count, features, cotangent,
        w_key.T, w_value.T, w_query.T, w_output,
    )
    square = sds((HD, HD), F32)
    return pl.pallas_call(
        hand_over_kernel,
        out_shape=(sds((BLK, WIDTH), BF), sds((BLK, WIDTH), BF), square, square, square, square),
        in_specs=[VM] * 3,
        out_specs=(VM,) * 6,
        name="hand_over",
    )(layer_out, grad_features, wg)


def solution(mesh):
    return jax.shard_map(
        local,
        mesh=mesh,
        in_specs=(
            P(("dom", "head"), None),
            P(None, "head"),
            P(None, "head"),
            P(None, "head"),
            P("head", None),
            P(("dom", "head"), None),
            P("dom", None),
            P("dom", None),
            P("dom"),
        ),
        out_specs=(
            P(("dom", "head"), None),
            P(("dom", "head"), None),
            P("dom", "head"),
            P("dom", "head"),
            P("dom", "head"),
            P("dom", "head"),
        ),
        check_vma=False,
    )
```

```python
import jax
import jax.numpy as jnp
from jax import lax
from jax.experimental import pallas as pl
from jax.experimental.pallas import tpu as pltpu
from jax.sharding import PartitionSpec as P

HD = 64
BLK = 128
CAP = 2
X = 4
Y = 4
Z = 8
PARTS = 16
NBLK = 16
WIDTH = 1024
GROUP = 256
CHUNK = 512
NEG_FILL = -1e30
MESH = pl.DeviceIdType.MESH
BF = jnp.bfloat16
F32 = jnp.float32


def mm(a, b):
    return jnp.dot(a, b, preferred_element_type=F32)


def mm_nt(a, b):
    return lax.dot_general(a, b, (((1,), (1,)), ((), ())), preferred_element_type=F32)


def place():
    d = lax.axis_index("dom")
    h = lax.axis_index("head")
    return d, lax.div(h, Y), lax.rem(h, Y)


def greet(peers, meanwhile):
    barrier = pltpu.get_barrier_semaphore()
    for peer in peers:
        pl.semaphore_signal(barrier, inc=1, device_id=peer, device_id_type=MESH)
    meanwhile()
    pl.semaphore_wait(barrier, len(peers))


def lanes(shape):
    return lax.broadcasted_iota(jnp.int32, shape, len(shape) - 1)


def turned(t):
    return lax.rem(t, 4) * 4 + lax.div(t, 4)


class Sems:
    def __init__(self, send, recv):
        self.send, self.recv, self.n, self.all = send, recv, 0, []

    def start(self, src, dst, to):
        c = pltpu.make_async_remote_copy(
            src_ref=src, dst_ref=dst, send_sem=self.send.at[self.n], recv_sem=self.recv.at[self.n],
            device_id=to, device_id_type=MESH,
        )
        c.start()
        self.n += 1
        self.all.append(c)
        return c

    def group(self, landing):
        g = Group(self, self.n, landing)
        self.n += 1
        self.all.append(g)
        return g


class Group:
    def __init__(self, net, n, landing):
        self.net, self.n, self.landing, self.to = net, n, landing, None

    def copy(self, src, dst, to):
        return pltpu.make_async_remote_copy(
            src_ref=src, dst_ref=dst, send_sem=self.net.send.at[self.n],
            recv_sem=self.net.recv.at[self.n], device_id=to, device_id_type=MESH,
        )

    def start(self, src, dst, to):
        self.to = to
        self.copy(src, dst, to).start()

    def wait_recv(self):
        self.copy(self.landing, self.landing, self.to).wait_recv()

    def wait_send(self):
        self.copy(self.landing, self.landing, self.to).wait_send()


def slot_tables(source, target, count, req, table):
    sub = lax.broadcasted_iota(jnp.int32, (128, 128), 0)
    row = lax.broadcasted_iota(jnp.int32, (8, 128), 0)
    lane = lax.broadcasted_iota(jnp.int32, (8, 128), 1)
    ask = jnp.zeros((128, 128), jnp.int32)
    tab = jnp.zeros((8, 128), jnp.int32)
    owners = []
    for j in range(16):
        src, tgt = source[0, j], target[0, j]
        owner, block = lax.div(src, NBLK), lax.rem(src, NBLK)
        position = jnp.int32(0)
        for o in owners:
            position = position + jnp.where(o == owner, 1, 0)
        owners.append(owner)
        position = jnp.minimum(position, CAP - 1)
        ask = ask + jnp.where(sub == owner * 8 + position, turned(block), 0)
        slot, pos = owner * CAP + position, turned(tgt)
        live = jnp.where(count[0] > j, 1, 0)
        here, there = lane == pos, lane == slot
        tab = tab + jnp.where((row == 0) & here, slot * live, 0)
        tab = tab + jnp.where((row == 1) & here, live, 0)
        tab = tab + jnp.where((row == 2) & there, pos * live, 0)
        tab = tab + jnp.where((row == 3) & there, live, 0)
    req[...] = ask.astype(F32).reshape(PARTS, 8, 128)
    table[...] = tab


def order_tables(asked, table):
    sub = lax.broadcasted_iota(jnp.int32, (128, 128), 0)
    lane = lax.broadcasted_iota(jnp.int32, (128, 128), 1)
    a = jnp.where((sub & 7) < CAP, asked[...].reshape(128, 128), 99.0)
    b = jnp.transpose(a)
    one, zero = jnp.ones((128, 128), F32), jnp.zeros((128, 128), F32)
    lanef = lane.astype(F32)
    less = jnp.where((b < a) | ((b == a) & (lane < sub)), one, zero)
    rank = jnp.sum(less, 1, keepdims=True)
    hot = jnp.where(rank == lanef, one, zero)
    where_from = ((sub >> 3) * CAP + (sub & 7)).astype(F32)
    order = jnp.sum(hot * where_from, 0, keepdims=True)
    value = jnp.sum(hot * a, 0, keepdims=True)
    end = jnp.sum(jnp.where(a <= lanef, one, zero), 0, keepdims=True) - 1.0
    has = jnp.sum(jnp.where(a == lanef, one, zero), 0, keepdims=True)
    wide = jnp.broadcast_to(value, (8, 128))
    same = jnp.where(wide == pltpu.roll(wide, 1, 1), one[:8], zero[:8])
    row = sub[:8]
    out = jnp.where(row == 0, jnp.minimum(b[:8], 15.0), zero[:8])
    for i, v in ((1, order), (2, same), (3, jnp.maximum(end, 0.0)), (4, has)):
        out = jnp.where(row == i, jnp.broadcast_to(v, (8, 128)), out)
    table[...] = out.astype(jnp.int32)


def layer_kernel(
    source, target, count, feat, cot, wk, wv, wq, wo,
    lo, gf, wg,
    req, tab_v, tab, feat_all, cot_all, wkv, wqo, feat_t, cot_t, asked, table, smem, kst, qst, kv_l, qg_l,
    outgoing, incoming, sending, returned, probs, scores, kvt, qd, outl, mrow, lrow, rl_s, rd_s,
    dkv, egrad, dses, qdt, runs, gkv, attp, gqp, g_kv, at_l, gq_l, part, gfq, rs, g2, wgf, sibs, sibr, ysend, yrecv,
    own, zsend, zrecv, send_sems, recv_sems, local_sem, tab_sem,
):
    d, x, y = place()
    core, z = lax.rem(d, 2), lax.div(d, 2)

    def dev(dd, xx, yy):
        return (dd, xx * Y + yy)

    xp, xm, x2 = [lax.rem(x + k, X) for k in (1, 3, 2)]
    yp, ym, y2 = [lax.rem(y + k, Y) for k in (1, 3, 2)]
    right, left, xopp = dev(d, xp, y), dev(d, xm, y), dev(d, x2, y)
    up, down, yopp = dev(d, x, yp), dev(d, x, ym), dev(d, x, y2)
    doms = [lax.rem(d + k, PARTS) for k in range(1, PARTS)]
    sibling = dev(d + 1 - 2 * core, x, y)

    def prepare():
        slot_tables(source, target, count, req, tab_v)
        for w, o in ((wkv, (wk, wv)), (wqo, (wq, wo))):
            w[y, 0:HD] = o[0][...]
            w[y, HD:128] = o[1][...]
        asked[d] = jnp.full((8, 128), 99.0, F32)
        feat_all[x] = feat[...]
        cot_all[x] = cot[...]

    greet([right, left, xopp, up, down, yopp] + [dev(q, x, y) for q in doms], prepare)
    tp = pltpu.make_async_copy(tab_v, tab, tab_sem)
    tp.start()
    net = Sems(send_sems, recv_sems)
    start = net.start
    ysteps = [(y2, yopp), (yp, up), (ym, down)]

    def along_x(own_rows, full):
        top, bottom = pl.ds(0, HD), pl.ds(HD, HD)
        out = []
        for first, second, to in ((top, bottom, right), (bottom, top, left)):
            out.append([start(own_rows.at[h], full.at[x, h], to) for h in (first, second)])
        return out

    fx = along_x(feat, feat_all)
    mine = pl.multiple_of(core * HD, HD)
    whole = pl.ds(mine, HD)
    upper, lower = pl.ds(mine, 32), pl.ds(mine + 32, 32)

    def wfirst(w):
        piece = w.at[y, whole]
        return start(piece, piece, up), start(piece, piece, down)

    wown = [wfirst(wkv)]
    tables = net.group(asked.at[pl.ds(0, PARTS - 1)])
    for q in doms:
        tables.start(req.at[q], asked.at[d], dev(q, x, y))

    def wmiddle(i):
        w = (wkv, wqo)[i]
        a, b = wown[i]
        a.wait_recv()
        p = w.at[ym, upper]
        f1 = start(p, p, up)
        p = w.at[ym, whole]
        s1 = start(p, p, sibling)
        b.wait_recv()
        p = w.at[yp, lower]
        f2 = start(p, p, down)
        p = w.at[yp, whole]
        s2 = start(p, p, sibling)
        return f1, f2, s1, s2

    def wlast(i, mid):
        w = (wkv, wqo)[i]
        mid[0].wait_recv()
        mid[1].wait_recv()
        p = w.at[y2, whole]
        s3 = start(p, p, sibling)
        mid[2].wait_recv()
        mid[3].wait_recv()
        s3.wait_recv()

    def xmiddle(full, halves):
        (a0, a1), (b0, b1) = halves
        a0.wait_recv()
        p = full.at[xm, pl.ds(0, HD)]
        f1 = start(p, p, right)
        b0.wait_recv()
        p = full.at[xp, pl.ds(HD, HD)]
        f2 = start(p, p, left)
        a1.wait_recv()
        b1.wait_recv()
        return f1, f2

    mkv = wmiddle(0)
    ffwd = xmiddle(feat_all, fx)
    wlast(0, mkv)
    low4 = (lanes((BLK, 512)) & 127) < HD

    def project_kv(b):
        r = mm_nt(feat_all[b], wkv[...].reshape(Y * 128, WIDTH)).astype(BF)
        for h in range(Y):
            kst[h, b] = r[:, h * 128 : (h + 1) * 128]
        kv_l[y, b] = kst[y, b]
        for yy, to in ysteps:
            kvs.start(kst.at[yy, b], kv_l.at[y, b], to)

    def project_qo(b):
        w = wqo[...].reshape(Y * 128, WIDTH)
        r = jnp.where(low4, mm_nt(feat_all[b], w), mm_nt(cot_all[b], w)).astype(BF)
        for h in range(Y):
            qst[h, b] = r[:, h * 128 : (h + 1) * 128]
        qg_l[y, b] = qst[y, b]
        for yy, to in ysteps:
            qgs.start(qst.at[yy, b], qg_l.at[y, b], to)

    kvs, qgs = net.group(kv_l.at[pl.ds(0, 3)]), net.group(qg_l.at[pl.ds(0, 3)])
    project_kv(x)
    project_kv(xm)
    project_kv(xp)
    tables.wait_recv()
    order_tables(asked, table)
    cp = pltpu.make_async_copy(table, smem, local_sem)
    cp.start()
    for c in ffwd:
        c.wait_recv()
    project_kv(x2)
    wown.append(wfirst(wqo))
    cx = along_x(cot, cot_all)
    cp.wait()
    tp.wait()
    kvs.wait_recv()

    going = net.group(incoming.at[pl.ds(0, CAP * (PARTS - 1))])
    for k, q in enumerate(doms):
        for c in range(CAP):
            at = jnp.clip(smem[0, q * 8 + c], 0, NBLK - 1)
            outgoing[k, c] = kv_l[lax.div(at, 4), lax.rem(at, 4)]
        going.start(outgoing.at[k], incoming.at[pl.ds(d * CAP, CAP)], dev(q, x, y))
    mqo = wmiddle(1)
    cfwd = xmiddle(cot_all, cx)
    wlast(1, mqo)
    project_qo(x)
    project_qo(xm)
    project_qo(xp)
    for c in cfwd:
        c.wait_recv()
    project_qo(x2)
    incoming[pl.ds(d * CAP, CAP)] = jnp.zeros((CAP, BLK, 128), BF)
    returned[pl.ds(d * CAP, CAP)] = jnp.zeros((CAP, BLK, 128), BF)
    for b in range(X):
        feat_t[:, b * BLK : (b + 1) * BLK] = jnp.transpose(feat_all[b])
        cot_t[:, b * BLK : (b + 1) * BLK] = jnp.transpose(cot_all[b])
    low1 = lanes((BLK, 128)) < HD
    low2 = lanes((GROUP, 128)) < HD
    for s in range(NBLK):
        kvt[s // 4, :, pl.ds((s % 4) * 128, 128)] = jnp.transpose(kv_l[s // 4, s % 4])
    qgs.wait_recv()
    for s in range(NBLK):
        p = qg_l[s // 4, s % 4]
        p = jnp.where(low1, p * 0.125, p)
        qd[s] = p
        qdt[s] = jnp.transpose(p)
    dkv[...] = jnp.zeros_like(dkv)

    nchunk = NBLK * BLK // CHUNK

    def fold(v, op):
        out = v[:, 0:128]
        for j in range(1, CHUNK // 128):
            out = op(out, v[:, j * 128 : (j + 1) * 128])
        return out

    def forward(g, _):
        p = qd[pl.ds(2 * g, 2)].reshape(GROUP, 128)
        qs = jnp.where(low2, p, jnp.zeros_like(p))
        top = None
        for c in range(nchunk):
            s = mm(qs, kvt[c])
            scores[c] = s
            t = fold(s, jnp.maximum)
            top = t if top is None else jnp.maximum(top, t)
        m = jnp.max(top, 1, keepdims=True)
        total, out = None, None
        for c in range(nchunk):
            e = jnp.exp(scores[c] - m)
            t = fold(e, jnp.add)
            total = t if total is None else total + t
            eb = e.astype(BF)
            probs[g, c] = eb
            o = mm(eb, kv_l[c].reshape(CHUNK, 128))
            out = o if out is None else out + o
        l = jnp.sum(total, 1, keepdims=True)
        outl[pl.ds(2 * g, 2)] = out.reshape(2, BLK, 128)
        mrow[pl.ds(2 * g, 2)] = jnp.broadcast_to(m, (GROUP, 128)).reshape(2, BLK, 128)
        lrow[pl.ds(2 * g, 2)] = jnp.broadcast_to(l, (GROUP, 128)).reshape(2, BLK, 128)
        return 0

    lax.fori_loop(0, NBLK // 2, forward, 0)
    going.wait_recv()

    batch = 8

    def extras(g, _):
        ids = [batch * g + i for i in range(batch)]
        blks = [qd[i] for i in ids]
        ekvs = [incoming[jnp.clip(tab[0, i], 0, PARTS * CAP - 1)] for i in ids]
        zero = jnp.zeros((BLK, 128), BF)
        ses = [mm_nt(jnp.where(low1, b, zero), e) for b, e in zip(blks, ekvs)]
        gos = [jnp.where(low1, zero, b) for b in blks]
        dps = [mm_nt(o, e) for o, e in zip(gos, ekvs)]
        ses = [jnp.where(tab[1, i] > 0, e, NEG_FILL) for i, e in zip(ids, ses)]
        mls = [mrow[i] for i in ids]
        bigs = [jnp.maximum(m, jnp.max(e, 1, keepdims=True)) for m, e in zip(mls, ses)]
        cs = [jnp.exp(m - b) for m, b in zip(mls, bigs)]
        ees = [jnp.exp(e - b) for e, b in zip(ses, bigs)]
        ls = [c * lrow[i] + jnp.sum(e, 1, keepdims=True) for c, i, e in zip(cs, ids, ees)]
        rs_ = [1.0 / v for v in ls]
        pes = [e * r for e, r in zip(ees, rs_)]
        pbs = [p.astype(BF) for p in pes]
        rls = [c * r for c, r in zip(cs, rs_)]
        outs = [
            (outl[i] * r + mm(p, e)).astype(BF).astype(F32)
            for i, r, p, e in zip(ids, rls, pbs, ekvs)
        ]
        deltas = [
            jnp.sum(o.astype(F32) * a, 1, keepdims=True) for o, a in zip(gos, outs)
        ]
        dss = [(p * (dp - dl)).astype(BF) for p, dp, dl in zip(pes, dps, deltas)]
        for n, i in enumerate(ids):
            bt = qdt[i]
            egrad[i, 0:HD] = mm(bt[0:HD], dss[n]).astype(BF)
            egrad[i, HD:128] = mm(bt[HD:128], pbs[n]).astype(BF)
        for n, i in enumerate(ids):
            dses[i] = dss[n]
            rl_s[i] = rls[n]
            rd_s[i] = rls[n] * deltas[n]
        for n in range(0, batch, 2):
            attp[(batch // 4) * g + n // 4, (n // 2) % 2] = jnp.where(
                low1, pltpu.roll(outs[n], HD, 1), outs[n + 1]
            ).astype(BF)
        return 0

    lax.fori_loop(0, NBLK // batch, extras, 0)
    home = net.group(returned.at[pl.ds(0, CAP * (PARTS - 1))])
    for k, q in enumerate(doms):
        for c in range(CAP):
            slot = q * CAP + c
            got = egrad[jnp.clip(tab[2, slot], 0, NBLK - 1)]
            sending[k, c] = jnp.where(tab[3, slot] > 0, got, jnp.zeros_like(got))
        home.start(sending.at[k], returned.at[pl.ds(d * CAP, CAP)], dev(q, x, y))
    ats = net.group(at_l.at[pl.ds(0, 3)])
    for yy, to in ysteps:
        ats.start(attp.at[yy], at_l.at[y], to)
    at_l[y] = attp[y]

    def backward(g, _):
        p = qd[pl.ds(2 * g, 2)].reshape(GROUP, 128)
        rl = rl_s[pl.ds(2 * g, 2)].reshape(GROUP, 128)
        rd = rd_s[pl.ds(2 * g, 2)].reshape(GROUP, 128)[:, :1]
        zz = jnp.where(low2, p, (p.astype(F32) * rl).astype(BF))
        zt = jnp.transpose(zz)
        go = jnp.where(low2, jnp.zeros_like(zz), zz)
        dq = jnp.concatenate(
            [
                mm(dses[2 * g + i], incoming[jnp.clip(tab[0, 2 * g + i], 0, PARTS * CAP - 1)])
                for i in range(2)
            ],
            0,
        )
        for c in range(nchunk):
            dp = mm(go, kvt[c])
            eb = probs[g, c]
            dsc = eb * (dp - rd).astype(BF)
            dq = dq + mm(dsc, kv_l[c].reshape(CHUNK, 128))
            dk = mm(zt[0:HD], dsc)
            dv = mm(zt[HD:128], eb)
            for i in range(CHUNK // 128):
                dkv[4 * c + i, 0:HD] += dk[:, i * 128 : (i + 1) * 128]
                dkv[4 * c + i, HD:128] += dv[:, i * 128 : (i + 1) * 128]
        dq = dq * 0.125
        gqp[lax.div(g, 2), lax.rem(g, 2)] = jnp.where(
            low1, dq[0:BLK], pltpu.roll(dq[BLK:GROUP], HD, 1)
        ).astype(BF)
        return 0

    lax.fori_loop(0, NBLK // 2, backward, 0)
    gqs = net.group(gq_l.at[pl.ds(0, 3)])
    for yy, to in ysteps:
        gqs.start(gqp.at[yy], gq_l.at[y], to)
    gq_l[y] = gqp[y]

    def two(ref, h, h2=None):
        h2 = h + 1 if h2 is None else h2
        return jnp.concatenate([ref[h].reshape(rows, 128), ref[h2].reshape(rows, 128)], 1)

    rows = X * BLK
    ats.wait_recv()
    for h in range(Y):
        for j in range(2):
            p = at_l[h, j].astype(F32)
            zero = jnp.zeros_like(p)
            g2[1, h, 2 * j] = jnp.where(low1, zero, pltpu.roll(p, HD, 1)).astype(BF)
            g2[1, h, 2 * j + 1] = jnp.where(low1, zero, p).astype(BF)
    for n in range(4):
        cols = pl.ds(n * 256, 256)
        o = None
        for h in range(0, Y, 2):
            t = mm(two(g2.at[1], h), wqo[h : h + 2, :, cols].reshape(256, 256))
            o = t if o is None else o + t
        part[:, 0, :, cols] = o.astype(BF).reshape(X, BLK, 256)
    xsteps = [(x2, xopp), (xp, right), (xm, left)]
    los, gfs = net.group(rs.at[:, 0]), net.group(rs.at[:, 1])
    for k, (xx, to) in enumerate(xsteps):
        los.start(part.at[xx, 0], rs.at[k, 0], to)

    yorder = [yy for yy, _ in ysteps] + [y]

    def weights(i, left_of):
        out = []
        for n in (0, 2):
            pick = yorder[n : n + 2]
            both = left_of(*pick)
            c = net.group(sibr.at[i, pl.ds(0, 2)])
            for j, h in enumerate(pick):
                wgf[i, h] = both[:, j * 128 : (j + 1) * 128].reshape(Z, 2, 64, 128)
                sibs[i, h] = wgf[i, h, :, 1 - core].astype(BF)
                c.start(sibs.at[i, h], sibr.at[i, h], sibling)
            out.append(c)
        return out

    def along_y(i, sib):
        out = net.group(yrecv.at[i])
        for k, (yy, to) in enumerate(ysteps):
            if k != 1:
                sib[k // 2].wait_recv()
            ysend[i, k] = (wgf[i, yy, :, core] + sibr[i, yy].astype(F32)).astype(BF)
            out.start(ysend.at[i, k], yrecv.at[i, k], to)
        return out

    zsteps = [lax.rem(z + k, Z) for k in (4, 3, 5, 2, 6, 1, 7)]

    def along_z(i, ys):
        total = wgf[i, y, :, core] + sibr[i, y].astype(F32)
        ys.wait_recv()
        for k in range(3):
            total = total + yrecv[i, k].astype(F32)
        own[i] = total
        zsend[i] = total.astype(BF)
        out = net.group(zrecv.at[i])
        for k, zz in enumerate(zsteps):
            out.start(zsend.at[i, zz], zrecv.at[i, k], dev(zz * 2 + core, x, y))
        return out

    def finish(i, zsum):
        res = own[i, z]
        zsum.wait_recv()
        for k in range(7):
            res = res + zrecv[i, k].astype(F32)
        wg[:, i * 128 : (i + 1) * 128] = res

    gqs.wait_recv()
    for h in range(Y):
        for j in range(2):
            p = gq_l[h, j].astype(F32)
            zero = jnp.zeros_like(p)
            g2[0, h, 2 * j] = jnp.where(low1, p, zero).astype(BF)
            g2[0, h, 2 * j + 1] = jnp.where(low1, pltpu.roll(p, HD, 1), zero).astype(BF)
    sib1 = weights(1, lambda h, h2: mm(feat_t[...], two(g2.at[0], h, h2)) + mm(cot_t[...], two(g2.at[1], h, h2)))
    y1 = along_y(1, sib1)
    for n in range(4):
        cols = pl.ds(n * 256, 256)
        o = None
        for h in range(0, Y, 2):
            t = mm(two(g2.at[0], h), wqo[h : h + 2, :, cols].reshape(256, 256))
            o = t if o is None else o + t
        gfq[:, :, cols] = o.reshape(X, BLK, 256)
    home.wait_recv()
    running = None
    for k in range(CAP * (PARTS - 1)):
        got = returned[jnp.clip(smem[1, k], 0, PARTS * CAP - 1)].astype(F32)
        running = got if k == 0 else got + running * smem[2, k].astype(F32)
        runs[k] = running
    xorder = [(x2, xopp), (xp, right), (xm, left), (x, None)]
    gks = []
    for b, _ in xorder:
        for h in range(Y):
            s = h * X + b
            more = jnp.where(
                smem[4, s] > 0,
                runs[jnp.clip(smem[3, s], 0, CAP * (PARTS - 1) - 1)],
                jnp.zeros((128, BLK), F32),
            )
            gkv[h, b] = jnp.transpose(dkv[s] + more).astype(BF)
        c = net.group(g_kv.at[pl.ds(0, 3), b])
        for yy, to in ysteps:
            c.start(gkv.at[yy, b], g_kv.at[y, b], to)
        gks.append(c)
    g_kv[y] = gkv[y]
    z1 = along_z(1, y1)

    def feature_part(b):
        o = gfq[b]
        for h in range(0, Y, 2):
            g = jnp.concatenate([g_kv[h, b], g_kv[h + 1, b]], 1)
            o = o + mm(g, wkv[h : h + 2].reshape(256, WIDTH))
        part[b, 1] = o.astype(BF)

    for k, (b, to) in enumerate(xorder):
        gks[k].wait_recv()
        if k < 3:
            feature_part(b)
            gfs.start(part.at[b, 1], rs.at[k, 1], to)
    sib0 = weights(0, lambda h, h2: mm(feat_t[...], two(g_kv, h, h2)))
    feature_part(x)
    y0 = along_y(0, sib0)
    for i, (copies, base, out) in enumerate(((los, feat, lo), (gfs, cot, gf))):
        if i == 1:
            finish(1, z1)
            z0 = along_z(0, y0)
        total = part[x, i].astype(F32)
        copies.wait_recv()
        for k in range(3):
            total = total + rs[k, i].astype(F32)
        out[...] = (base[...].astype(F32) + total).astype(BF)
    finish(0, z0)
    for c in net.all:
        c.wait_send()


def hand_over_kernel(lo, gf, wg, lo_o, gf_o, q_o, k_o, v_o, o_o):
    lo_o[...] = lo[...]
    gf_o[...] = gf[...]
    for i, o in enumerate((k_o, v_o, q_o, o_o)):
        o[...] = wg[:, i * HD : (i + 1) * HD]


VM = pl.BlockSpec(memory_space=pltpu.VMEM)
SM = pl.BlockSpec(memory_space=pltpu.SMEM)
COPIES = 47


def sds(shape, dtype):
    return jax.ShapeDtypeStruct(shape, dtype)


def params(cid):
    return pltpu.CompilerParams(
        collective_id=cid, has_side_effects=True, vmem_limit_bytes=60 * 1024 * 1024
    )


def local(
    features, w_query, w_key, w_value, w_output, cotangent, cross_source, cross_target, cross_count
):
    v = pltpu.VMEM
    full = (X, BLK, WIDTH)
    four = (Y, X, BLK, 128)
    pair = (Y, 2, BLK, 128)
    blocks = (NBLK, BLK, 128)
    layer_out, grad_features, wg = pl.pallas_call(
        layer_kernel,
        out_shape=(sds((BLK, WIDTH), BF), sds((BLK, WIDTH), BF), sds((64, 256), F32)),
        in_specs=[SM] * 3 + [VM] * 6,
        out_specs=(VM,) * 3,
        scratch_shapes=[
            v((PARTS, 8, 128), F32), v((8, 128), jnp.int32), pltpu.SMEM((8, 128), jnp.int32),
            v(full, BF), v(full, BF), v((Y, 128, WIDTH), BF), v((Y, 128, WIDTH), BF),
            v((WIDTH, X * BLK), BF), v((WIDTH, X * BLK), BF),
            v((PARTS, 8, 128), F32), v((8, 128), jnp.int32), pltpu.SMEM((8, 128), jnp.int32),
            v(four, BF), v(four, BF), v(four, BF), v(four, BF),
            v((15, CAP, BLK, 128), BF), v((PARTS * CAP, BLK, 128), BF),
            v((15, CAP, BLK, 128), BF), v((PARTS * CAP, BLK, 128), BF),
            v((NBLK // 2, 4, GROUP, CHUNK), BF), v((4, GROUP, CHUNK), F32), v((4, 128, CHUNK), BF),
            v(blocks, BF), v(blocks, F32), v(blocks, F32), v(blocks, F32), v(blocks, F32),
            v(blocks, F32),
            v(blocks, F32), v(blocks, BF), v(blocks, BF), v(blocks, BF), v((30, 128, BLK), F32), v(four, BF),
            v(pair, BF), v(pair, BF), v(four, BF), v(pair, BF), v(pair, BF),
            v((X, 2, BLK, WIDTH), BF), v((X, BLK, WIDTH), F32), v((3, 2, BLK, WIDTH), BF), v((2,) + four, BF),
            v((2, Y, Z, 2, 64, 128), F32), v((2, Y, Z, 64, 128), BF), v((2, Y, Z, 64, 128), BF),
            v((2, 3, Z, 64, 128), BF), v((2, 3, Z, 64, 128), BF),
            v((2, Z, 64, 128), F32), v((2, Z, 64, 128), BF), v((2, 7, 64, 128), BF),
            pltpu.SemaphoreType.DMA((COPIES,)), pltpu.SemaphoreType.DMA((COPIES,)),
            pltpu.SemaphoreType.DMA, pltpu.SemaphoreType.DMA,
        ],
        compiler_params=params(1),
        name="layer",
    )(
        cross_source, cross_target, cross_count, features, cotangent,
        w_key.T, w_value.T, w_query.T, w_output,
    )
    square = sds((HD, HD), F32)
    return pl.pallas_call(
        hand_over_kernel,
        out_shape=(sds((BLK, WIDTH), BF), sds((BLK, WIDTH), BF), square, square, square, square),
        in_specs=[VM] * 3,
        out_specs=(VM,) * 6,
        name="hand_over",
    )(layer_out, grad_features, wg)


def solution(mesh):
    return jax.shard_map(
        local,
        mesh=mesh,
        in_specs=(
            P(("dom", "head"), None),
            P(None, "head"),
            P(None, "head"),
            P(None, "head"),
            P("head", None),
            P(("dom", "head"), None),
            P("dom", None),
            P("dom", None),
            P("dom"),
        ),
        out_specs=(
            P(("dom", "head"), None),
            P(("dom", "head"), None),
            P("dom", "head"),
            P("dom", "head"),
            P("dom", "head"),
            P("dom", "head"),
        ),
        check_vma=False,
    )
```

```python
import jax
import jax.numpy as jnp
from jax import lax
from jax.experimental import pallas as pl
from jax.experimental.pallas import tpu as pltpu
from jax.sharding import PartitionSpec as P

HD = 64
BLK = 128
CAP = 2
X = 4
Y = 4
Z = 8
PARTS = 16
NBLK = 16
WIDTH = 1024
GROUP = 256
CHUNK = 512
NEG_FILL = -1e30
MESH = pl.DeviceIdType.MESH
BF = jnp.bfloat16
F32 = jnp.float32


def mm(a, b):
    return jnp.dot(a, b, preferred_element_type=F32)


def mm_nt(a, b):
    return lax.dot_general(a, b, (((1,), (1,)), ((), ())), preferred_element_type=F32)


def place():
    d = lax.axis_index("dom")
    h = lax.axis_index("head")
    return d, lax.div(h, Y), lax.rem(h, Y)


def greet(peers, meanwhile):
    barrier = pltpu.get_barrier_semaphore()
    for peer in peers:
        pl.semaphore_signal(barrier, inc=1, device_id=peer, device_id_type=MESH)
    meanwhile()
    pl.semaphore_wait(barrier, len(peers))


def lanes(shape):
    return lax.broadcasted_iota(jnp.int32, shape, len(shape) - 1)


def turned(t):
    return lax.rem(t, 4) * 4 + lax.div(t, 4)


class Sems:
    def __init__(self, send, recv):
        self.send, self.recv, self.n, self.all = send, recv, 0, []

    def start(self, src, dst, to):
        c = pltpu.make_async_remote_copy(
            src_ref=src, dst_ref=dst, send_sem=self.send.at[self.n], recv_sem=self.recv.at[self.n],
            device_id=to, device_id_type=MESH,
        )
        c.start()
        self.n += 1
        self.all.append(c)
        return c

    def group(self, landing):
        g = Group(self, self.n, landing)
        self.n += 1
        self.all.append(g)
        return g


class Group:
    def __init__(self, net, n, landing):
        self.net, self.n, self.landing, self.to = net, n, landing, None

    def copy(self, src, dst, to):
        return pltpu.make_async_remote_copy(
            src_ref=src, dst_ref=dst, send_sem=self.net.send.at[self.n],
            recv_sem=self.net.recv.at[self.n], device_id=to, device_id_type=MESH,
        )

    def start(self, src, dst, to):
        self.to = to
        self.copy(src, dst, to).start()

    def wait_recv(self):
        self.copy(self.landing, self.landing, self.to).wait_recv()

    def wait_send(self):
        self.copy(self.landing, self.landing, self.to).wait_send()


def slot_tables(source, target, count, req, table):
    sub = lax.broadcasted_iota(jnp.int32, (128, 128), 0)
    row = lax.broadcasted_iota(jnp.int32, (8, 128), 0)
    lane = lax.broadcasted_iota(jnp.int32, (8, 128), 1)
    ask = jnp.zeros((128, 128), jnp.int32)
    tab = jnp.zeros((8, 128), jnp.int32)
    owners = []
    for j in range(16):
        src, tgt = source[0, j], target[0, j]
        owner, block = lax.div(src, NBLK), lax.rem(src, NBLK)
        position = jnp.int32(0)
        for o in owners:
            position = position + jnp.where(o == owner, 1, 0)
        owners.append(owner)
        position = jnp.minimum(position, CAP - 1)
        ask = ask + jnp.where(sub == owner * 8 + position, turned(block), 0)
        slot, pos = owner * CAP + position, turned(tgt)
        live = jnp.where(count[0] > j, 1, 0)
        here, there = lane == pos, lane == slot
        tab = tab + jnp.where((row == 0) & here, slot * live, 0)
        tab = tab + jnp.where((row == 1) & here, live, 0)
        tab = tab + jnp.where((row == 2) & there, pos * live, 0)
        tab = tab + jnp.where((row == 3) & there, live, 0)
    req[...] = ask.astype(F32).reshape(PARTS, 8, 128)
    table[...] = tab


def order_tables(asked, table):
    sub = lax.broadcasted_iota(jnp.int32, (128, 128), 0)
    lane = lax.broadcasted_iota(jnp.int32, (128, 128), 1)
    a = jnp.where((sub & 7) < CAP, asked[...].reshape(128, 128), 99.0)
    b = jnp.transpose(a)
    one, zero = jnp.ones((128, 128), F32), jnp.zeros((128, 128), F32)
    lanef = lane.astype(F32)
    less = jnp.where((b < a) | ((b == a) & (lane < sub)), one, zero)
    rank = jnp.sum(less, 1, keepdims=True)
    hot = jnp.where(rank == lanef, one, zero)
    where_from = ((sub >> 3) * CAP + (sub & 7)).astype(F32)
    order = jnp.sum(hot * where_from, 0, keepdims=True)
    value = jnp.sum(hot * a, 0, keepdims=True)
    end = jnp.sum(jnp.where(a <= lanef, one, zero), 0, keepdims=True) - 1.0
    has = jnp.sum(jnp.where(a == lanef, one, zero), 0, keepdims=True)
    wide = jnp.broadcast_to(value, (8, 128))
    same = jnp.where(wide == pltpu.roll(wide, 1, 1), one[:8], zero[:8])
    row = sub[:8]
    out = jnp.where(row == 0, jnp.minimum(b[:8], 15.0), zero[:8])
    for i, v in ((1, order), (2, same), (3, jnp.maximum(end, 0.0)), (4, has)):
        out = jnp.where(row == i, jnp.broadcast_to(v, (8, 128)), out)
    table[...] = out.astype(jnp.int32)


def layer_kernel(
    source, target, count, feat, cot, wk, wv, wq, wo,
    lo, gf, wg,
    req, tab_v, tab, feat_all, cot_all, wkv, wqo, feat_t, cot_t, asked, table, smem, kst, qst, kv_l, qg_l,
    outgoing, incoming, sending, returned, probs, scores, kvt, qd, outl, mrow, lrow, rl_s, rd_s,
    dkv, egrad, dses, qdt, runs, gkv, attp, gqp, g_kv, at_l, gq_l, part, gfq, rs, g2, wgf, sibs, sibr, ysend, yrecv,
    own, zsend, zrecv, send_sems, recv_sems, local_sem, tab_sem,
):
    d, x, y = place()
    core, z = lax.rem(d, 2), lax.div(d, 2)

    def dev(dd, xx, yy):
        return (dd, xx * Y + yy)

    xp, xm, x2 = [lax.rem(x + k, X) for k in (1, 3, 2)]
    yp, ym, y2 = [lax.rem(y + k, Y) for k in (1, 3, 2)]
    right, left, xopp = dev(d, xp, y), dev(d, xm, y), dev(d, x2, y)
    up, down, yopp = dev(d, x, yp), dev(d, x, ym), dev(d, x, y2)
    doms = [lax.rem(d + k, PARTS) for k in range(1, PARTS)]
    sibling = dev(d + 1 - 2 * core, x, y)

    def prepare():
        slot_tables(source, target, count, req, tab_v)
        for w, o in ((wkv, (wk, wv)), (wqo, (wq, wo))):
            w[y, 0:HD] = o[0][...]
            w[y, HD:128] = o[1][...]
        asked[d] = jnp.full((8, 128), 99.0, F32)
        feat_all[x] = feat[...]
        cot_all[x] = cot[...]

    greet([right, left, xopp, up, down, yopp] + [dev(q, x, y) for q in doms], prepare)
    tp = pltpu.make_async_copy(tab_v, tab, tab_sem)
    tp.start()
    net = Sems(send_sems, recv_sems)
    start = net.start
    ysteps = [(y2, yopp), (yp, up), (ym, down)]

    def along_x(own_rows, full):
        top, bottom = pl.ds(0, HD), pl.ds(HD, HD)
        out = []
        for first, second, to in ((top, bottom, right), (bottom, top, left)):
            out.append([start(own_rows.at[h], full.at[x, h], to) for h in (first, second)])
        return out

    fx = along_x(feat, feat_all)
    mine = pl.multiple_of(core * HD, HD)
    whole = pl.ds(mine, HD)
    upper, lower = pl.ds(mine, 32), pl.ds(mine + 32, 32)

    def wfirst(w):
        piece = w.at[y, whole]
        return start(piece, piece, up), start(piece, piece, down)

    wown = [wfirst(wkv)]
    tables = net.group(asked.at[pl.ds(0, PARTS - 1)])
    for q in doms:
        tables.start(req.at[q], asked.at[d], dev(q, x, y))

    def wmiddle(i):
        w = (wkv, wqo)[i]
        a, b = wown[i]
        a.wait_recv()
        p = w.at[ym, upper]
        f1 = start(p, p, up)
        p = w.at[ym, whole]
        s1 = start(p, p, sibling)
        b.wait_recv()
        p = w.at[yp, lower]
        f2 = start(p, p, down)
        p = w.at[yp, whole]
        s2 = start(p, p, sibling)
        return f1, f2, s1, s2

    def wlast(i, mid):
        w = (wkv, wqo)[i]
        mid[0].wait_recv()
        mid[1].wait_recv()
        p = w.at[y2, whole]
        s3 = start(p, p, sibling)
        mid[2].wait_recv()
        mid[3].wait_recv()
        s3.wait_recv()

    def xmiddle(full, halves):
        a0, b0 = halves[0][0], halves[1][0]
        a0.wait_recv()
        p = full.at[xm, pl.ds(0, HD)]
        f1 = start(p, p, right)
        b0.wait_recv()
        p = full.at[xp, pl.ds(HD, HD)]
        f2 = start(p, p, left)
        return f1, f2

    mkv = wmiddle(0)
    ffwd = xmiddle(feat_all, fx)
    wlast(0, mkv)
    low4 = (lanes((BLK, 512)) & 127) < HD

    def project_kv(b):
        r = mm_nt(feat_all[b], wkv[...].reshape(Y * 128, WIDTH)).astype(BF)
        for h in range(Y):
            kst[h, b] = r[:, h * 128 : (h + 1) * 128]
        kv_l[y, b] = kst[y, b]
        for yy, to in ysteps:
            kvs.start(kst.at[yy, b], kv_l.at[y, b], to)

    def project_qo(b):
        w = wqo[...].reshape(Y * 128, WIDTH)
        r = jnp.where(low4, mm_nt(feat_all[b], w), mm_nt(cot_all[b], w)).astype(BF)
        for h in range(Y):
            qst[h, b] = r[:, h * 128 : (h + 1) * 128]
        qg_l[y, b] = qst[y, b]
        for yy, to in ysteps:
            qgs.start(qst.at[yy, b], qg_l.at[y, b], to)

    kvs, qgs = net.group(kv_l.at[pl.ds(0, 3)]), net.group(qg_l.at[pl.ds(0, 3)])
    project_kv(x)
    fx[0][1].wait_recv()
    project_kv(xm)
    fx[1][1].wait_recv()
    project_kv(xp)
    tables.wait_recv()
    order_tables(asked, table)
    cp = pltpu.make_async_copy(table, smem, local_sem)
    cp.start()
    for c in ffwd:
        c.wait_recv()
    project_kv(x2)
    wown.append(wfirst(wqo))
    cx = along_x(cot, cot_all)
    cp.wait()
    tp.wait()
    kvs.wait_recv()

    going = net.group(incoming.at[pl.ds(0, CAP * (PARTS - 1))])
    for k, q in enumerate(doms):
        for c in range(CAP):
            at = jnp.clip(smem[0, q * 8 + c], 0, NBLK - 1)
            outgoing[k, c] = kv_l[lax.div(at, 4), lax.rem(at, 4)]
        going.start(outgoing.at[k], incoming.at[pl.ds(d * CAP, CAP)], dev(q, x, y))
    mqo = wmiddle(1)
    cfwd = xmiddle(cot_all, cx)
    cx[0][1].wait_recv()
    cx[1][1].wait_recv()
    wlast(1, mqo)
    project_qo(x)
    project_qo(xm)
    project_qo(xp)
    for c in cfwd:
        c.wait_recv()
    project_qo(x2)
    incoming[pl.ds(d * CAP, CAP)] = jnp.zeros((CAP, BLK, 128), BF)
    returned[pl.ds(d * CAP, CAP)] = jnp.zeros((CAP, BLK, 128), BF)
    for b in range(X):
        feat_t[:, b * BLK : (b + 1) * BLK] = jnp.transpose(feat_all[b])
        cot_t[:, b * BLK : (b + 1) * BLK] = jnp.transpose(cot_all[b])
    low1 = lanes((BLK, 128)) < HD
    low2 = lanes((GROUP, 128)) < HD
    for s in range(NBLK):
        kvt[s // 4, :, pl.ds((s % 4) * 128, 128)] = jnp.transpose(kv_l[s // 4, s % 4])
    qgs.wait_recv()
    for s in range(NBLK):
        p = qg_l[s // 4, s % 4]
        p = jnp.where(low1, p * 0.125, p)
        qd[s] = p
        qdt[s] = jnp.transpose(p)
    dkv[...] = jnp.zeros_like(dkv)

    nchunk = NBLK * BLK // CHUNK

    def fold(v, op):
        out = v[:, 0:128]
        for j in range(1, CHUNK // 128):
            out = op(out, v[:, j * 128 : (j + 1) * 128])
        return out

    def forward(g, _):
        p = qd[pl.ds(2 * g, 2)].reshape(GROUP, 128)
        qs = jnp.where(low2, p, jnp.zeros_like(p))
        top = None
        for c in range(nchunk):
            s = mm(qs, kvt[c])
            scores[c] = s
            t = fold(s, jnp.maximum)
            top = t if top is None else jnp.maximum(top, t)
        m = jnp.max(top, 1, keepdims=True)
        total, out = None, None
        for c in range(nchunk):
            e = jnp.exp(scores[c] - m)
            t = fold(e, jnp.add)
            total = t if total is None else total + t
            eb = e.astype(BF)
            probs[g, c] = eb
            o = mm(eb, kv_l[c].reshape(CHUNK, 128))
            out = o if out is None else out + o
        l = jnp.sum(total, 1, keepdims=True)
        outl[pl.ds(2 * g, 2)] = out.reshape(2, BLK, 128)
        mrow[pl.ds(2 * g, 2)] = jnp.broadcast_to(m, (GROUP, 128)).reshape(2, BLK, 128)
        lrow[pl.ds(2 * g, 2)] = jnp.broadcast_to(l, (GROUP, 128)).reshape(2, BLK, 128)
        return 0

    lax.fori_loop(0, NBLK // 2, forward, 0)
    going.wait_recv()

    batch = 16

    def extras(g, _):
        ids = [batch * g + i for i in range(batch)]
        blks = [qd[i] for i in ids]
        ekvs = [incoming[jnp.clip(tab[0, i], 0, PARTS * CAP - 1)] for i in ids]
        zero = jnp.zeros((BLK, 128), BF)
        ses = [mm_nt(jnp.where(low1, b, zero), e) for b, e in zip(blks, ekvs)]
        gos = [jnp.where(low1, zero, b) for b in blks]
        dps = [mm_nt(o, e) for o, e in zip(gos, ekvs)]
        ses = [jnp.where(tab[1, i] > 0, e, NEG_FILL) for i, e in zip(ids, ses)]
        mls = [mrow[i] for i in ids]
        bigs = [jnp.maximum(m, jnp.max(e, 1, keepdims=True)) for m, e in zip(mls, ses)]
        cs = [jnp.exp(m - b) for m, b in zip(mls, bigs)]
        ees = [jnp.exp(e - b) for e, b in zip(ses, bigs)]
        ls = [c * lrow[i] + jnp.sum(e, 1, keepdims=True) for c, i, e in zip(cs, ids, ees)]
        rs_ = [1.0 / v for v in ls]
        pes = [e * r for e, r in zip(ees, rs_)]
        pbs = [p.astype(BF) for p in pes]
        rls = [c * r for c, r in zip(cs, rs_)]
        outs = [
            (outl[i] * r + mm(p, e)).astype(BF).astype(F32)
            for i, r, p, e in zip(ids, rls, pbs, ekvs)
        ]
        deltas = [
            jnp.sum(o.astype(F32) * a, 1, keepdims=True) for o, a in zip(gos, outs)
        ]
        dss = [(p * (dp - dl)).astype(BF) for p, dp, dl in zip(pes, dps, deltas)]
        for n, i in enumerate(ids):
            bt = qdt[i]
            egrad[i, 0:HD] = mm(bt[0:HD], dss[n]).astype(BF)
            egrad[i, HD:128] = mm(bt[HD:128], pbs[n]).astype(BF)
        for n, i in enumerate(ids):
            dses[i] = dss[n]
            rl_s[i] = rls[n]
            rd_s[i] = rls[n] * deltas[n]
        for n in range(0, batch, 2):
            attp[(batch // 4) * g + n // 4, (n // 2) % 2] = jnp.where(
                low1, pltpu.roll(outs[n], HD, 1), outs[n + 1]
            ).astype(BF)
        return 0

    lax.fori_loop(0, NBLK // batch, extras, 0)
    home = net.group(returned.at[pl.ds(0, CAP * (PARTS - 1))])
    for k, q in enumerate(doms):
        for c in range(CAP):
            slot = q * CAP + c
            got = egrad[jnp.clip(tab[2, slot], 0, NBLK - 1)]
            sending[k, c] = jnp.where(tab[3, slot] > 0, got, jnp.zeros_like(got))
        home.start(sending.at[k], returned.at[pl.ds(d * CAP, CAP)], dev(q, x, y))
    ats = net.group(at_l.at[pl.ds(0, 3)])
    for yy, to in ysteps:
        ats.start(attp.at[yy], at_l.at[y], to)
    at_l[y] = attp[y]

    def backward(g, _):
        p = qd[pl.ds(2 * g, 2)].reshape(GROUP, 128)
        rl = rl_s[pl.ds(2 * g, 2)].reshape(GROUP, 128)
        rd = rd_s[pl.ds(2 * g, 2)].reshape(GROUP, 128)[:, :1]
        zz = jnp.where(low2, p, (p.astype(F32) * rl).astype(BF))
        zt = jnp.transpose(zz)
        go = jnp.where(low2, jnp.zeros_like(zz), zz)
        dq = jnp.concatenate(
            [
                mm(dses[2 * g + i], incoming[jnp.clip(tab[0, 2 * g + i], 0, PARTS * CAP - 1)])
                for i in range(2)
            ],
            0,
        )
        for c in range(nchunk):
            dp = mm(go, kvt[c])
            eb = probs[g, c]
            dsc = eb * (dp - rd).astype(BF)
            dq = dq + mm(dsc, kv_l[c].reshape(CHUNK, 128))
            dk = mm(zt[0:HD], dsc)
            dv = mm(zt[HD:128], eb)
            for i in range(CHUNK // 128):
                dkv[4 * c + i, 0:HD] += dk[:, i * 128 : (i + 1) * 128]
                dkv[4 * c + i, HD:128] += dv[:, i * 128 : (i + 1) * 128]
        dq = dq * 0.125
        gqp[lax.div(g, 2), lax.rem(g, 2)] = jnp.where(
            low1, dq[0:BLK], pltpu.roll(dq[BLK:GROUP], HD, 1)
        ).astype(BF)
        return 0

    lax.fori_loop(0, NBLK // 2, backward, 0)
    gqs = net.group(gq_l.at[pl.ds(0, 3)])
    for yy, to in ysteps:
        gqs.start(gqp.at[yy], gq_l.at[y], to)
    gq_l[y] = gqp[y]

    def two(ref, h, h2=None):
        h2 = h + 1 if h2 is None else h2
        return jnp.concatenate([ref[h].reshape(rows, 128), ref[h2].reshape(rows, 128)], 1)

    rows = X * BLK
    ats.wait_recv()
    for h in range(Y):
        for j in range(2):
            p = at_l[h, j].astype(F32)
            zero = jnp.zeros_like(p)
            g2[1, h, 2 * j] = jnp.where(low1, zero, pltpu.roll(p, HD, 1)).astype(BF)
            g2[1, h, 2 * j + 1] = jnp.where(low1, zero, p).astype(BF)
    for n in range(4):
        cols = pl.ds(n * 256, 256)
        o = None
        for h in range(0, Y, 2):
            t = mm(two(g2.at[1], h), wqo[h : h + 2, :, cols].reshape(256, 256))
            o = t if o is None else o + t
        part[:, 0, :, cols] = o.astype(BF).reshape(X, BLK, 256)
    xsteps = [(x2, xopp), (xp, right), (xm, left)]
    los, gfs = net.group(rs.at[:, 0]), net.group(rs.at[:, 1])
    for k, (xx, to) in enumerate(xsteps):
        los.start(part.at[xx, 0], rs.at[k, 0], to)

    yorder = [yy for yy, _ in ysteps] + [y]

    def weights(i, left_of):
        out = []
        for n in (0, 2):
            pick = yorder[n : n + 2]
            both = left_of(*pick)
            c = net.group(sibr.at[i, pl.ds(0, 2)])
            for j, h in enumerate(pick):
                wgf[i, h] = both[:, j * 128 : (j + 1) * 128].reshape(Z, 2, 64, 128)
                sibs[i, h] = wgf[i, h, :, 1 - core].astype(BF)
                c.start(sibs.at[i, h], sibr.at[i, h], sibling)
            out.append(c)
        return out

    def along_y(i, sib):
        out = net.group(yrecv.at[i])
        for k, (yy, to) in enumerate(ysteps):
            if k != 1:
                sib[k // 2].wait_recv()
            ysend[i, k] = (wgf[i, yy, :, core] + sibr[i, yy].astype(F32)).astype(BF)
            out.start(ysend.at[i, k], yrecv.at[i, k], to)
        return out

    zsteps = [lax.rem(z + k, Z) for k in (4, 3, 5, 2, 6, 1, 7)]

    def along_z(i, ys):
        total = wgf[i, y, :, core] + sibr[i, y].astype(F32)
        ys.wait_recv()
        for k in range(3):
            total = total + yrecv[i, k].astype(F32)
        own[i] = total
        zsend[i] = total.astype(BF)
        out = net.group(zrecv.at[i])
        for k, zz in enumerate(zsteps):
            out.start(zsend.at[i, zz], zrecv.at[i, k], dev(zz * 2 + core, x, y))
        return out

    def finish(i, zsum):
        res = own[i, z]
        zsum.wait_recv()
        for k in range(7):
            res = res + zrecv[i, k].astype(F32)
        wg[:, i * 128 : (i + 1) * 128] = res

    gqs.wait_recv()
    for h in range(Y):
        for j in range(2):
            p = gq_l[h, j].astype(F32)
            zero = jnp.zeros_like(p)
            g2[0, h, 2 * j] = jnp.where(low1, p, zero).astype(BF)
            g2[0, h, 2 * j + 1] = jnp.where(low1, pltpu.roll(p, HD, 1), zero).astype(BF)
    sib1 = weights(1, lambda h, h2: mm(feat_t[...], two(g2.at[0], h, h2)) + mm(cot_t[...], two(g2.at[1], h, h2)))
    y1 = along_y(1, sib1)
    for n in range(4):
        cols = pl.ds(n * 256, 256)
        o = None
        for h in range(0, Y, 2):
            t = mm(two(g2.at[0], h), wqo[h : h + 2, :, cols].reshape(256, 256))
            o = t if o is None else o + t
        gfq[:, :, cols] = o.reshape(X, BLK, 256)
    home.wait_recv()
    running = None
    for k in range(CAP * (PARTS - 1)):
        got = returned[jnp.clip(smem[1, k], 0, PARTS * CAP - 1)].astype(F32)
        running = got if k == 0 else got + running * smem[2, k].astype(F32)
        runs[k] = running
    xorder = [(x2, xopp), (xp, right), (xm, left), (x, None)]
    gks = []
    for b, _ in xorder:
        for h in range(Y):
            s = h * X + b
            more = jnp.where(
                smem[4, s] > 0,
                runs[jnp.clip(smem[3, s], 0, CAP * (PARTS - 1) - 1)],
                jnp.zeros((128, BLK), F32),
            )
            gkv[h, b] = jnp.transpose(dkv[s] + more).astype(BF)
        c = net.group(g_kv.at[pl.ds(0, 3), b])
        for yy, to in ysteps:
            c.start(gkv.at[yy, b], g_kv.at[y, b], to)
        gks.append(c)
    g_kv[y] = gkv[y]
    z1 = along_z(1, y1)

    def feature_part(b):
        o = gfq[b]
        for h in range(0, Y, 2):
            g = jnp.concatenate([g_kv[h, b], g_kv[h + 1, b]], 1)
            o = o + mm(g, wkv[h : h + 2].reshape(256, WIDTH))
        part[b, 1] = o.astype(BF)

    for k, (b, to) in enumerate(xorder):
        gks[k].wait_recv()
        if k < 3:
            feature_part(b)
            gfs.start(part.at[b, 1], rs.at[k, 1], to)
    sib0 = weights(0, lambda h, h2: mm(feat_t[...], two(g_kv, h, h2)))
    feature_part(x)
    y0 = along_y(0, sib0)
    for i, (copies, base, out) in enumerate(((los, feat, lo), (gfs, cot, gf))):
        if i == 1:
            finish(1, z1)
            z0 = along_z(0, y0)
        total = part[x, i].astype(F32)
        copies.wait_recv()
        for k in range(3):
            total = total + rs[k, i].astype(F32)
        out[...] = (base[...].astype(F32) + total).astype(BF)
    finish(0, z0)
    for c in net.all:
        c.wait_send()


def hand_over_kernel(lo, gf, wg, lo_o, gf_o, q_o, k_o, v_o, o_o):
    lo_o[...] = lo[...]
    gf_o[...] = gf[...]
    for i, o in enumerate((k_o, v_o, q_o, o_o)):
        o[...] = wg[:, i * HD : (i + 1) * HD]


VM = pl.BlockSpec(memory_space=pltpu.VMEM)
SM = pl.BlockSpec(memory_space=pltpu.SMEM)
COPIES = 47


def sds(shape, dtype):
    return jax.ShapeDtypeStruct(shape, dtype)


def params(cid):
    return pltpu.CompilerParams(
        collective_id=cid, has_side_effects=True, vmem_limit_bytes=60 * 1024 * 1024
    )


def local(
    features, w_query, w_key, w_value, w_output, cotangent, cross_source, cross_target, cross_count
):
    v = pltpu.VMEM
    full = (X, BLK, WIDTH)
    four = (Y, X, BLK, 128)
    pair = (Y, 2, BLK, 128)
    blocks = (NBLK, BLK, 128)
    layer_out, grad_features, wg = pl.pallas_call(
        layer_kernel,
        out_shape=(sds((BLK, WIDTH), BF), sds((BLK, WIDTH), BF), sds((64, 256), F32)),
        in_specs=[SM] * 3 + [VM] * 6,
        out_specs=(VM,) * 3,
        scratch_shapes=[
            v((PARTS, 8, 128), F32), v((8, 128), jnp.int32), pltpu.SMEM((8, 128), jnp.int32),
            v(full, BF), v(full, BF), v((Y, 128, WIDTH), BF), v((Y, 128, WIDTH), BF),
            v((WIDTH, X * BLK), BF), v((WIDTH, X * BLK), BF),
            v((PARTS, 8, 128), F32), v((8, 128), jnp.int32), pltpu.SMEM((8, 128), jnp.int32),
            v(four, BF), v(four, BF), v(four, BF), v(four, BF),
            v((15, CAP, BLK, 128), BF), v((PARTS * CAP, BLK, 128), BF),
            v((15, CAP, BLK, 128), BF), v((PARTS * CAP, BLK, 128), BF),
            v((NBLK // 2, 4, GROUP, CHUNK), BF), v((4, GROUP, CHUNK), F32), v((4, 128, CHUNK), BF),
            v(blocks, BF), v(blocks, F32), v(blocks, F32), v(blocks, F32), v(blocks, F32),
            v(blocks, F32),
            v(blocks, F32), v(blocks, BF), v(blocks, BF), v(blocks, BF), v((30, 128, BLK), F32), v(four, BF),
            v(pair, BF), v(pair, BF), v(four, BF), v(pair, BF), v(pair, BF),
            v((X, 2, BLK, WIDTH), BF), v((X, BLK, WIDTH), F32), v((3, 2, BLK, WIDTH), BF), v((2,) + four, BF),
            v((2, Y, Z, 2, 64, 128), F32), v((2, Y, Z, 64, 128), BF), v((2, Y, Z, 64, 128), BF),
            v((2, 3, Z, 64, 128), BF), v((2, 3, Z, 64, 128), BF),
            v((2, Z, 64, 128), F32), v((2, Z, 64, 128), BF), v((2, 7, 64, 128), BF),
            pltpu.SemaphoreType.DMA((COPIES,)), pltpu.SemaphoreType.DMA((COPIES,)),
            pltpu.SemaphoreType.DMA, pltpu.SemaphoreType.DMA,
        ],
        compiler_params=params(1),
        name="layer",
    )(
        cross_source, cross_target, cross_count, features, cotangent,
        w_key.T, w_value.T, w_query.T, w_output,
    )
    square = sds((HD, HD), F32)
    return pl.pallas_call(
        hand_over_kernel,
        out_shape=(sds((BLK, WIDTH), BF), sds((BLK, WIDTH), BF), square, square, square, square),
        in_specs=[VM] * 3,
        out_specs=(VM,) * 6,
        name="hand_over",
    )(layer_out, grad_features, wg)


def solution(mesh):
    return jax.shard_map(
        local,
        mesh=mesh,
        in_specs=(
            P(("dom", "head"), None),
            P(None, "head"),
            P(None, "head"),
            P(None, "head"),
            P("head", None),
            P(("dom", "head"), None),
            P("dom", None),
            P("dom", None),
            P("dom"),
        ),
        out_specs=(
            P(("dom", "head"), None),
            P(("dom", "head"), None),
            P("dom", "head"),
            P("dom", "head"),
            P("dom", "head"),
            P("dom", "head"),
        ),
        check_vma=False,
    )
```
